32 devices in a mesh: gz: 4 (over z), gy: 8 (over y, x, core).
Axes of the slice: x: 2, y: 2, z: 4, core: 2. Of those that a mesh axis runs over, the one named last changes fastest.
Arguments:
- tracer: float32 [128, 256, 128], P('gz', 'gy'), may hold values from 0.1 to 10
- y_speed: float32 [128, 256, 128], P('gz', 'gy'), may hold values from -0.4 to 0.4
- z_speed: float32 [128, 256, 128], P('gz', 'gy'), may hold values from -0.4 to 0.4
- kappa: float32 [128, 256, 128], P('gz', 'gy'), may hold values from 0.5 to 8
Outputs:
- updated: float32 [128, 256, 128], P('gz', 'gy')
The draws below stay inside these ranges and needn't reach their ends.
All inputs are finite; a program needn't handle non-finite values.
Results may differ from the reference program's by a relative error of at most 0.0003.
Values sent between devices are 32-bit elements; how exact they have to be, the bound alone decides.
No kernel may reach another device: no remote copies, remote signals or barrier semaphores. Data moves between devices by JAX's collectives and lax.ppermute only.
A program may use at most 64 MiB of HBM per device.

```python
import math
import jax
import jax.numpy as jnp
from jax import lax

XW = 128
NSUB = 4
NZ = 128
NY = 256


def smooth_wave(count, cycles, phase):
    positions = (jnp.arange(count, dtype=jnp.float32) + 0.5) / count
    return jnp.sin(2.0 * math.pi * cycles * positions + phase)


def draw_tracer(key, part):
    phase_key = jax.random.fold_in(key, 11)
    noise_key = jax.random.fold_in(key, 12)
    phases = jax.random.uniform(phase_key, (2,), jnp.float32, 0.0, 2.0 * math.pi)
    smooth = 1.9 + 0.7 * smooth_wave(NZ, 1, phases[0])[:, None, None] + 0.7 * smooth_wave(NY, 2, phases[1])[None, :, None]
    rough = jnp.exp(jax.random.uniform(noise_key, (NZ, NY, XW), jnp.float32, math.log(0.2), math.log(3.0)))
    return smooth * rough


def draw_y_speed(key, part):
    phase_key = jax.random.fold_in(key, 21)
    noise_key = jax.random.fold_in(key, 22)
    phases = jax.random.uniform(phase_key, (2,), jnp.float32, 0.0, 2.0 * math.pi)
    noise = jax.random.uniform(noise_key, (NZ, NY, XW), jnp.float32, -0.22, 0.22)
    along_y = smooth_wave(NY, 2, phases[0])[None, :, None]
    along_z = smooth_wave(NZ, 1, phases[1])[:, None, None]
    smooth = 0.12 * along_y + 0.06 * along_z
    return smooth + noise


def draw_z_speed(key, part):
    phase_key = jax.random.fold_in(key, 31)
    noise_key = jax.random.fold_in(key, 32)
    phases = jax.random.uniform(phase_key, (2,), jnp.float32, 0.0, 2.0 * math.pi)
    noise = jax.random.uniform(noise_key, (NZ, NY, XW), jnp.float32, -0.22, 0.22)
    along_z = smooth_wave(NZ, 1, phases[0])[:, None, None]
    along_y = smooth_wave(NY, 2, phases[1])[None, :, None]
    smooth = 0.12 * along_z + 0.06 * along_y
    return smooth + noise


def levels(stream_key, dims, shards, least, high):
    level = 1.0
    for axis_at, parts in shards:
        draws = jax.random.uniform(jax.random.fold_in(jax.random.fold_in(stream_key, 6), axis_at), (parts,), jnp.float32, least / len(shards), high / len(shards))
        level = level * jnp.repeat(jnp.exp(draws), dims[axis_at] // parts).reshape((-1,) + (1,) * (len(dims) - 1 - axis_at))
    return level


def setup_inputs(seed: int = 0) -> dict:
    keys = jax.random.split(jax.random.key(seed), 5)
    return {
        "tracer": draw_tracer(jax.random.fold_in(keys[4], 71), 0),
        "y_speed": draw_y_speed(jax.random.fold_in(keys[4], 71), 0),
        "z_speed": draw_z_speed(jax.random.fold_in(keys[4], 71), 0),
        "kappa": jnp.clip(jnp.exp(math.log(8.0) - 2.7725887 * jax.random.uniform(keys[3], (NZ, NY, XW), jnp.float32) ** levels(keys[3], (NZ, NY, XW), ((0, 4), (1, 8)), -0.2, 0.2)), 0.5, 8.0),
    }


rate_const = 500.0

def advect_once(tracer, y_speed, z_speed):
    face_y = 0.5 * (y_speed[:, 1:] + y_speed[:, :-1])
    flux_y = jnp.maximum(face_y, 0.0) * tracer[:, :-1] + jnp.minimum(face_y, 0.0) * tracer[:, 1:]
    diff_y = flux_y[:, 1:] - flux_y[:, :-1]
    face_z = 0.5 * (z_speed[1:] + z_speed[:-1])
    flux_z = jnp.maximum(face_z, 0.0) * tracer[:-1] + jnp.minimum(face_z, 0.0) * tracer[1:]
    diff_z = flux_z[1:] - flux_z[:-1]
    return tracer[1:-1, 1:-1] - diff_y[1:-1] - diff_z[:, 1:-1]

def edge_faces(kappa):
    inner = rate_const * 0.5 * (kappa[..., 1:] + kappa[..., :-1])
    lower = jnp.concatenate([rate_const * kappa[..., :1], inner], axis=-1)
    upper = jnp.concatenate([inner, rate_const * kappa[..., -1:]], axis=-1)
    return (lower, upper)

def line_solve(right, lower, upper):
    low_diag = (-lower).at[..., 0].set(0.0)
    up_diag = (-upper).at[..., -1].set(0.0)
    main_diag = 1.0 + lower + upper
    return lax.linalg.tridiagonal_solve(low_diag, main_diag, up_diag, right[..., None])[..., 0]

def reference(tracer, y_speed, z_speed, kappa):
    widths = ((1, 1), (1, 1), (0, 0))
    padded_y = jnp.pad(y_speed, widths)
    padded_z = jnp.pad(z_speed, widths)
    state = tracer
    for step in range(NSUB):
        state = advect_once(jnp.pad(state, widths), padded_y, padded_z)
    lower, upper = edge_faces(jnp.moveaxis(kappa, 1, 2))
    state = jnp.moveaxis(line_solve(jnp.moveaxis(state, 1, 2), lower, upper), 2, 1)
    lower, upper = edge_faces(jnp.moveaxis(kappa, 0, 2))
    state = jnp.moveaxis(line_solve(jnp.moveaxis(state, 0, 2), lower, upper), 2, 0)
    return state
```

```python
import functools

import jax
import jax.numpy as jnp
from jax import lax
from jax.experimental import pallas as pl
from jax.experimental.pallas import tpu as pltpu
from jax.sharding import PartitionSpec as P

NSUB = 4
RATE = 500.0
AXES = ("gz", "gy")
F32 = jnp.float32


def vmem(count):
    return [pl.BlockSpec(memory_space=pltpu.VMEM)] * count


def shape(*dims):
    return jax.ShapeDtypeStruct(dims, F32)


def place():
    return (
        lax.axis_index("gz"),
        lax.axis_index("gy"),
        lax.axis_size("gz"),
        lax.axis_size("gy"),
    )


def pair_up(index):
    return index ^ 1


def pair_other(index, count):
    return (index + 1 if index % 2 else index - 1) % count


def permutation(z_partner, y_partner):
    z_count, y_count = lax.axis_size("gz"), lax.axis_size("gy")
    pairs = []
    for z in range(z_count):
        for y in range(y_count):
            to_z, to_y = z_partner(z), y_partner(y)
            if not 0 <= to_z < z_count:
                to_z, to_y = z, pair_up(y)
            pairs.append((z * y_count + y, to_z * y_count + to_y))
    return pairs


def same(index):
    return index


def z_other(index):
    return index + 1 if index % 2 else index - 1


def y_other(index):
    return pair_other(index, lax.axis_size("gy"))


def send(x, z_partner=same, y_partner=same):
    return lax.ppermute(x, AXES, permutation(z_partner, y_partner))


def pack_kernel(c, ys, zs, a_ref, b_ref, o_ref, e_ref, oa_ref, ob_ref):
    z, y, _, _ = place()
    depth, width = c.shape[0], c.shape[1]
    z_odd, y_odd = lax.rem(z, 2), lax.rem(y, 2)
    for ref, low in ((a_ref, z_odd), (b_ref, 1 - z_odd)):
        four, three = (1 - low) * (depth - 4), (1 - low) * (depth - 3)
        ref[0:4] = c[pl.ds(four, 4)]
        ref[4:8] = zs[pl.ds(four, 4)]
        ref[8:11] = ys[pl.ds(three, 3)]

    def rims(o_start, e_start):
        for ref, start in ((o_ref, o_start), (e_ref, e_start)):
            high = int(start > 0)
            for k in range(4):
                ref[k] = c[:, start + k, :]
                ref[4 + k] = ys[:, start + k, :]
            for k in range(3):
                ref[8 + k] = zs[:, start + high + k, :]

        def corner(ref, z_start):
            high = int(o_start > 0)
            for f, field in enumerate((c, ys, zs)):
                for k in range(3):
                    ref[3 * f + k] = field[z_start : z_start + 8, o_start + high + k, :]

        @pl.when(z_odd == 0)
        def _():
            corner(oa_ref, depth - 8)
            corner(ob_ref, 0)

        @pl.when(z_odd == 1)
        def _():
            corner(oa_ref, 0)
            corner(ob_ref, depth - 8)

    @pl.when(y_odd == 0)
    def _():
        rims(0, width - 4)

    @pl.when(y_odd == 1)
    def _():
        rims(width - 4, 0)


def pack(tracer, y_speed, z_speed):
    depth, width, band = tracer.shape
    return pl.pallas_call(
        pack_kernel,
        out_shape=(
            shape(11, width, band),
            shape(11, width, band),
            shape(11, depth, band),
            shape(11, depth, band),
            shape(9, 8, band),
            shape(9, 8, band),
        ),
        in_specs=vmem(3),
        out_specs=vmem(6),
        name="pack",
    )(tracer, y_speed, z_speed)


def rim_kernel(a, b, out):
    _, y, _, _ = place()
    width = a.shape[1]

    def fill(start):
        for half, ref in enumerate((a, b)):
            for k in range(11):
                out[11 * half + k] = ref[k, start : start + 8, :]

    @pl.when(lax.rem(y, 2) == 0)
    def _():
        fill(width - 8)

    @pl.when(lax.rem(y, 2) == 1)
    def _():
        fill(0)


def rim(a, b):
    return pl.pallas_call(
        rim_kernel,
        out_shape=shape(22, 8, a.shape[2]),
        in_specs=vmem(2),
        out_specs=vmem(1)[0],
        name="rim",
    )(a, b)


def advect_kernel(
    tracer, y_speed, z_speed, a, b, o, e, oa, ob, ab, weight_y, first_y,
    forward, ports, c, ys, zs, yp, yn, zp, zn,
):
    z, y, z_count, y_count = place()
    depth, width, band = tracer.shape
    rows, cols = depth + 8, width + 8
    z_odd, y_odd = lax.rem(z, 2), lax.rem(y, 2)
    keep_b = jnp.where((z_odd == 0) & (z == 0) | (z_odd == 1) & (z == z_count - 1), 0.0, 1.0)
    keep_o = jnp.where((y_odd == 0) & (y == 0) | (y_odd == 1) & (y == y_count - 1), 0.0, 1.0)
    column = lax.broadcasted_iota(jnp.int32, (8, band), 0)
    outside = (column < 4) & (y == y_count - 1) | (column >= 4) & (y == 0)
    inside = jnp.where(outside, 0.0, 1.0)

    for field, own in ((c, tracer), (ys, y_speed), (zs, z_speed)):
        field[4 : 4 + depth, 0:width, :] = own[...]
        field[0:4, width:cols, :] = jnp.zeros((4, 8, band), F32)
        field[4 + depth : rows, width:cols, :] = jnp.zeros((4, 8, band), F32)
    ys[0:1, 0:width, :] = jnp.zeros((1, width, band), F32)
    ys[rows - 1 : rows, 0:width, :] = jnp.zeros((1, width, band), F32)
    for ref, low, keep in ((a, z_odd, None), (b, 1 - z_odd, keep_b)):
        scale = (lambda v: v) if keep is None else (lambda v: v * keep)
        four = jnp.where(low == 1, 0, depth + 4)
        three = jnp.where(low == 1, 1, depth + 4)
        c[pl.ds(four, 4), 0:width, :] = scale(ref[0:4])
        zs[pl.ds(four, 4), 0:width, :] = scale(ref[4:8])
        ys[pl.ds(three, 3), 0:width, :] = scale(ref[8:11])

    def sides(o_low):
        def columns(ref, low, scale):
            start = width + 4 * int(low)
            shift = int(low)
            for k in range(4):
                c[4 : 4 + depth, start + k, :] = scale(ref[k])
                ys[4 : 4 + depth, start + k, :] = scale(ref[4 + k])
            for k in range(3):
                zs[4 : 4 + depth, start + shift + k, :] = scale(ref[8 + k])
            far = start if low else start + 3
            zs[4 : 4 + depth, far, :] = jnp.zeros((depth, band), F32)

        columns(o, o_low, lambda v: v * keep_o)
        columns(e, not o_low, lambda v: v)

        def from_pair(half, z_low):
            start = width + 4 * int(o_low is False)
            low = not o_low
            from_col = 0 if not low else 4
            zr = 0 if z_low else depth + 4
            z3 = 1 if z_low else depth + 4
            keep = 1.0 if half == 0 else keep_b
            block = slice(from_col, from_col + 4)
            c[zr : zr + 4, start : start + 4, :] = ab[11 * half : 11 * half + 4, block, :] * keep
            zs[zr : zr + 4, start : start + 4, :] = ab[11 * half + 4 : 11 * half + 8, block, :] * keep
            ys[z3 : z3 + 3, start : start + 4, :] = ab[11 * half + 8 : 11 * half + 11, block, :] * keep

        def from_corner(ref, z_low, keep):
            start = width + (5 if o_low else 0)
            zr = 1 if z_low else depth + 4
            src = 5 if z_low else 0
            for f, field in enumerate((c, ys, zs)):
                for k in range(3):
                    field[zr : zr + 3, start + k, :] = ref[3 * f + k, src : src + 3, :] * keep

        @pl.when(z_odd == 0)
        def _():
            from_pair(0, False)
            from_pair(1, True)
            from_corner(oa, False, keep_o)
            from_corner(ob, True, keep_o * keep_b)

        @pl.when(z_odd == 1)
        def _():
            from_pair(0, True)
            from_pair(1, False)
            from_corner(oa, True, keep_o)
            from_corner(ob, False, keep_o * keep_b)

    @pl.when(y_odd == 0)
    def _():
        sides(True)

    @pl.when(y_odd == 1)
    def _():
        sides(False)

    def up(v):
        return pltpu.roll(v, cols - 1, 0)

    def down(v):
        return pltpu.roll(v, 1, 0)

    def faces(r, _):
        v = ys[r]
        s = 0.5 * (v + up(v))
        yp[r] = jnp.maximum(s, 0.0)
        yn[r] = jnp.minimum(s, 0.0)
        s = 0.5 * (zs[r] + zs[jnp.minimum(r + 1, rows - 1)])
        zp[r] = jnp.maximum(s, 0.0)
        zn[r] = jnp.minimum(s, 0.0)
        return 0

    lax.fori_loop(0, rows, faces, 0, unroll=4)

    for step in range(1, NSUB + 1):
        low = jnp.where(z == 0, 4, step)
        high = jnp.where(z == z_count - 1, rows - 4, rows - step)
        here = c[low]
        flux = zp[low - 1] * c[low - 1] + zn[low - 1] * here

        def row(r, carry):
            here, below = carry
            after = c[r + 1]
            above = zp[r] * here + zn[r] * after
            across = yp[r] * here + yn[r] * up(here)
            new = here - (across - down(across)) - (above - below)
            c[r, 0:width, :] = new[0:width]
            c[r, width:cols, :] = new[width:cols] * inside
            return after, above

        lax.fori_loop(low, high, row, (here, flux))

    total = jnp.zeros((depth, band), F32)
    carry = jnp.zeros((depth, band), F32)
    for j in range(width):
        value = c[4 : 4 + depth, j, :]
        total = total + first_y[j] * value
        carry = value + weight_y[j] * carry
        forward[j] = carry
    ports[0] = total
    ports[1] = carry


def advect(tracer, y_speed, z_speed, halos, weight_y, first_y):
    depth, width, band = tracer.shape
    padded = pltpu.VMEM((depth + 8, width + 8, band), F32)
    return pl.pallas_call(
        advect_kernel,
        out_shape=(shape(width, depth, band), shape(2, depth, band)),
        in_specs=vmem(12),
        out_specs=vmem(2),
        scratch_shapes=[padded] * 7,
        name="advect",
    )(tracer, y_speed, z_speed, *halos, weight_y, first_y)


def factor_rows(read, count, edge_low, edge_high, weight, inverse, first, last, ports):
    face = [None] * (count + 1)
    before = read(0)
    low_kappa = before
    for j in range(1, count):
        here = read(j)
        face[j] = 0.5 * RATE * (before + here)
        before = here
    high_kappa = before
    left = 1.0 + edge_low * (RATE * low_kappa)
    right = 1.0 + edge_high * (RATE * high_kappa)
    ratios = [None] * count
    weight[0] = jnp.zeros_like(low_kappa)
    for j in range(1, count):
        inv = 1.0 / (face[j] + left)
        ratio = face[j] * inv
        inverse[j - 1] = inv
        weight[j] = ratio
        left = 1.0 + left * ratio
        back = count - j
        ratio = face[back] / (face[back] + right)
        ratios[back] = ratio
        right = 1.0 + right * ratio
    end = 1.0 / (left + edge_high * (RATE * high_kappa))
    inverse[count - 1] = end
    start = 1.0 / (right + edge_low * (RATE * low_kappa))
    ports[0] = start
    ports[2] = end
    ports[3] = low_kappa
    ports[4] = high_kappa
    value = start
    first[0] = value
    back_value = end
    last[count - 1] = end
    for j in range(1, count):
        value = value * ratios[j]
        first[j] = value
        back = count - j
        back_value = back_value * weight[back]
        last[back - 1] = back_value
    ports[1] = value


def factor_kernel(kappa, wy, py, fy, ly, ports_y, wz, pz, fz, lz, ports_z):
    z, y, z_count, y_count = place()
    depth, width, _ = kappa.shape

    def flag(condition):
        return jnp.where(condition, 1.0, 0.0)

    factor_rows(
        lambda j: kappa[:, j, :], width, flag(y == 0), flag(y == y_count - 1), wy, py, fy, ly, ports_y
    )
    factor_rows(
        lambda j: kappa[j], depth, flag(z == 0), flag(z == z_count - 1), wz, pz, fz, lz, ports_z
    )


def factor(kappa):
    depth, width, band = kappa.shape
    along_y = [shape(width, depth, band)] * 4 + [shape(5, depth, band)]
    along_z = [shape(depth, width, band)] * 4 + [shape(5, width, band)]
    return pl.pallas_call(
        factor_kernel,
        out_shape=tuple(along_y + along_z),
        in_specs=vmem(1),
        out_specs=vmem(10),
        name="factor",
    )(kappa)


def backward_kernel(forward, weight, inverse, out):
    count = forward.shape[0]
    value = forward[count - 1] * inverse[count - 1]
    out[count - 1] = value
    for j in range(count - 2, -1, -1):
        value = forward[j] * inverse[j] + weight[j + 1] * value
        out[j] = value


def backward(forward, weight, inverse):
    return pl.pallas_call(
        backward_kernel,
        out_shape=shape(*forward.shape),
        in_specs=vmem(3),
        out_specs=vmem(1)[0],
        name="backward",
    )(forward, weight, inverse)


def turn_kernel(base, first_y, last_y, currents, weight_z, first_z, forward, ports, u):
    width, depth, band = base.shape
    low, high = currents[0], currents[1]
    for j in range(width):
        u[:, j, :] = base[j] + low * first_y[j] + high * last_y[j]
    total = jnp.zeros((width, band), F32)
    carry = jnp.zeros((width, band), F32)
    for k in range(depth):
        value = u[k]
        total = total + first_z[k] * value
        carry = value + weight_z[k] * carry
        forward[k] = carry
    ports[0] = total
    ports[1] = carry


def turn(base, first_y, last_y, currents, weight_z, first_z):
    width, depth, band = base.shape
    return pl.pallas_call(
        turn_kernel,
        out_shape=(shape(depth, width, band), shape(2, width, band)),
        in_specs=vmem(6),
        out_specs=vmem(2),
        scratch_shapes=[pltpu.VMEM((depth, width, band), F32)],
        name="turn",
    )(base, first_y, last_y, currents, weight_z, first_z)


def finish_kernel(base, first, last, currents, out):
    low, high = currents[0], currents[1]
    for k in range(base.shape[0]):
        out[k] = base[k] + low * first[k] + high * last[k]


def finish(base, first, last, currents):
    return pl.pallas_call(
        finish_kernel,
        out_shape=shape(*base.shape),
        in_specs=vmem(4),
        out_specs=vmem(1)[0],
        name="finish",
    )(base, first, last, currents)


def xor_exchange(x, axis, level):
    step = 1 << level
    return lax.ppermute(x, axis, [(i, i ^ step) for i in range(lax.axis_size(axis))])


def levels_of(axis):
    return (lax.axis_size(axis) - 1).bit_length()


def join_ports(ports, axis):
    index = lax.axis_index(axis)
    joins = []
    for level in range(levels_of(axis)):
        theirs = xor_exchange(ports, axis, level)
        is_left = (lax.shift_right_logical(index, level) & 1) == 0
        left = jnp.where(is_left, ports, theirs)
        right = jnp.where(is_left, theirs, ports)
        face = 0.5 * RATE * (left[4] + right[3])
        d = 1.0 / (1.0 / face + left[2] + right[0])
        joins.append((is_left, d, left[1], right[1]))
        ports = jnp.stack(
            [
                left[0] - left[1] * left[1] * d,
                left[1] * right[1] * d,
                right[2] - right[1] * right[1] * d,
                left[3],
                right[4],
            ]
        )
    return joins


def port_currents(sources, joins, axis):
    found = []
    count = len(joins)
    for level, (is_left, d, z_left, z_right) in enumerate(joins):
        theirs = xor_exchange(sources, axis, level)
        left = jnp.where(is_left, sources, theirs)
        right = jnp.where(is_left, theirs, sources)
        flow = (left[1] - right[0]) * d
        found.append(flow)
        if level + 1 < count:
            sources = jnp.stack([left[0] - z_left * flow, right[1] + z_right * flow])
    low = jnp.zeros_like(found[0])
    high = low
    for (is_left, d, z_left, z_right), flow in zip(joins[::-1], found[::-1]):
        flow = flow + (z_left * low - z_right * high) * d
        low, high = jnp.where(is_left, low, flow), jnp.where(is_left, -flow, high)
    return jnp.stack([low, high])


def local(tracer, y_speed, z_speed, kappa):
    a, b, o, e, oa, ob = pack(tracer, y_speed, z_speed)
    a = send(a, z_partner=pair_up)
    b = send(b, z_partner=z_other)
    o = send(o, y_partner=y_other)
    e = send(e, y_partner=pair_up)
    oa = send(oa, z_partner=pair_up, y_partner=y_other)
    ob = send(ob, z_partner=z_other, y_partner=y_other)
    ab = send(rim(a, b), y_partner=pair_up)
    wy, py, fy, ly, ports_y, wz, pz, fz, lz, ports_z = factor(kappa)
    joins_y = join_ports(ports_y, "gy")
    joins_z = join_ports(ports_z, "gz")
    forward, sources = advect(tracer, y_speed, z_speed, (a, b, o, e, oa, ob, ab), wy, fy)
    sources = jnp.stack([sources[0], sources[1] * py[-1]])
    currents = port_currents(sources, joins_y, "gy")
    base = backward(forward, wy, py)
    forward, sources = turn(base, fy, ly, currents, wz, fz)
    sources = jnp.stack([sources[0], sources[1] * pz[-1]])
    currents = port_currents(sources, joins_z, "gz")
    base = backward(forward, wz, pz)
    return finish(base, fz, lz, currents)


def solution(mesh):
    spec = P("gz", "gy", None)
    return jax.shard_map(
        local, mesh=mesh, in_specs=(spec,) * 4, out_specs=spec, check_vma=False
    )
```

```python
import jax
import jax.numpy as jnp
from jax import lax
from jax.experimental import pallas as pl
from jax.experimental.pallas import tpu as pltpu
from jax.sharding import PartitionSpec as P

NSUB = 4
RATE = 500.0
AXES = ("gz", "gy")
F32 = jnp.float32
VMEM_BYTES = 12 << 20


def near(*dims):
    return pltpu.VMEM(dims, F32)


def far(*dims):
    return pltpu.HBM(dims, F32)


def call(kernel, name, outs, operands, scratch=(), cycles=0):
    whole, away = pl.BlockSpec(memory_space=pltpu.VMEM), pl.BlockSpec(memory_space=pltpu.HBM)
    inputs, in_specs = [], []
    for operand in operands:
        where, x = operand if isinstance(operand, tuple) else ("near", operand)
        x = pltpu.with_memory_space_constraint(x, pltpu.VMEM if where == "near" else pltpu.HBM)
        inputs.append(x)
        in_specs.append(away if where == "far" else whole)
    out_specs = [away if isinstance(out, tuple) else whole for out in outs]
    result = pl.pallas_call(
        kernel,
        out_shape=[out[1] if isinstance(out, tuple) else out for out in outs],
        in_specs=in_specs,
        out_specs=out_specs,
        scratch_shapes=scratch,
        compiler_params=pltpu.CompilerParams(vmem_limit_bytes=VMEM_BYTES),
        cost_estimate=pl.CostEstimate(flops=0, bytes_accessed=cycles * 1024, transcendentals=0) if cycles else None,
        name=name,
    )(*inputs)
    return result if len(outs) > 1 else result[0]


def place():
    return (
        lax.axis_index("gz"),
        lax.axis_index("gy"),
        lax.axis_size("gz"),
        lax.axis_size("gy"),
    )


def pair_up(index):
    return index ^ 1


def same(index):
    return index


def z_other(index):
    return index + 1 if index % 2 else index - 1


def y_other(index):
    return (index + 1 if index % 2 else index - 1) % lax.axis_size("gy")


def permutation(z_partner, y_partner):
    z_count, y_count = lax.axis_size("gz"), lax.axis_size("gy")
    pairs = []
    for z in range(z_count):
        for y in range(y_count):
            to_z, to_y = z_partner(z), y_partner(y)
            if not 0 <= to_z < z_count:
                to_z, to_y = z, pair_up(y)
            pairs.append((z * y_count + y, to_z * y_count + to_y))
    return pairs


def send(x, z_partner=same, y_partner=same):
    return lax.ppermute(x, AXES, permutation(z_partner, y_partner))


def swap(x, axis, level):
    step = 1 << level
    if axis == "gy":
        step |= 1
    return lax.ppermute(x, axis, [(i, i ^ step) for i in range(lax.axis_size(axis))])


def levels_of(axis):
    return (lax.axis_size(axis) - 1).bit_length()


def rim_kernel(a, b, oa, ob, out):
    _, y, _, _ = place()
    width = a.shape[1]
    start = pl.multiple_of((1 - lax.rem(y, 2)) * (width - 8), 8)
    for half, ref in enumerate((a, b)):
        for k in range(11):
            out[11 * half + k] = ref[k, pl.ds(start, 8), :]


def rim(a, b, oa, ob):
    return call(rim_kernel, "rim", [near(22, 8, a.shape[2])], [a, b, oa, ob], cycles=200)


def reciprocal(x):
    r = pl.reciprocal(x, approx=True)
    return r * (2.0 - x * r)


def factor(sides):
    state = []
    for read, count, r, phi, psi, ports, edge_low, edge_high in sides:
        first = read(0)
        before = first
        for j in range(1, count):
            here = read(j)
            r[j] = reciprocal((0.5 * RATE) * (before + here))
            before = here
        ports[3] = first
        ports[4] = before
        one = jnp.ones_like(first)
        phi[0] = one
        psi[count - 1] = one
        state.append([one, 1.0 + edge_low * first, one, 1.0 + edge_high * before])
    for j in range(1, max(side[1] for side in sides)):
        for (_, count, r, phi, psi, _, _, _), s in zip(sides, state):
            if j < count:
                s[0] = s[0] + r[j] * s[1]
                s[1] = s[1] + s[0]
                phi[j] = s[0]
                s[2] = s[2] + r[count - j] * s[3]
                s[3] = s[3] + s[2]
                psi[count - 1 - j] = s[2]
    for (_, _, _, _, _, ports, _, edge_high), s in zip(sides, state):
        inverse = reciprocal(s[1] + edge_high * ports[4] * s[0])
        ports[0] = s[2] * inverse
        ports[1] = inverse
        ports[2] = s[0] * inverse


def begin_kernel(
    tracer, y_speed, z_speed, kappa_far, a_ref, b_ref, o_ref, e_ref, oa_ref, ob_ref,
    phi_y_far, psi_y_far, phi_z_far, psi_z_far,
    c, ys, zs, kappa, r_y, r_z, phi_y, psi_y, phi_z, psi_z, sem,
):
    arrivals = [
        pltpu.make_async_copy(source, target, sem.at[k])
        for k, (source, target) in enumerate(((kappa_far, kappa), (tracer, c), (y_speed, ys), (z_speed, zs)))
    ]
    for copy in arrivals:
        copy.start()
    z, y, z_count, y_count = place()
    depth, width, _ = c.shape

    def flag(condition):
        return jnp.where(condition, RATE, 0.0)

    arrivals[0].wait()
    factor((
        (lambda j: kappa[:, j, :], width, r_y, phi_y, psi_y, e_ref.at[11:16], flag(y == 0), flag(y == y_count - 1)),
        (lambda j: kappa[j], depth, r_z, phi_z, psi_z, a_ref.at[11:16], flag(z == 0), flag(z == z_count - 1)),
    ))
    results = [
        pltpu.make_async_copy(source, target, sem.at[4 + k])
        for k, (source, target) in enumerate(
            ((phi_y, phi_y_far), (psi_y, psi_y_far), (phi_z, phi_z_far), (psi_z, psi_z_far))
        )
    ]
    for copy in results:
        copy.start()
    for copy in arrivals[1:]:
        copy.wait()

    z_odd, y_odd = lax.rem(z, 2), lax.rem(y, 2)
    for ref, low in ((a_ref, z_odd), (b_ref, 1 - z_odd)):
        four, three = (1 - low) * (depth - 4), (1 - low) * (depth - 3)
        ref[0:4] = c[pl.ds(four, 4)]
        ref[4:8] = zs[pl.ds(four, 4)]
        ref[8:11] = ys[pl.ds(three, 3)]

    def rims(o_start, e_start):
        for ref, start in ((o_ref, o_start), (e_ref, e_start)):
            high = int(start > 0)
            for k in range(4):
                ref[k] = c[:, start + k, :]
                ref[4 + k] = ys[:, start + k, :]
            for k in range(3):
                ref[8 + k] = zs[:, start + high + k, :]
        high = int(o_start > 0)
        oa_start = pl.multiple_of((1 - z_odd) * (depth - 8), 8)
        ob_start = pl.multiple_of(z_odd * (depth - 8), 8)
        for f, field in enumerate((c, ys, zs)):
            for k in range(3):
                oa_ref[3 * f + k] = field[pl.ds(oa_start, 8), o_start + high + k, :]
                ob_ref[3 * f + k] = field[pl.ds(ob_start, 8), o_start + high + k, :]

    @pl.when(y_odd == 0)
    def _():
        rims(0, width - 4)

    @pl.when(y_odd == 1)
    def _():
        rims(width - 4, 0)

    for copy in results:
        copy.wait()


def begin(tracer, y_speed, z_speed, kappa):
    depth, width, band = tracer.shape
    along_y, along_z = (width, depth, band), (depth, width, band)
    return call(
        begin_kernel,
        "begin",
        [near(16, width, band), near(11, width, band), near(11, depth, band), near(16, depth, band)]
        + [near(9, 8, band)] * 2
        + [("far", far(*along_y))] * 2
        + [("far", far(*along_z))] * 2,
        [("far", x) for x in (tracer, y_speed, z_speed, kappa)],
        scratch=[near(*along_z)] * 4 + [near(*along_y), near(*along_z)] + [near(*along_y)] * 2
        + [near(*along_z)] * 2 + [pltpu.SemaphoreType.DMA((8,))],
        cycles=4000,
    )


def ports_kernel(axis, level, first_row, mine, theirs, out, joint):
    is_left = (lax.shift_right_logical(lax.axis_index(axis), level) & 1) == 0
    pairs = [(mine[first_row + k], theirs[first_row + k]) for k in range(5)]
    left = [jnp.where(is_left, m, t) for m, t in pairs]
    right = [jnp.where(is_left, t, m) for m, t in pairs]
    d = reciprocal(reciprocal((0.5 * RATE) * (left[4] + right[3])) + left[2] + right[0])
    out[0] = left[0] - left[1] * left[1] * d
    out[1] = left[1] * right[1] * d
    out[2] = right[2] - right[1] * right[1] * d
    out[3] = left[3]
    out[4] = right[4]
    joint[0] = d
    joint[1] = left[1]
    joint[2] = right[1]


def join_ports(mine, theirs, axis, level, first_row=0):
    _, lines, band = mine.shape

    def kernel(*refs):
        ports_kernel(axis, level, first_row, *refs)

    return call(kernel, "join_ports", [near(5, lines, band), near(3, lines, band)], [mine, theirs], cycles=100)


def join_levels(mine, theirs, axis):
    ports, joint = join_ports(mine, theirs, axis, 0, first_row=11)
    joints = [joint]
    for level in range(1, levels_of(axis) - 1):
        ports, joint = join_ports(ports, swap(ports, axis, level), axis, level)
        joints.append(joint)
    return ports, joints


def source_kernel(axis, level, last, mine, theirs, joint, ports, out, flow_ref):
    index = lax.axis_index(axis)
    is_left = (lax.shift_right_logical(index, level) & 1) == 0
    pairs = [(mine[k], theirs[k]) for k in range(2)]
    left = [jnp.where(is_left, m, t) for m, t in pairs]
    right = [jnp.where(is_left, t, m) for m, t in pairs]
    flow = (left[1] - right[0]) * joint[0]
    flow_ref[0] = flow
    low, high = left[0] - joint[1] * flow, right[1] + joint[2] * flow
    if not last:
        out[0] = low
        out[1] = high
        return
    next_left = (lax.shift_right_logical(index, level + 1) & 1) == 0
    out[0] = jnp.where(next_left, high, low)
    out[1] = jnp.where(next_left, ports[2], ports[0])
    out[2] = jnp.where(next_left, ports[4], ports[3])


def join_sources(mine, theirs, joint, ports, axis, level):
    _, lines, band = mine.shape
    last = level + 2 == levels_of(axis)

    def kernel(*refs):
        source_kernel(axis, level, last, *refs)

    outs = [near(3 if last else 2, lines, band), near(1, lines, band)]
    return call(kernel, "join_sources", outs, [mine, theirs, joint, ports], cycles=100)


def end_currents(axis, mine, theirs, joints, flows):
    index = lax.axis_index(axis)
    level = len(joints)
    is_left = (lax.shift_right_logical(index, level) & 1) == 0
    d = reciprocal(reciprocal((0.5 * RATE) * (mine[2] + theirs[2])) + mine[1] + theirs[1])
    flow = (mine[0] - theirs[0]) * d
    zero = jnp.zeros_like(flow)
    low, high = jnp.where(is_left, zero, -flow), jnp.where(is_left, -flow, zero)
    for level in range(level - 1, -1, -1):
        joint = joints[level]
        is_left = (lax.shift_right_logical(index, level) & 1) == 0
        flow = flows[level][0] + (joint[1] * low - joint[2] * high) * joint[0]
        low, high = jnp.where(is_left, low, flow), jnp.where(is_left, -flow, high)
    return low, high


def solve_open(read, phi, psi, scale, base, ports, kept):
    count = base.shape[0]
    total = jnp.zeros(base.shape[1:], F32)
    for j in range(count):
        value = scale * read(j)
        kept[j] = value
        total = total + phi[j] * value
        base[j] = psi[j] * total
    ports[1] = total
    total = jnp.zeros(base.shape[1:], F32)
    for j in range(count - 1, -1, -1):
        base[j] = base[j] + phi[j] * total
        total = total + psi[j] * kept[j]
    ports[0] = total


def advect_kernel(
    tracer, y_speed, z_speed, a, b, o, e, oa, ob, ab, e_mine, phi_far, psi_far,
    base, sources, phi, psi, c, ys, zs, sy, sz, kept, sem,
):
    z, y, z_count, y_count = place()
    depth, width, band = tracer.shape
    rows, cols = depth + 8, width + 8
    copies = [
        pltpu.make_async_copy(own, field.at[pl.ds(4, depth), pl.ds(0, width), :], sem.at[k])
        for k, (field, own) in enumerate(((c, tracer), (ys, y_speed), (zs, z_speed)))
    ]
    copies += [
        pltpu.make_async_copy(phi_far, phi, sem.at[3]),
        pltpu.make_async_copy(psi_far, psi, sem.at[4]),
    ]
    for copy in copies:
        copy.start()
    z_odd, y_odd = lax.rem(z, 2), lax.rem(y, 2)
    keep_b = jnp.where((z_odd == 0) & (z == 0) | (z_odd == 1) & (z == z_count - 1), 0.0, 1.0)
    keep_o = jnp.where((y_odd == 0) & (y == 0) | (y_odd == 1) & (y == y_count - 1), 0.0, 1.0)
    column = lax.broadcasted_iota(jnp.int32, (8, band), 0)
    outside = (column < 4) & (y == y_count - 1) | (column >= 4) & (y == 0)
    inside = jnp.where(outside, 0.0, 1.0)

    for field in (c, ys, zs):
        field[0:4, width:cols, :] = jnp.zeros((4, 8, band), F32)
        field[4 + depth : rows, width:cols, :] = jnp.zeros((4, 8, band), F32)
    ys[0:1, 0:width, :] = jnp.zeros((1, width, band), F32)
    ys[rows - 1 : rows, 0:width, :] = jnp.zeros((1, width, band), F32)
    for ref, low, keep in ((a, z_odd, None), (b, 1 - z_odd, keep_b)):
        scale = (lambda v: v) if keep is None else (lambda v: v * keep)
        four = jnp.where(low == 1, 0, depth + 4)
        three = jnp.where(low == 1, 1, depth + 4)
        c[pl.ds(four, 4), 0:width, :] = scale(ref[0:4])
        zs[pl.ds(four, 4), 0:width, :] = scale(ref[4:8])
        ys[pl.ds(three, 3), 0:width, :] = scale(ref[8:11])

    def sides(o_low):
        def columns(ref, low, scale):
            start = width + 4 * int(low)
            shift = int(low)
            for k in range(4):
                c[4 : 4 + depth, start + k, :] = scale(ref[k])
                ys[4 : 4 + depth, start + k, :] = scale(ref[4 + k])
            for k in range(3):
                zs[4 : 4 + depth, start + shift + k, :] = scale(ref[8 + k])
            far_column = start if low else start + 3
            zs[4 : 4 + depth, far_column, :] = jnp.zeros((depth, band), F32)

        columns(o, o_low, lambda v: v * keep_o)
        columns(e, not o_low, lambda v: v)

        def from_pair(half, z_low):
            start = width if o_low else width + 4
            block = slice(0, 4) if o_low else slice(4, 8)
            zr = 0 if z_low else depth + 4
            z3 = 1 if z_low else depth + 4
            keep = 1.0 if half == 0 else keep_b
            c[zr : zr + 4, start : start + 4, :] = ab[11 * half : 11 * half + 4, block, :] * keep
            zs[zr : zr + 4, start : start + 4, :] = ab[11 * half + 4 : 11 * half + 8, block, :] * keep
            ys[z3 : z3 + 3, start : start + 4, :] = ab[11 * half + 8 : 11 * half + 11, block, :] * keep

        def from_corner(ref, z_low, keep):
            start = width + (5 if o_low else 0)
            zr = 1 if z_low else depth + 4
            src = 5 if z_low else 0
            for f, field in enumerate((c, ys, zs)):
                for k in range(3):
                    field[zr : zr + 3, start + k, :] = ref[3 * f + k, src : src + 3, :] * keep

        @pl.when(z_odd == 0)
        def _():
            from_pair(0, False)
            from_pair(1, True)
            from_corner(oa, False, keep_o)
            from_corner(ob, True, keep_o * keep_b)

        @pl.when(z_odd == 1)
        def _():
            from_pair(0, True)
            from_pair(1, False)
            from_corner(oa, True, keep_o)
            from_corner(ob, False, keep_o * keep_b)

    @pl.when(y_odd == 0)
    def _():
        sides(True)

    @pl.when(y_odd == 1)
    def _():
        sides(False)

    for copy in copies[:3]:
        copy.wait()

    def up(v):
        return pltpu.roll(v, cols - 1, 0)

    def down(v):
        return pltpu.roll(v, 1, 0)

    def flux(speed, here, after):
        return speed * jnp.where(speed > 0.0, here, after)

    def faces(r, before):
        v = ys[r]
        sy[r] = 0.5 * (v + up(v))
        after = zs[r + 1]
        sz[r] = 0.5 * (before + after)
        return after

    lax.fori_loop(0, rows - 1, faces, zs[0], unroll=3)

    keep_low = jnp.where(z == 0, 0.0, 1.0)
    keep_high = jnp.where(z == z_count - 1, 0.0, 1.0)
    for step in range(1, NSUB + 1):
        here = c[step]

        def row(r, carry):
            here, below = carry
            after = c[r + 1]
            above = flux(sz[r], here, after)
            across = flux(sy[r], here, up(here))
            new = here - (across - down(across)) - (above - below)
            c[r, 0:width, :] = new[0:width]
            c[r, width:cols, :] = new[width:cols] * inside
            return after, above

        lax.fori_loop(step, rows - step, row, (here, flux(sz[step - 1], c[step - 1], here)), unroll=4)
        if step < NSUB:
            c[3] = c[3] * keep_low
            c[4 + depth] = c[4 + depth] * keep_high

    for copy in copies[3:]:
        copy.wait()
    solve_open(lambda j: c[4 : 4 + depth, j, :], phi, psi, e_mine[12], base, sources, kept)


def advect(tracer, y_speed, z_speed, halos, e_mine, phi, psi):
    depth, width, band = tracer.shape
    padded = near(depth + 8, width + 8, band)
    along_y = near(width, depth, band)
    return call(
        advect_kernel,
        "advect",
        [along_y, near(2, depth, band), along_y, along_y],
        [("far", x) for x in (tracer, y_speed, z_speed)]
        + list(halos)
        + [e_mine, ("far", phi), ("far", psi)],
        scratch=[padded] * 5 + [along_y, pltpu.SemaphoreType.DMA((5,))],
        cycles=5000,
    )


def turn_kernel(levels, *refs):
    mine, theirs = refs[0:2]
    joints, flows = refs[2 : 2 + levels], refs[2 + levels : 2 + 2 * levels]
    (
        ports_y, base_y, phi_y, psi_y, ports_z, phi_far, psi_far,
        base, sources, phi, psi, u, kept, sem,
    ) = refs[2 + 2 * levels :]
    copies = [
        pltpu.make_async_copy(phi_far, phi, sem.at[0]),
        pltpu.make_async_copy(psi_far, psi, sem.at[1]),
    ]
    for copy in copies:
        copy.start()
    low, high = end_currents("gy", mine, theirs, joints, flows)
    scale = ports_y[12]
    low, high = low * scale, high * scale
    for j in range(base_y.shape[0]):
        u[:, j, :] = base_y[j] + low * psi_y[j] + high * phi_y[j]
    for copy in copies:
        copy.wait()
    solve_open(lambda k: u[k], phi, psi, ports_z[12], base, sources, kept)


def turn(mine, theirs, joints, flows, ports_y, base_y, phi_y, psi_y, ports_z, phi_z, psi_z):
    width, depth, band = base_y.shape
    along_z = near(depth, width, band)

    def kernel(*refs):
        turn_kernel(len(joints), *refs)

    return call(
        kernel,
        "turn",
        [along_z, near(2, width, band), along_z, along_z],
        [mine, theirs, *joints, *flows, ports_y, base_y, phi_y, psi_y, ports_z]
        + [("far", phi_z), ("far", psi_z)],
        scratch=[along_z, along_z, pltpu.SemaphoreType.DMA((2,))],
        cycles=1500,
    )


def finish_kernel(levels, *refs):
    mine, theirs = refs[0:2]
    joints, flows = refs[2 : 2 + levels], refs[2 + levels : 2 + 2 * levels]
    ports_z, base, phi, psi, out, u, sem = refs[2 + 2 * levels :]
    low, high = end_currents("gz", mine, theirs, joints, flows)
    scale = ports_z[12]
    low, high = low * scale, high * scale
    depth = base.shape[0]
    part = depth // 4
    copies = []
    for p in range(4):
        for k in range(p * part, (p + 1) * part):
            u[k] = base[k] + low * psi[k] + high * phi[k]
        block = pl.ds(p * part, part)
        copies.append(pltpu.make_async_copy(u.at[block], out.at[block], sem.at[p]))
        copies[-1].start()
    for copy in copies:
        copy.wait()


def finish(mine, theirs, joints, flows, ports_z, base, phi, psi):
    def kernel(*refs):
        finish_kernel(len(joints), *refs)

    return call(
        kernel,
        "finish",
        [("far", jax.ShapeDtypeStruct(base.shape, F32))],
        [mine, theirs, *joints, *flows, ports_z, base, phi, psi],
        scratch=[near(*base.shape), pltpu.SemaphoreType.DMA((4,))],
        cycles=1000,
    )


def exchange_sources(sources, ports, joints, axis):
    flows = []
    for level, joint in enumerate(joints):
        theirs = swap(sources, axis, level)
        sources, flow = join_sources(sources, theirs, joint, ports, axis, level)
        flows.append(flow)
    return sources, swap(sources, axis, len(joints)), flows


def local(tracer, y_speed, z_speed, kappa):
    a_mine, b, o, e_mine, oa, ob, phi_y, psi_y, phi_z, psi_z = begin(tracer, y_speed, z_speed, kappa)
    a = send(a_mine, z_partner=pair_up)
    b = send(b, z_partner=z_other)
    o = send(o, y_partner=y_other)
    oa = send(oa, z_partner=pair_up, y_partner=y_other)
    ob = send(ob, z_partner=z_other, y_partner=y_other)
    e = swap(e_mine, "gy", 0)
    ab = send(rim(a, b, oa, ob), y_partner=pair_up)

    ports_y, joints_y = join_levels(e_mine, e, "gy")
    ports_z, joints_z = join_levels(a_mine, a, "gz")

    base, sources, phi_y, psi_y = advect(
        tracer, y_speed, z_speed, (a, b, o, e, oa, ob, ab), e_mine, phi_y, psi_y
    )
    mine, theirs, flows = exchange_sources(sources, ports_y, joints_y, "gy")
    base, sources, phi_z, psi_z = turn(
        mine, theirs, joints_y, flows, e_mine, base, phi_y, psi_y, a_mine, phi_z, psi_z
    )
    mine, theirs, flows = exchange_sources(sources, ports_z, joints_z, "gz")
    return finish(mine, theirs, joints_z, flows, a_mine, base, phi_z, psi_z)


def solution(mesh):
    spec = P("gz", "gy", None)
    return jax.shard_map(
        local, mesh=mesh, in_specs=(spec,) * 4, out_specs=spec, check_vma=False
    )
```

```python
import jax
import jax.numpy as jnp
from jax import lax
from jax.experimental import pallas as pl
from jax.experimental.pallas import tpu as pltpu
from jax.sharding import PartitionSpec as P

NSUB = 4
RATE = 500.0
AXES = ("gz", "gy")
F32 = jnp.float32
VMEM_BYTES = 12 << 20


def near(*dims):
    return pltpu.VMEM(dims, F32)


def far(*dims):
    return pltpu.HBM(dims, F32)


def call(kernel, name, outs, operands, scratch=(), cycles=0):
    whole, away = pl.BlockSpec(memory_space=pltpu.VMEM), pl.BlockSpec(memory_space=pltpu.HBM)
    inputs, in_specs = [], []
    for operand in operands:
        where, x = operand if isinstance(operand, tuple) else ("near", operand)
        if where != "plain":
            x = pltpu.with_memory_space_constraint(x, pltpu.VMEM if where == "near" else pltpu.HBM)
        inputs.append(x)
        in_specs.append(away if where == "far" else whole)
    out_specs = [away if isinstance(out, tuple) else whole for out in outs]
    result = pl.pallas_call(
        kernel,
        out_shape=[out[1] if isinstance(out, tuple) else out for out in outs],
        in_specs=in_specs,
        out_specs=out_specs,
        scratch_shapes=scratch,
        compiler_params=pltpu.CompilerParams(vmem_limit_bytes=VMEM_BYTES),
        cost_estimate=pl.CostEstimate(flops=0, bytes_accessed=cycles * 1024, transcendentals=0) if cycles else None,
        name=name,
    )(*inputs)
    return result if len(outs) > 1 else result[0]


def place():
    return (
        lax.axis_index("gz"),
        lax.axis_index("gy"),
        lax.axis_size("gz"),
        lax.axis_size("gy"),
    )


def pair_up(index):
    return index ^ 1


def same(index):
    return index


def z_other(index):
    return index + 1 if index % 2 else index - 1


def y_other(index):
    return (index + 1 if index % 2 else index - 1) % lax.axis_size("gy")


def permutation(z_partner, y_partner):
    z_count, y_count = lax.axis_size("gz"), lax.axis_size("gy")
    pairs = []
    for z in range(z_count):
        for y in range(y_count):
            to_z, to_y = z_partner(z), y_partner(y)
            if not 0 <= to_z < z_count:
                to_z, to_y = z, pair_up(y)
            pairs.append((z * y_count + y, to_z * y_count + to_y))
    return pairs


def send(x, z_partner=same, y_partner=same):
    return lax.ppermute(x, AXES, permutation(z_partner, y_partner))


def swap(x, axis, level):
    step = 1 << level
    if axis == "gy":
        step |= 1
    return lax.ppermute(x, axis, [(i, i ^ step) for i in range(lax.axis_size(axis))])


def levels_of(axis):
    return (lax.axis_size(axis) - 1).bit_length()


def rim_kernel(a, b, oa, ob, _, out):
    _, y, _, _ = place()
    width = a.shape[1]
    start = pl.multiple_of((1 - lax.rem(y, 2)) * (width - 8), 8)
    for half, ref in enumerate((a, b)):
        for k in range(11):
            out[11 * half + k] = ref[k, pl.ds(start, 8), :]


def rim(a, b, oa, ob, after):
    return call(rim_kernel, "rim", [near(22, 8, a.shape[2])], [a, b, oa, ob, ("far", after)], cycles=200)


def reciprocal(x):
    r = pl.reciprocal(x, approx=True)
    return r * (2.0 - x * r)


def factor(sides):
    state = []
    for read, count, r, phi, psi, ports, edge_low, edge_high in sides:
        first = read(0)
        before = first
        following = read(1)
        for j in range(1, count):
            here = following
            if j + 1 < count:
                following = read(j + 1)
            r[j] = reciprocal((0.5 * RATE) * (before + here))
            before = here
        one = jnp.ones_like(first)
        if phi is not None:
            phi[0] = one
            psi[count - 1] = one
        state.append([one, 1.0 + edge_low * first, one, 1.0 + edge_high * before, first, before])

    def faces(j):
        return [(r[j], r[count - j]) if j < count else None for _, count, r, _, _, _, _, _ in sides]

    longest = max(side[1] for side in sides)
    following = faces(1)
    for j in range(1, longest):
        here, following = following, faces(j + 1)
        for (_, count, _, _, _, _, _, _), s, pair in zip(sides, state, here):
            if pair is not None:
                s[0] = s[0] + pair[0] * s[1]
                s[1] = s[1] + s[0]
                s[2] = s[2] + pair[1] * s[3]
                s[3] = s[3] + s[2]
        for (_, count, _, phi, psi, _, _, _), s, pair in zip(sides, state, here):
            if pair is not None and phi is not None:
                phi[j] = s[0]
                psi[count - 1 - j] = s[2]
    for (_, _, _, _, _, ports, _, edge_high), s in zip(sides, state):
        if ports is not None:
            inverse = reciprocal(s[1] + edge_high * s[5] * s[0])
            ports[0] = s[2] * inverse
            ports[1] = inverse
            ports[2] = s[0] * inverse
            ports[3] = s[4]
            ports[4] = s[5]


def factor_sides(kappa, r_y, r_z, wanted_y, wanted_z):
    z, y, z_count, y_count = place()
    depth, width, _ = kappa.shape

    def flag(condition):
        return jnp.where(condition, RATE, 0.0)

    return (
        (lambda j: kappa[:, j, :], width, r_y, *wanted_y, flag(y == 0), flag(y == y_count - 1)),
        (lambda j: kappa[j], depth, r_z, *wanted_z, flag(z == 0), flag(z == z_count - 1)),
    )


def factor_kernel(kappa, _, phi_y, psi_y, phi_z, psi_z, r_y, r_z):
    factor(factor_sides(kappa, r_y, r_z, (phi_y, psi_y, None), (phi_z, psi_z, None)))


def factor_again(kappa, after):
    depth, width, band = kappa.shape
    along_y, along_z = (width, depth, band), (depth, width, band)
    return call(
        factor_kernel,
        "factor",
        [far(*along_y)] * 2 + [far(*along_z)] * 2,
        [("plain", kappa), after],
        scratch=[near(*along_y), near(*along_z)],
        cycles=4000,
    )


def begin_kernel(
    tracer, y_speed, z_speed, kappa_far, a_ref, b_ref, o_ref, e_ref, oa_ref, ob_ref,
    c, ys, zs, kappa, r_y, r_z, sem,
):
    arrivals = [
        pltpu.make_async_copy(source, target, sem.at[k])
        for k, (source, target) in enumerate(((kappa_far, kappa), (tracer, c), (y_speed, ys), (z_speed, zs)))
    ]
    for copy in arrivals:
        copy.start()
    z, y, _, _ = place()
    depth, width, _ = c.shape
    arrivals[0].wait()
    factor(factor_sides(kappa, r_y, r_z, (None, None, e_ref.at[11:16]), (None, None, a_ref.at[11:16])))
    for copy in arrivals[1:]:
        copy.wait()

    z_odd, y_odd = lax.rem(z, 2), lax.rem(y, 2)
    for ref, low in ((a_ref, z_odd), (b_ref, 1 - z_odd)):
        four, three = (1 - low) * (depth - 4), (1 - low) * (depth - 3)
        ref[0:4] = c[pl.ds(four, 4)]
        ref[4:8] = zs[pl.ds(four, 4)]
        ref[8:11] = ys[pl.ds(three, 3)]

    def rims(o_start, e_start):
        for ref, start in ((o_ref, o_start), (e_ref, e_start)):
            high = int(start > 0)
            for k in range(4):
                ref[k] = c[:, start + k, :]
                ref[4 + k] = ys[:, start + k, :]
            for k in range(3):
                ref[8 + k] = zs[:, start + high + k, :]
        high = int(o_start > 0)
        oa_start = pl.multiple_of((1 - z_odd) * (depth - 8), 8)
        ob_start = pl.multiple_of(z_odd * (depth - 8), 8)
        for f, field in enumerate((c, ys, zs)):
            for k in range(3):
                oa_ref[3 * f + k] = field[pl.ds(oa_start, 8), o_start + high + k, :]
                ob_ref[3 * f + k] = field[pl.ds(ob_start, 8), o_start + high + k, :]

    @pl.when(y_odd == 0)
    def _():
        rims(0, width - 4)

    @pl.when(y_odd == 1)
    def _():
        rims(width - 4, 0)


def begin(tracer, y_speed, z_speed, kappa):
    depth, width, band = tracer.shape
    along_y, along_z = (width, depth, band), (depth, width, band)
    return call(
        begin_kernel,
        "begin",
        [near(16, width, band), near(11, width, band), near(11, depth, band), near(16, depth, band)]
        + [near(9, 8, band)] * 2,
        [("far", x) for x in (tracer, y_speed, z_speed, kappa)],
        scratch=[near(*along_z)] * 4 + [near(*along_y), near(*along_z), pltpu.SemaphoreType.DMA((4,))],
        cycles=4000,
    )


def ports_kernel(axis, level, first_row, mine, theirs, out, joint):
    is_left = (lax.shift_right_logical(lax.axis_index(axis), level) & 1) == 0
    pairs = [(mine[first_row + k], theirs[first_row + k]) for k in range(5)]
    left = [jnp.where(is_left, m, t) for m, t in pairs]
    right = [jnp.where(is_left, t, m) for m, t in pairs]
    d = reciprocal(reciprocal((0.5 * RATE) * (left[4] + right[3])) + left[2] + right[0])
    out[0] = left[0] - left[1] * left[1] * d
    out[1] = left[1] * right[1] * d
    out[2] = right[2] - right[1] * right[1] * d
    out[3] = left[3]
    out[4] = right[4]
    joint[0] = d
    joint[1] = left[1]
    joint[2] = right[1]


def join_ports(mine, theirs, axis, level, first_row=0):
    _, lines, band = mine.shape

    def kernel(*refs):
        ports_kernel(axis, level, first_row, *refs)

    return call(kernel, "join_ports", [near(5, lines, band), near(3, lines, band)], [mine, theirs], cycles=100)


def join_levels(ports, axis, done):
    joints = []
    for level in range(done, levels_of(axis) - 1):
        ports, joint = join_ports(ports, swap(ports, axis, level), axis, level)
        joints.append(joint)
    return ports, joints


def first_join_kernel(mine, theirs, oa, ob, out, joint, oa_out, ob_out):
    ports_kernel("gy", 0, 11, mine, theirs, out, joint)
    oa_out[...] = oa[...]
    ob_out[...] = ob[...]


def first_join(mine, theirs, oa, ob):
    _, lines, band = mine.shape
    return call(
        first_join_kernel,
        "first_join",
        [near(5, lines, band), near(3, lines, band), near(*oa.shape), near(*ob.shape)],
        [mine, theirs, oa, ob],
        cycles=100,
    )


def source_kernel(axis, level, last, mine, theirs, joint, ports, out, flow_ref):
    index = lax.axis_index(axis)
    is_left = (lax.shift_right_logical(index, level) & 1) == 0
    pairs = [(mine[k], theirs[k]) for k in range(2)]
    left = [jnp.where(is_left, m, t) for m, t in pairs]
    right = [jnp.where(is_left, t, m) for m, t in pairs]
    flow = (left[1] - right[0]) * joint[0]
    flow_ref[0] = flow
    low, high = left[0] - joint[1] * flow, right[1] + joint[2] * flow
    if not last:
        out[0] = low
        out[1] = high
        return
    next_left = (lax.shift_right_logical(index, level + 1) & 1) == 0
    out[0] = jnp.where(next_left, high, low)
    out[1] = jnp.where(next_left, ports[2], ports[0])
    out[2] = jnp.where(next_left, ports[4], ports[3])


def join_sources(mine, theirs, joint, ports, axis, level):
    _, lines, band = mine.shape
    last = level + 2 == levels_of(axis)

    def kernel(*refs):
        source_kernel(axis, level, last, *refs)

    outs = [near(3 if last else 2, lines, band), near(1, lines, band)]
    return call(kernel, "join_sources", outs, [mine, theirs, joint, ports], cycles=100)


def end_currents(axis, mine, theirs, joints, flows):
    index = lax.axis_index(axis)
    level = len(joints)
    is_left = (lax.shift_right_logical(index, level) & 1) == 0
    d = reciprocal(reciprocal((0.5 * RATE) * (mine[2] + theirs[2])) + mine[1] + theirs[1])
    flow = (mine[0] - theirs[0]) * d
    zero = jnp.zeros_like(flow)
    low, high = jnp.where(is_left, zero, -flow), jnp.where(is_left, -flow, zero)
    for level in range(level - 1, -1, -1):
        joint = joints[level]
        is_left = (lax.shift_right_logical(index, level) & 1) == 0
        flow = flows[level][0] + (joint[1] * low - joint[2] * high) * joint[0]
        low, high = jnp.where(is_left, low, flow), jnp.where(is_left, -flow, high)
    return low, high


def solve_open(read, phi, psi, scale, base, ports, kept):
    count = base.shape[0]
    total = jnp.zeros(base.shape[1:], F32)
    for j in range(count):
        value = scale * read(j)
        kept[j] = value
        total = total + phi[j] * value
        base[j] = psi[j] * total
    ports[1] = total
    total = jnp.zeros(base.shape[1:], F32)
    for j in range(count - 1, -1, -1):
        base[j] = base[j] + phi[j] * total
        total = total + psi[j] * kept[j]
    ports[0] = total


def advect_kernel(
    tracer, y_speed, z_speed, a, b, o, e, oa, ob, ab, e_mine, phi_far, psi_far,
    base, sources, phi, psi, c, ys, zs, sy, sz, kept, sem,
):
    z, y, z_count, y_count = place()
    depth, width, band = tracer.shape
    rows, cols = depth + 8, width + 8
    copies = [
        pltpu.make_async_copy(own, field.at[pl.ds(4, depth), pl.ds(0, width), :], sem.at[k])
        for k, (field, own) in enumerate(((c, tracer), (ys, y_speed), (zs, z_speed)))
    ]
    copies += [
        pltpu.make_async_copy(phi_far, phi, sem.at[3]),
        pltpu.make_async_copy(psi_far, psi, sem.at[4]),
    ]
    for copy in copies:
        copy.start()
    z_odd, y_odd = lax.rem(z, 2), lax.rem(y, 2)
    keep_b = jnp.where((z_odd == 0) & (z == 0) | (z_odd == 1) & (z == z_count - 1), 0.0, 1.0)
    keep_o = jnp.where((y_odd == 0) & (y == 0) | (y_odd == 1) & (y == y_count - 1), 0.0, 1.0)
    column = lax.broadcasted_iota(jnp.int32, (8, band), 0)
    outside = (column < 4) & (y == y_count - 1) | (column >= 4) & (y == 0)
    inside = jnp.where(outside, 0.0, 1.0)

    for field in (c, ys, zs):
        field[0:4, width:cols, :] = jnp.zeros((4, 8, band), F32)
        field[4 + depth : rows, width:cols, :] = jnp.zeros((4, 8, band), F32)
    ys[0:1, 0:width, :] = jnp.zeros((1, width, band), F32)
    ys[rows - 1 : rows, 0:width, :] = jnp.zeros((1, width, band), F32)
    for ref, low, keep in ((a, z_odd, None), (b, 1 - z_odd, keep_b)):
        scale = (lambda v: v) if keep is None else (lambda v: v * keep)
        four = jnp.where(low == 1, 0, depth + 4)
        three = jnp.where(low == 1, 1, depth + 4)
        c[pl.ds(four, 4), 0:width, :] = scale(ref[0:4])
        zs[pl.ds(four, 4), 0:width, :] = scale(ref[4:8])
        ys[pl.ds(three, 3), 0:width, :] = scale(ref[8:11])

    def sides(o_low):
        def columns(ref, low, scale):
            start = width + 4 * int(low)
            shift = int(low)
            for k in range(4):
                c[4 : 4 + depth, start + k, :] = scale(ref[k])
                ys[4 : 4 + depth, start + k, :] = scale(ref[4 + k])
            for k in range(3):
                zs[4 : 4 + depth, start + shift + k, :] = scale(ref[8 + k])
            far_column = start if low else start + 3
            zs[4 : 4 + depth, far_column, :] = jnp.zeros((depth, band), F32)

        columns(o, o_low, lambda v: v * keep_o)
        columns(e, not o_low, lambda v: v)

        def from_pair(half, z_low):
            start = width if o_low else width + 4
            block = slice(0, 4) if o_low else slice(4, 8)
            zr = 0 if z_low else depth + 4
            z3 = 1 if z_low else depth + 4
            keep = 1.0 if half == 0 else keep_b
            c[zr : zr + 4, start : start + 4, :] = ab[11 * half : 11 * half + 4, block, :] * keep
            zs[zr : zr + 4, start : start + 4, :] = ab[11 * half + 4 : 11 * half + 8, block, :] * keep
            ys[z3 : z3 + 3, start : start + 4, :] = ab[11 * half + 8 : 11 * half + 11, block, :] * keep

        def from_corner(ref, z_low, keep):
            start = width + (5 if o_low else 0)
            zr = 1 if z_low else depth + 4
            src = 5 if z_low else 0
            for f, field in enumerate((c, ys, zs)):
                for k in range(3):
                    field[zr : zr + 3, start + k, :] = ref[3 * f + k, src : src + 3, :] * keep

        @pl.when(z_odd == 0)
        def _():
            from_pair(0, False)
            from_pair(1, True)
            from_corner(oa, False, keep_o)
            from_corner(ob, True, keep_o * keep_b)

        @pl.when(z_odd == 1)
        def _():
            from_pair(0, True)
            from_pair(1, False)
            from_corner(oa, True, keep_o)
            from_corner(ob, False, keep_o * keep_b)

    @pl.when(y_odd == 0)
    def _():
        sides(True)

    @pl.when(y_odd == 1)
    def _():
        sides(False)

    for copy in copies[:3]:
        copy.wait()

    def up(v):
        return pltpu.roll(v, cols - 1, 0)

    def down(v):
        return pltpu.roll(v, 1, 0)

    def flux(speed, here, after):
        return speed * jnp.where(speed > 0.0, here, after)

    def faces(r, before):
        v = ys[r]
        sy[r] = 0.5 * (v + up(v))
        after = zs[r + 1]
        sz[r] = 0.5 * (before + after)
        return after

    lax.fori_loop(0, rows - 1, faces, zs[0], unroll=3)

    keep_low = jnp.where(z == 0, 0.0, 1.0)
    keep_high = jnp.where(z == z_count - 1, 0.0, 1.0)
    for step in range(1, NSUB + 1):
        here = c[step]

        def row(r, carry):
            here, below = carry
            after = c[r + 1]
            above = flux(sz[r], here, after)
            across = flux(sy[r], here, up(here))
            new = here - (across - down(across)) - (above - below)
            c[r, 0:width, :] = new[0:width]
            c[r, width:cols, :] = new[width:cols] * inside
            return after, above

        lax.fori_loop(step, rows - step, row, (here, flux(sz[step - 1], c[step - 1], here)), unroll=4)
        if step < NSUB:
            c[3] = c[3] * keep_low
            c[4 + depth] = c[4 + depth] * keep_high

    for copy in copies[3:]:
        copy.wait()
    solve_open(lambda j: c[4 : 4 + depth, j, :], phi, psi, e_mine[12], base, sources, kept)


def advect(tracer, y_speed, z_speed, halos, e_mine, phi, psi):
    depth, width, band = tracer.shape
    padded = near(depth + 8, width + 8, band)
    along_y = near(width, depth, band)
    return call(
        advect_kernel,
        "advect",
        [along_y, near(2, depth, band), along_y, along_y],
        [("far", x) for x in (tracer, y_speed, z_speed)]
        + list(halos)
        + [e_mine, ("far", phi), ("far", psi)],
        scratch=[padded] * 5 + [along_y, pltpu.SemaphoreType.DMA((5,))],
        cycles=5000,
    )


def turn_kernel(levels, *refs):
    mine, theirs = refs[0:2]
    joints, flows = refs[2 : 2 + levels], refs[2 + levels : 2 + 2 * levels]
    (
        ports_y, base_y, phi_y, psi_y, ports_z, phi_far, psi_far,
        base, sources, phi, psi, u, kept, sem,
    ) = refs[2 + 2 * levels :]
    copies = [
        pltpu.make_async_copy(phi_far, phi, sem.at[0]),
        pltpu.make_async_copy(psi_far, psi, sem.at[1]),
    ]
    for copy in copies:
        copy.start()
    low, high = end_currents("gy", mine, theirs, joints, flows)
    scale = ports_y[12]
    low, high = low * scale, high * scale
    for j in range(base_y.shape[0]):
        u[:, j, :] = base_y[j] + low * psi_y[j] + high * phi_y[j]
    for copy in copies:
        copy.wait()
    solve_open(lambda k: u[k], phi, psi, ports_z[12], base, sources, kept)


def turn(mine, theirs, joints, flows, ports_y, base_y, phi_y, psi_y, ports_z, phi_z, psi_z):
    width, depth, band = base_y.shape
    along_z = near(depth, width, band)

    def kernel(*refs):
        turn_kernel(len(joints), *refs)

    return call(
        kernel,
        "turn",
        [along_z, near(2, width, band), along_z, along_z],
        [mine, theirs, *joints, *flows, ports_y, base_y, phi_y, psi_y, ports_z]
        + [("far", phi_z), ("far", psi_z)],
        scratch=[along_z, along_z, pltpu.SemaphoreType.DMA((2,))],
        cycles=1500,
    )


def finish_kernel(levels, *refs):
    mine, theirs = refs[0:2]
    joints, flows = refs[2 : 2 + levels], refs[2 + levels : 2 + 2 * levels]
    ports_z, base, phi, psi, out, u, sem = refs[2 + 2 * levels :]
    low, high = end_currents("gz", mine, theirs, joints, flows)
    scale = ports_z[12]
    low, high = low * scale, high * scale
    depth = base.shape[0]
    part = depth // 4
    copies = []
    for p in range(4):
        for k in range(p * part, (p + 1) * part):
            u[k] = base[k] + low * psi[k] + high * phi[k]
        block = pl.ds(p * part, part)
        copies.append(pltpu.make_async_copy(u.at[block], out.at[block], sem.at[p]))
        copies[-1].start()
    for copy in copies:
        copy.wait()


def finish(mine, theirs, joints, flows, ports_z, base, phi, psi):
    def kernel(*refs):
        finish_kernel(len(joints), *refs)

    return call(
        kernel,
        "finish",
        [("far", jax.ShapeDtypeStruct(base.shape, F32))],
        [mine, theirs, *joints, *flows, ports_z, base, phi, psi],
        scratch=[near(*base.shape), pltpu.SemaphoreType.DMA((4,))],
        cycles=1000,
    )


def exchange_sources(sources, ports, joints, axis):
    flows = []
    for level, joint in enumerate(joints):
        theirs = swap(sources, axis, level)
        sources, flow = join_sources(sources, theirs, joint, ports, axis, level)
        flows.append(flow)
    return sources, swap(sources, axis, len(joints)), flows


def local(tracer, y_speed, z_speed, kappa):
    a_mine, b, o, e_mine, oa, ob = begin(tracer, y_speed, z_speed, kappa)
    o = send(o, y_partner=y_other)
    e = swap(e_mine, "gy", 0)
    a = send(a_mine, z_partner=pair_up)
    b = send(b, z_partner=z_other)
    ports_y, joint_y, oa, ob = first_join(e_mine, e, oa, ob)
    oa = send(oa, z_partner=pair_up, y_partner=y_other)
    ob = send(ob, z_partner=z_other, y_partner=y_other)
    phi_y, psi_y, phi_z, psi_z = factor_again(kappa, ports_y)
    ab = send(rim(a, b, oa, ob, phi_y), y_partner=pair_up)

    ports_y, joints = join_levels(ports_y, "gy", 1)
    joints_y = [joint_y] + joints
    ports_z, joint_z = join_ports(a_mine, a, "gz", 0, first_row=11)
    ports_z, joints = join_levels(ports_z, "gz", 1)
    joints_z = [joint_z] + joints

    base, sources, phi_y, psi_y = advect(
        tracer, y_speed, z_speed, (a, b, o, e, oa, ob, ab), e_mine, phi_y, psi_y
    )
    mine, theirs, flows = exchange_sources(sources, ports_y, joints_y, "gy")
    base, sources, phi_z, psi_z = turn(
        mine, theirs, joints_y, flows, e_mine, base, phi_y, psi_y, a_mine, phi_z, psi_z
    )
    mine, theirs, flows = exchange_sources(sources, ports_z, joints_z, "gz")
    return finish(mine, theirs, joints_z, flows, a_mine, base, phi_z, psi_z)


def solution(mesh):
    spec = P("gz", "gy", None)
    return jax.shard_map(
        local, mesh=mesh, in_specs=(spec,) * 4, out_specs=spec, check_vma=False
    )
```

```python
import jax
import jax.numpy as jnp
from jax import lax
from jax.experimental import pallas as pl
from jax.experimental.pallas import tpu as pltpu
from jax.sharding import PartitionSpec as P

NSUB = 4
RATE = 500.0
AXES = ("gz", "gy")
F32 = jnp.float32
VMEM_BYTES = 12 << 20


def near(*dims):
    return pltpu.VMEM(dims, F32)


def far(*dims):
    return pltpu.HBM(dims, F32)


def call(kernel, name, outs, operands, scratch=(), cycles=0):
    whole, away = pl.BlockSpec(memory_space=pltpu.VMEM), pl.BlockSpec(memory_space=pltpu.HBM)
    inputs, in_specs = [], []
    for operand in operands:
        where, x = operand if isinstance(operand, tuple) else ("near", operand)
        if where != "plain":
            x = pltpu.with_memory_space_constraint(x, pltpu.VMEM if where == "near" else pltpu.HBM)
        inputs.append(x)
        in_specs.append(away if where == "far" else whole)
    out_specs = [away if isinstance(out, tuple) else whole for out in outs]
    result = pl.pallas_call(
        kernel,
        out_shape=[out[1] if isinstance(out, tuple) else out for out in outs],
        in_specs=in_specs,
        out_specs=out_specs,
        scratch_shapes=scratch,
        compiler_params=pltpu.CompilerParams(vmem_limit_bytes=VMEM_BYTES),
        cost_estimate=pl.CostEstimate(flops=0, bytes_accessed=cycles * 1024, transcendentals=0) if cycles else None,
        name=name,
    )(*inputs)
    return result if len(outs) > 1 else result[0]


def place():
    return (
        lax.axis_index("gz"),
        lax.axis_index("gy"),
        lax.axis_size("gz"),
        lax.axis_size("gy"),
    )


def pair_up(index):
    return index ^ 1


def same(index):
    return index


def z_other(index):
    return index + 1 if index % 2 else index - 1


def y_other(index):
    return (index + 1 if index % 2 else index - 1) % lax.axis_size("gy")


def permutation(z_partner, y_partner):
    z_count, y_count = lax.axis_size("gz"), lax.axis_size("gy")
    pairs = []
    for z in range(z_count):
        for y in range(y_count):
            to_z, to_y = z_partner(z), y_partner(y)
            if not 0 <= to_z < z_count:
                to_z, to_y = z, pair_up(y)
            pairs.append((z * y_count + y, to_z * y_count + to_y))
    return pairs


def send(x, z_partner=same, y_partner=same):
    return lax.ppermute(x, AXES, permutation(z_partner, y_partner))


def swap(x, axis, level):
    step = 1 << level
    if axis == "gy":
        step |= 1
    return lax.ppermute(x, axis, [(i, i ^ step) for i in range(lax.axis_size(axis))])


def levels_of(axis):
    return (lax.axis_size(axis) - 1).bit_length()


def begin_kernel(tracer, y_speed, z_speed, kappa_far, a_ref, b_ref, o_ref, e_ref, c, ys, zs, kappa, kappa_y, r_y, sem):
    arrivals = [
        pltpu.make_async_copy(source, target, sem.at[k])
        for k, (source, target) in enumerate(((kappa_far, kappa), (tracer, c), (z_speed, zs), (y_speed, ys)))
    ]
    for copy in arrivals:
        copy.start()
    z, y, _, y_count = place()
    depth, width, _ = c.shape
    z_odd, y_odd = lax.rem(z, 2), lax.rem(y, 2)
    arrivals[0].wait()
    ports = e_ref.at[11:16]
    kappa_y[...] = turned(kappa[...])
    ports[3], ports[4] = resistances(kappa_y, r_y)
    factor(((lambda j: r_y[j], width, *outer(ports, y, y_count), None, ports),))
    for copy in arrivals[1:]:
        copy.wait()
    for ref, low in ((a_ref, z_odd), (b_ref, 1 - z_odd)):
        four, three = (1 - low) * (depth - 4), (1 - low) * (depth - 3)
        ref[0:4] = c[pl.ds(four, 4)]
        ref[4:8] = zs[pl.ds(four, 4)]
        ref[8:11] = ys[pl.ds(three, 3)]

    def rims(o_low):
        for ref, low in ((o_ref, o_low), (e_ref, not o_low)):
            tile = slice(0, 8) if low else slice(width - 8, width)
            four, three = (0, 0) if low else (4, 5)
            ref[0:4] = turned(c[:, tile, :])[four : four + 4]
            ref[4:8] = turned(ys[:, tile, :])[four : four + 4]
            ref[8:11] = turned(zs[:, tile, :])[three : three + 3]

    @pl.when(y_odd == 0)
    def _():
        rims(True)

    @pl.when(y_odd == 1)
    def _():
        rims(False)


def begin(tracer, y_speed, z_speed, kappa):
    depth, width, band = tracer.shape
    return call(
        begin_kernel,
        "begin",
        [near(11, width, band)] * 2 + [near(11, depth, band), near(16, depth, band)],
        [("far", x) for x in (tracer, y_speed, z_speed, kappa)],
        scratch=[near(depth, width, band)] * 4 + [near(width, depth, band)] * 2 + [pltpu.SemaphoreType.DMA((4,))],
        cycles=2000,
    )


RIM_ROWS = 22


def rim_kernel(a, b, _, for_pair, for_other):
    z, y, _, _ = place()
    width = a.shape[1]
    z_odd, y_odd = lax.rem(z, 2) == 1, lax.rem(y, 2)
    start = pl.multiple_of((1 - y_odd) * (width - 8), 8)

    def corners(first):
        for f, (row, count) in enumerate(((0, 4), (8, 3), (4, 4))):
            for k in range(3):
                column_a, column_b = (ref[row : row + count, first + k, :] for ref in (a, b))
                for_other[3 * f + k, 4 - count : 4, :] = jnp.where(z_odd, column_a, column_b)
                for_other[3 * f + k, 4 : 4 + count, :] = jnp.where(z_odd, column_b, column_a)

    for tile in range(3, 6):
        for_other[tile] = jnp.zeros(for_other.shape[1:], F32)

    @pl.when(y_odd == 0)
    def _():
        corners(0)

    @pl.when(y_odd == 1)
    def _():
        corners(width - 3)

    for half, ref in enumerate((a, b)):
        for k in range(11):
            for_pair[11 * half + k] = ref[k, pl.ds(start, 8), :]


def rim(a, b, after):
    band = a.shape[2]
    return call(rim_kernel, "rim", [near(22, 8, band), near(9, 8, band)], [a, b, after], cycles=200)


def reciprocal(x):
    r = pl.reciprocal(x, approx=True)
    return r * (2.0 - x * r)


def turned(x):
    return jnp.swapaxes(x, 0, 1)


def resistances(kappa, r):
    count = kappa.shape[0]
    before, following = kappa[0], kappa[1]
    r[0] = jnp.zeros_like(before)
    for j in range(1, count):
        here = following
        if j + 1 < count:
            following = kappa[j + 1]
        r[j] = reciprocal((0.5 * RATE) * (before + here))
        before = here
    return kappa[0], before


def factor(sides):
    state = []
    for read, count, edge_low, edge_high, keep, _ in sides:
        one = jnp.ones_like(edge_low)
        if keep:
            keep[0][0] = one
            keep[1][count - 1] = one
        state.append([one, 1.0 + edge_low, one, 1.0 + edge_high])

    def faces(j):
        return [(read(j), read(count - j)) if j < count else None for read, count, _, _, _, _ in sides]

    longest = max(side[1] for side in sides)
    following = faces(1)
    for j in range(1, longest):
        here, following = following, faces(j + 1)
        for s, pair in zip(state, here):
            if pair is not None:
                s[0] = s[0] + pair[0] * s[1]
                s[1] = s[1] + s[0]
                s[2] = s[2] + pair[1] * s[3]
                s[3] = s[3] + s[2]
        for (_, count, _, _, keep, _), s, pair in zip(sides, state, here):
            if pair is not None and keep:
                keep[0][j] = s[0]
                keep[1][count - 1 - j] = s[2]
    for (_, _, _, edge_high, _, ports), s in zip(sides, state):
        if ports is not None:
            inverse = reciprocal(s[1] + edge_high * s[0])
            ports[0] = s[2] * inverse
            ports[1] = inverse
            ports[2] = s[0] * inverse


def outer(ports, index, count):
    return jnp.where(index == 0, RATE, 0.0) * ports[3], jnp.where(index == count - 1, RATE, 0.0) * ports[4]


def factor_kernel(kappa, r_y_far, r_z_far, ports_z, kappa_y, r_y, r_z, sem):
    z, _, z_count, _ = place()
    depth = kappa.shape[0]
    y_copy = pltpu.make_async_copy(r_y, r_y_far, sem.at[0])
    z_copy = pltpu.make_async_copy(r_z, r_z_far, sem.at[1])
    ports_z[3], ports_z[4] = resistances(kappa, r_z)
    z_copy.start()
    kappa_y[...] = turned(kappa[...])
    resistances(kappa_y, r_y)
    y_copy.start()
    factor(((lambda j: r_z[j], depth, *outer(ports_z, z, z_count), None, ports_z),))
    y_copy.wait()
    z_copy.wait()


def factor_lines(kappa):
    depth, width, band = kappa.shape
    along_y, along_z = (width, depth, band), (depth, width, band)
    return call(
        factor_kernel,
        "factor",
        [("far", far(*along_y)), ("far", far(*along_z)), near(5, width, band)],
        [("plain", kappa)],
        scratch=[near(*along_y), near(*along_y), near(*along_z), pltpu.SemaphoreType.DMA((2,))],
        cycles=4000,
    )


def ports_kernel(axis, level, first_row, mine, theirs, out, joint):
    is_left = (lax.shift_right_logical(lax.axis_index(axis), level) & 1) == 0
    pairs = [(mine[first_row + k], theirs[first_row + k]) for k in range(5)]
    left = [jnp.where(is_left, m, t) for m, t in pairs]
    right = [jnp.where(is_left, t, m) for m, t in pairs]
    d = reciprocal(reciprocal((0.5 * RATE) * (left[4] + right[3])) + left[2] + right[0])
    out[0] = left[0] - left[1] * left[1] * d
    out[1] = left[1] * right[1] * d
    out[2] = right[2] - right[1] * right[1] * d
    out[3] = left[3]
    out[4] = right[4]
    joint[0] = d
    joint[1] = left[1]
    joint[2] = right[1]


def join_ports(mine, theirs, axis, level, first_row=0):
    _, lines, band = mine.shape

    def kernel(*refs):
        ports_kernel(axis, level, first_row, *refs)

    return call(kernel, "join_ports", [near(5, lines, band), near(3, lines, band)], [mine, theirs], cycles=100)


def join_levels(ports, axis, done):
    joints = []
    for level in range(done, levels_of(axis) - 1):
        ports, joint = join_ports(ports, swap(ports, axis, level), axis, level)
        joints.append(joint)
    return ports, joints


def source_kernel(axis, level, mine, theirs, joint, *refs):
    *ports, out, flow_ref = refs
    index = lax.axis_index(axis)
    is_left = (lax.shift_right_logical(index, level) & 1) == 0
    pairs = [(mine[k], theirs[k]) for k in range(2)]
    left = [jnp.where(is_left, m, t) for m, t in pairs]
    right = [jnp.where(is_left, t, m) for m, t in pairs]
    flow = (left[1] - right[0]) * joint[0]
    flow_ref[0] = flow
    low, high = left[0] - joint[1] * flow, right[1] + joint[2] * flow
    if not ports:
        out[0] = low
        out[1] = high
        return
    ports = ports[0]
    next_left = (lax.shift_right_logical(index, level + 1) & 1) == 0
    out[0] = jnp.where(next_left, high, low)
    out[1] = jnp.where(next_left, ports[2], ports[0])
    out[2] = jnp.where(next_left, ports[4], ports[3])


def join_sources(mine, theirs, joint, ports, axis, level):
    _, lines, band = mine.shape
    last = [ports] if level + 2 == levels_of(axis) else []

    def kernel(*refs):
        source_kernel(axis, level, *refs)

    outs = [near(3 if last else 2, lines, band), near(1, lines, band)]
    return call(kernel, "join_sources", outs, [mine, theirs, joint, *last], cycles=100)


def end_currents(axis, mine, theirs, joints, flows):
    index = lax.axis_index(axis)
    level = len(joints)
    is_left = (lax.shift_right_logical(index, level) & 1) == 0
    d = reciprocal(reciprocal((0.5 * RATE) * (mine[2] + theirs[2])) + mine[1] + theirs[1])
    flow = (mine[0] - theirs[0]) * d
    zero = jnp.zeros_like(flow)
    low, high = jnp.where(is_left, zero, -flow), jnp.where(is_left, -flow, zero)
    for level in range(level - 1, -1, -1):
        joint = joints[level]
        is_left = (lax.shift_right_logical(index, level) & 1) == 0
        flow = flows[level][0] + (joint[1] * low - joint[2] * high) * joint[0]
        low, high = jnp.where(is_left, low, flow), jnp.where(is_left, -flow, high)
    return low, high


def solve_open(values, phi, psi, scale, base, ports):
    count = base.shape[0]
    total = jnp.zeros(base.shape[1:], F32)
    following = (values[0], phi[0], psi[0])
    for j in range(count):
        value, low, high = following
        if j + 1 < count:
            following = (values[j + 1], phi[j + 1], psi[j + 1])
        total = total + low * value
        base[j] = high * total
    ports[1] = scale * total
    total = jnp.zeros(base.shape[1:], F32)
    following = (base[count - 1], values[count - 1], phi[count - 1], psi[count - 1])
    for j in range(count - 1, -1, -1):
        below, value, low, high = following
        if j > 0:
            following = (base[j - 1], values[j - 1], phi[j - 1], psi[j - 1])
        base[j] = scale * (below + low * total)
        total = total + high * value
    ports[0] = scale * total


def advect_kernel(
    tracer, y_speed, z_speed, a, b, o, e, corner, ab, e_mine, r_y_far, r_z_far, ports_z,
    base, sources, r_y, r_z, ports_out, c, ys, zs, sy, sz, phi, psi, kept, sem,
):
    z, y, z_count, y_count = place()
    depth, width, band = tracer.shape
    rows, cols = depth + 8, width + 8
    copies = [
        pltpu.make_async_copy(own, field.at[pl.ds(4, depth), pl.ds(0, width), :], sem.at[k])
        for k, (field, own) in enumerate(((ys, y_speed), (zs, z_speed), (c, tracer)))
    ]
    y_copy = pltpu.make_async_copy(r_y_far, r_y, sem.at[3])
    z_copy = pltpu.make_async_copy(r_z_far, r_z, sem.at[4])
    y_copy.start()
    for copy in copies:
        copy.start()
    z_copy.start()
    ports_out[...] = ports_z[...]
    z_odd, y_odd = lax.rem(z, 2), lax.rem(y, 2)
    keep_b = jnp.where((z_odd == 0) & (z == 0) | (z_odd == 1) & (z == z_count - 1), 0.0, 1.0)
    keep_o = jnp.where((y_odd == 0) & (y == 0) | (y_odd == 1) & (y == y_count - 1), 0.0, 1.0)
    keep_below = keep_o * jnp.where(z_odd == 0, keep_b, 1.0)
    keep_above = keep_o * jnp.where(z_odd == 1, keep_b, 1.0)
    column = lax.broadcasted_iota(jnp.int32, (8, band), 0)
    outside = (column < 4) & (y == y_count - 1) | (column >= 4) & (y == 0)
    inside = jnp.where(outside, 0.0, 1.0)

    for field in (c, ys, zs):
        field[0:4, width:cols, :] = jnp.zeros((4, 8, band), F32)
        field[4 + depth : rows, width:cols, :] = jnp.zeros((4, 8, band), F32)
    ys[0:1, 0:width, :] = jnp.zeros((1, width, band), F32)
    ys[rows - 1 : rows, 0:width, :] = jnp.zeros((1, width, band), F32)
    for ref, low, keep in ((a, z_odd, None), (b, 1 - z_odd, keep_b)):
        scale = (lambda v: v) if keep is None else (lambda v: v * keep)
        four = jnp.where(low == 1, 0, depth + 4)
        three = jnp.where(low == 1, 1, depth + 4)
        c[pl.ds(four, 4), 0:width, :] = scale(ref[0:4])
        zs[pl.ds(four, 4), 0:width, :] = scale(ref[4:8])
        ys[pl.ds(three, 3), 0:width, :] = scale(ref[8:11])

    def sides(o_low):
        def columns(first, count):
            other, pair = o[first : first + count] * keep_o, e[first : first + count]
            above, below = (pair, other) if o_low else (other, pair)
            empty = [jnp.zeros((4 - count, depth, band), F32)] if count < 4 else []
            return turned(jnp.concatenate([above, *empty, *empty, below], axis=0))

        c[4 : 4 + depth, width:cols, :] = columns(0, 4)
        ys[4 : 4 + depth, width:cols, :] = columns(4, 4)
        zs[4 : 4 + depth, width:cols, :] = columns(8, 3)

        def from_pair(half, z_low):
            start = width if o_low else width + 4
            first = 0 if o_low else 4
            zr = 0 if z_low else depth + 4
            z3 = 1 if z_low else depth + 4
            keep = 1.0 if half == 0 else keep_b
            for k in range(11):
                field, row = ((c, zr + k), (zs, zr + k - 4), (ys, z3 + k - 8))[k // 4]
                field[row, start : start + 4, :] = ab[11 * half + k, first : first + 4, :] * keep

        start = width + (5 if o_low else 0)
        for f, (field, count) in enumerate(((c, 4), (ys, 3), (zs, 4))):
            for k in range(3):
                below, above = corner[3 * f + k, 4 - count : 4, :], corner[3 * f + k, 4 : 4 + count, :]
                field[4 - count : 4, start + k, :] = below * keep_below
                field[depth + 4 : depth + 4 + count, start + k, :] = above * keep_above

        @pl.when(z_odd == 0)
        def _():
            from_pair(0, False)
            from_pair(1, True)

        @pl.when(z_odd == 1)
        def _():
            from_pair(0, True)
            from_pair(1, False)

    @pl.when(y_odd == 0)
    def _():
        sides(True)

    @pl.when(y_odd == 1)
    def _():
        sides(False)

    y_copy.wait()
    factor(((lambda j: r_y[j], width, *outer(e_mine.at[11:16], y, y_count), (phi, psi), None),))
    for copy in copies[:2]:
        copy.wait()

    def up(v):
        return pltpu.roll(v, cols - 1, 0)

    def down(v):
        return pltpu.roll(v, 1, 0)

    def flux(speed, here, after):
        return speed * jnp.where(speed > 0.0, here, after)

    def faces(r, before):
        v = ys[r]
        sy[r] = 0.5 * (v + up(v))
        after = zs[r + 1]
        sz[r] = 0.5 * (before + after)
        return after

    lax.fori_loop(0, rows - 1, faces, zs[0], unroll=3)
    copies[2].wait()

    keep_low = jnp.where(z == 0, 0.0, 1.0)
    keep_high = jnp.where(z == z_count - 1, 0.0, 1.0)
    for step in range(1, NSUB + 1):
        here = c[step]

        def row(r, carry):
            here, below = carry
            after = c[r + 1]
            above = flux(sz[r], here, after)
            across = flux(sy[r], here, up(here))
            new = here - (across - down(across)) - (above - below)
            c[r, 0:width, :] = new[0:width]
            c[r, width:cols, :] = new[width:cols] * inside
            return after, above

        lax.fori_loop(step, rows - step, row, (here, flux(sz[step - 1], c[step - 1], here)), unroll=4)
        if step < NSUB:
            c[3] = c[3] * keep_low
            c[4 + depth] = c[4 + depth] * keep_high

    z_copy.wait()
    kept[...] = turned(c[4 : 4 + depth, 0:width, :])
    solve_open(kept, phi, psi, e_mine[12], base, sources)


def advect(tracer, y_speed, z_speed, halos, ports_y, r_y, r_z, ports_z):
    depth, width, band = tracer.shape
    padded = near(depth + 8, width + 8, band)
    along_y, along_z = near(width, depth, band), near(depth, width, band)
    return call(
        advect_kernel,
        "advect",
        [along_y, near(2, depth, band), along_y, along_z, near(5, width, band)],
        [("far", x) for x in (tracer, y_speed, z_speed)]
        + list(halos)
        + [ports_y, ("far", r_y), ("far", r_z), ports_z],
        scratch=[padded] * 5 + [along_y] * 3 + [pltpu.SemaphoreType.DMA((5,))],
        cycles=5000,
    )


def turn_kernel(levels, *refs):
    mine, theirs = refs[0:2]
    joints, flows = refs[2 : 2 + levels], refs[2 + levels : 2 + 2 * levels]
    ports_y, base_y, r_y, ports_z, r_z, _, base, sources, phi, psi, u, kept = refs[2 + 2 * levels :]
    z, y, z_count, y_count = place()
    width, depth = base_y.shape[0], base.shape[0]
    ports_y = ports_y.at[11:16]
    low, high = end_currents("gy", mine, theirs, joints, flows)
    edge, _ = outer(ports_y, y, y_count)
    value = low * ports_y[0] + high * ports_y[1]
    current = (1.0 + edge) * value - low
    u[0] = base_y[0] + value
    following = (r_y[1], base_y[1])
    for j in range(1, width):
        (r, own), following = following, (r_y[j + 1], base_y[j + 1]) if j + 1 < width else None
        value = value + r * current
        current = current + value
        u[j] = own + value
    factor(((lambda k: r_z[k], depth, *outer(ports_z, z, z_count), (phi, psi), None),))
    kept[...] = turned(u[...])
    solve_open(kept, phi, psi, ports_z[1], base, sources)


def turn(mine, theirs, joints, flows, ports_y, base_y, r_y, ports_z, r_z, after):
    width, depth, band = base_y.shape
    along_z = near(depth, width, band)

    def kernel(*refs):
        turn_kernel(len(joints), *refs)

    return call(
        kernel,
        "turn",
        [along_z, near(2, width, band), along_z, along_z],
        [mine, theirs, *joints, *flows, ports_y, base_y, r_y, ports_z, r_z, after],
        scratch=[near(width, depth, band), along_z],
        cycles=1500,
    )


def finish_kernel(levels, *refs):
    mine, theirs = refs[0:2]
    joints, flows = refs[2 : 2 + levels], refs[2 + levels : 2 + 2 * levels]
    ports_z, base, phi, psi, out, u, sem = refs[2 + 2 * levels :]
    low, high = end_currents("gz", mine, theirs, joints, flows)
    scale = ports_z[1]
    low, high = low * scale, high * scale
    depth = base.shape[0]
    part = depth // 4
    copies = []
    for p in range(4):
        for k in range(p * part, (p + 1) * part):
            u[k] = base[k] + low * psi[k] + high * phi[k]
        block = pl.ds(p * part, part)
        copies.append(pltpu.make_async_copy(u.at[block], out.at[block], sem.at[p]))
        copies[-1].start()
    for copy in copies:
        copy.wait()


def finish(mine, theirs, joints, flows, ports_z, base, phi, psi):
    def kernel(*refs):
        finish_kernel(len(joints), *refs)

    return call(
        kernel,
        "finish",
        [("far", jax.ShapeDtypeStruct(base.shape, F32))],
        [mine, theirs, *joints, *flows, ports_z, base, phi, psi],
        scratch=[near(*base.shape), pltpu.SemaphoreType.DMA((4,))],
        cycles=1000,
    )


def exchange_sources(sources, ports, joints, axis):
    flows = []
    for level, joint in enumerate(joints):
        theirs = swap(sources, axis, level)
        sources, flow = join_sources(sources, theirs, joint, ports, axis, level)
        flows.append(flow)
    return sources, swap(sources, axis, len(joints)), flows


def local(tracer, y_speed, z_speed, kappa):
    a, b, o, e_mine = begin(tracer, y_speed, z_speed, kappa)
    e = swap(e_mine, "gy", 0)
    a = send(a, z_partner=pair_up)
    b = send(b, z_partner=z_other)
    o = send(o, y_partner=y_other)
    r_y, r_z, ports_z = factor_lines(kappa)
    for_pair, for_other = rim(a, b, ports_z)
    corner = send(for_other, y_partner=y_other)
    ab = swap(for_pair, "gy", 0)

    joined_y, joint_y = join_ports(e_mine, e, "gy", 0, first_row=11)
    joined_y, joints = join_levels(joined_y, "gy", 1)
    joints_y = [joint_y] + joints

    base, sources, r_y, r_z, ports_z = advect(
        tracer, y_speed, z_speed, (a, b, o, e, corner, ab), e_mine, r_y, r_z, ports_z
    )
    joined_z, joints_z = join_levels(ports_z, "gz", 0)
    mine, theirs, flows = exchange_sources(sources, joined_y, joints_y, "gy")
    base, sources, phi_z, psi_z = turn(
        mine, theirs, joints_y, flows, e_mine, base, r_y, ports_z, r_z, joints_z[-1]
    )
    mine, theirs, flows = exchange_sources(sources, joined_z, joints_z, "gz")
    return finish(mine, theirs, joints_z, flows, ports_z, base, phi_z, psi_z)


def solution(mesh):
    spec = P("gz", "gy", None)
    return jax.shard_map(
        local, mesh=mesh, in_specs=(spec,) * 4, out_specs=spec, check_vma=False
    )
```

```python
import jax
import jax.numpy as jnp
from jax import lax
from jax.experimental import pallas as pl
from jax.experimental.pallas import tpu as pltpu
from jax.sharding import PartitionSpec as P

NSUB = 4
RATE = 500.0
AXES = ("gz", "gy")
F32 = jnp.float32
VMEM_BYTES = 12 << 20


def near(*dims):
    return pltpu.VMEM(dims, F32)


def far(*dims):
    return pltpu.HBM(dims, F32)


def call(kernel, name, outs, operands, scratch=(), cycles=0):
    whole, away = pl.BlockSpec(memory_space=pltpu.VMEM), pl.BlockSpec(memory_space=pltpu.HBM)
    inputs, in_specs = [], []
    for operand in operands:
        where, x = operand if isinstance(operand, tuple) else ("near", operand)
        if where != "plain":
            x = pltpu.with_memory_space_constraint(x, pltpu.VMEM if where == "near" else pltpu.HBM)
        inputs.append(x)
        in_specs.append(away if where == "far" else whole)
    out_specs = [away if isinstance(out, tuple) else whole for out in outs]
    result = pl.pallas_call(
        kernel,
        out_shape=[out[1] if isinstance(out, tuple) else out for out in outs],
        in_specs=in_specs,
        out_specs=out_specs,
        scratch_shapes=scratch,
        compiler_params=pltpu.CompilerParams(vmem_limit_bytes=VMEM_BYTES),
        cost_estimate=pl.CostEstimate(flops=0, bytes_accessed=cycles * 1024, transcendentals=0) if cycles else None,
        name=name,
    )(*inputs)
    return result if len(outs) > 1 else result[0]


def place():
    return (
        lax.axis_index("gz"),
        lax.axis_index("gy"),
        lax.axis_size("gz"),
        lax.axis_size("gy"),
    )


def pair_up(index):
    return index ^ 1


def same(index):
    return index


def z_other(index):
    return index + 1 if index % 2 else index - 1


def y_other(index):
    return (index + 1 if index % 2 else index - 1) % lax.axis_size("gy")


def permutation(z_partner, y_partner):
    z_count, y_count = lax.axis_size("gz"), lax.axis_size("gy")
    pairs = []
    for z in range(z_count):
        for y in range(y_count):
            to_z, to_y = z_partner(z), y_partner(y)
            if not 0 <= to_z < z_count:
                to_z, to_y = z, pair_up(y)
            pairs.append((z * y_count + y, to_z * y_count + to_y))
    return pairs


def send(x, z_partner=same, y_partner=same):
    return lax.ppermute(x, AXES, permutation(z_partner, y_partner))


def swap(x, axis, level):
    step = 1 << level
    if axis == "gy":
        step |= 1
    return lax.ppermute(x, axis, [(i, i ^ step) for i in range(lax.axis_size(axis))])


def levels_of(axis):
    return (lax.axis_size(axis) - 1).bit_length()


def z_rims_kernel(tracer, y_speed, z_speed, a_ref, b_ref, sem):
    z, _, _, _ = place()
    depth = tracer.shape[0]
    z_odd = lax.rem(z, 2)
    copies = []
    for ref, low in ((a_ref, z_odd), (b_ref, 1 - z_odd)):
        four, three = (1 - low) * (depth - 4), (1 - low) * (depth - 3)
        for source, start, count, row in ((tracer, four, 4, 0), (z_speed, four, 4, 4), (y_speed, three, 3, 8)):
            copies.append(
                pltpu.make_async_copy(
                    source.at[pl.ds(start, count)], ref.at[pl.ds(row, count)], sem.at[len(copies)]
                )
            )
            copies[-1].start()
    for copy in copies:
        copy.wait()


def z_rims(tracer, y_speed, z_speed):
    _, width, band = tracer.shape
    return call(
        z_rims_kernel,
        "z_rims",
        [near(11, width, band)] * 2,
        [("far", x) for x in (tracer, y_speed, z_speed)],
        scratch=[pltpu.SemaphoreType.DMA((6,))],
        cycles=1000,
    )


def begin_kernel(tracer, y_speed, z_speed, kappa_far, _, o_ref, e_ref, ports, c, ys, zs, kappa, kappa_y, r_y, sem):
    arrivals = [
        pltpu.make_async_copy(source, target, sem.at[k])
        for k, (source, target) in enumerate(((kappa_far, kappa), (tracer, c), (z_speed, zs), (y_speed, ys)))
    ]
    for copy in arrivals:
        copy.start()
    _, y, _, y_count = place()
    width = c.shape[1]
    y_odd = lax.rem(y, 2)
    arrivals[0].wait()
    kappa_y[...] = turned(kappa[...])
    ports[3], ports[4] = resistances(kappa_y, r_y)
    factor(((lambda j: r_y[j], width, *outer(ports, y, y_count), None, ports),))
    for copy in arrivals[1:]:
        copy.wait()

    def rims(o_low):
        for ref, low in ((o_ref, o_low), (e_ref, not o_low)):
            tile = slice(0, 8) if low else slice(width - 8, width)
            four, three = (0, 0) if low else (4, 5)
            ref[0:4] = turned(c[:, tile, :])[four : four + 4]
            ref[4:8] = turned(ys[:, tile, :])[four : four + 4]
            ref[8:11] = turned(zs[:, tile, :])[three : three + 3]

    @pl.when(y_odd == 0)
    def _():
        rims(True)

    @pl.when(y_odd == 1)
    def _():
        rims(False)


def begin(tracer, y_speed, z_speed, kappa, after):
    depth, width, band = tracer.shape
    return call(
        begin_kernel,
        "begin",
        [near(11, depth, band)] * 2 + [near(5, depth, band)],
        [("far", x) for x in (tracer, y_speed, z_speed, kappa)] + [after],
        scratch=[near(depth, width, band)] * 4 + [near(width, depth, band)] * 2 + [pltpu.SemaphoreType.DMA((4,))],
        cycles=2000,
    )


PAD_TILES = 3


def rim_kernel(a, b, _, for_pair, for_other):
    z, y, _, _ = place()
    width = a.shape[1]
    z_odd, y_odd = lax.rem(z, 2) == 1, lax.rem(y, 2)

    def corners(out, low):
        tile, first = (slice(0, 8), 0) if low else (slice(width - 8, width), 5)
        for f, (row, count) in enumerate(((0, 4), (8, 3), (4, 4))):
            empty = [jnp.zeros((3, 4 - count, out.shape[2]), F32)] if count < 4 else []
            side_a, side_b = (turned(ref[row : row + count, tile, :])[first : first + 3] for ref in (a, b))
            below, above = jnp.where(z_odd, side_a, side_b), jnp.where(z_odd, side_b, side_a)
            out[3 * f : 3 * f + 3] = jnp.concatenate([*empty, below, above, *empty], axis=1)

    @pl.when(y_odd == 0)
    def _():
        corners(for_other, True)
        corners(for_pair, False)

    @pl.when(y_odd == 1)
    def _():
        corners(for_other, False)
        corners(for_pair, True)

    for_other[9:] = jnp.zeros((PAD_TILES, 8, for_other.shape[2]), F32)


def rim(a, b, after):
    band = a.shape[2]
    return call(rim_kernel, "rim", [near(9, 8, band), near(9 + PAD_TILES, 8, band)], [a, b, after], cycles=200)


def reciprocal(x):
    r = pl.reciprocal(x, approx=True)
    return r * (2.0 - x * r)


def turned(x):
    return jnp.swapaxes(x, 0, 1)


def resistances(kappa, r):
    count = kappa.shape[0]
    before, following = kappa[0], kappa[1]
    r[0] = jnp.zeros_like(before)
    for j in range(1, count):
        here = following
        if j + 1 < count:
            following = kappa[j + 1]
        r[j] = reciprocal((0.5 * RATE) * (before + here))
        before = here
    return kappa[0], before


def factor(sides):
    state = []
    for read, count, edge_low, edge_high, keep, _ in sides:
        one = jnp.ones_like(edge_low)
        if keep:
            keep[0][0] = one
            keep[1][count - 1] = one
        state.append([one, 1.0 + edge_low, one, 1.0 + edge_high])

    def faces(j):
        return [(read(j), read(count - j)) if j < count else None for read, count, _, _, _, _ in sides]

    longest = max(side[1] for side in sides)
    following = faces(1)
    for j in range(1, longest):
        here, following = following, faces(j + 1)
        for s, pair in zip(state, here):
            if pair is not None:
                s[0] = s[0] + pair[0] * s[1]
                s[1] = s[1] + s[0]
                s[2] = s[2] + pair[1] * s[3]
                s[3] = s[3] + s[2]
        for (_, count, _, _, keep, _), s, pair in zip(sides, state, here):
            if pair is not None and keep:
                keep[0][j] = s[0]
                keep[1][count - 1 - j] = s[2]
    for (_, _, _, edge_high, _, ports), s in zip(sides, state):
        if ports is not None:
            inverse = reciprocal(s[1] + edge_high * s[0])
            ports[0] = s[2] * inverse
            ports[1] = inverse
            ports[2] = s[0] * inverse


def outer(ports, index, count):
    return jnp.where(index == 0, RATE, 0.0) * ports[3], jnp.where(index == count - 1, RATE, 0.0) * ports[4]


def factor_kernel(kappa, r_y_far, r_z_far, ports_z, kappa_y, r_y, r_z, sem):
    z, _, z_count, _ = place()
    depth = kappa.shape[0]
    y_copy = pltpu.make_async_copy(r_y, r_y_far, sem.at[0])
    z_copy = pltpu.make_async_copy(r_z, r_z_far, sem.at[1])
    ports_z[3], ports_z[4] = resistances(kappa, r_z)
    z_copy.start()
    kappa_y[...] = turned(kappa[...])
    resistances(kappa_y, r_y)
    y_copy.start()
    factor(((lambda j: r_z[j], depth, *outer(ports_z, z, z_count), None, ports_z),))
    y_copy.wait()
    z_copy.wait()


def factor_lines(kappa):
    depth, width, band = kappa.shape
    along_y, along_z = (width, depth, band), (depth, width, band)
    return call(
        factor_kernel,
        "factor",
        [("far", far(*along_y)), ("far", far(*along_z)), near(5, width, band)],
        [("plain", kappa)],
        scratch=[near(*along_y), near(*along_y), near(*along_z), pltpu.SemaphoreType.DMA((2,))],
        cycles=4000,
    )


def ports_kernel(axis, level, mine, theirs, joint, out):
    index = lax.axis_index(axis)
    is_left = (lax.shift_right_logical(index, level) & 1) == 0
    pairs = [(mine[k], theirs[k]) for k in range(5)]
    left = [jnp.where(is_left, m, t) for m, t in pairs]
    right = [jnp.where(is_left, t, m) for m, t in pairs]
    d = reciprocal(reciprocal((0.5 * RATE) * (left[4] + right[3])) + left[2] + right[0])
    low, high = left[0] - left[1] * left[1] * d, right[2] - right[1] * right[1] * d
    joint[0] = d
    joint[1] = left[1]
    joint[2] = right[1]
    if level + 2 == levels_of(axis):
        next_left = (lax.shift_right_logical(index, level + 1) & 1) == 0
        out[0] = jnp.where(next_left, high, low)
        out[1] = jnp.where(next_left, right[4], left[3])
    else:
        out[0] = low
        out[1] = left[1] * right[1] * d
        out[2] = high
        out[3] = left[3]
        out[4] = right[4]


def join_ports(mine, theirs, axis, level):
    _, lines, band = mine.shape

    def kernel(*refs):
        ports_kernel(axis, level, *refs)

    last = level + 2 == levels_of(axis)
    outs = [near(3, lines, band), near(2 if last else 5, lines, band)]
    return call(kernel, "join_ports", outs, [mine, theirs], cycles=100)


def join_all(ports, axis):
    joints = []
    for level in range(levels_of(axis) - 1):
        joint, ports = join_ports(ports, swap(ports, axis, level), axis, level)
        joints.append(joint)
    return joints, ports, swap(ports, axis, len(joints))


def source_kernel(axis, level, last, mine, theirs, joint, out, flow_ref):
    index = lax.axis_index(axis)
    is_left = (lax.shift_right_logical(index, level) & 1) == 0
    pairs = [(mine[k], theirs[k]) for k in range(2)]
    left = [jnp.where(is_left, m, t) for m, t in pairs]
    right = [jnp.where(is_left, t, m) for m, t in pairs]
    flow = (left[1] - right[0]) * joint[0]
    flow_ref[0] = flow
    low, high = left[0] - joint[1] * flow, right[1] + joint[2] * flow
    if last:
        next_left = (lax.shift_right_logical(index, level + 1) & 1) == 0
        out[0] = jnp.where(next_left, high, low)
    else:
        out[0] = low
        out[1] = high


def join_sources(mine, theirs, joint, axis, level):
    _, lines, band = mine.shape
    last = level + 2 == levels_of(axis)

    def kernel(*refs):
        source_kernel(axis, level, last, *refs)

    outs = [near(1 if last else 2, lines, band), near(1, lines, band)]
    return call(kernel, "join_sources", outs, [mine, theirs, joint], cycles=100)


def end_currents(axis, mine, theirs, edge, edge_theirs, joints, flows):
    index = lax.axis_index(axis)
    level = len(joints)
    is_left = (lax.shift_right_logical(index, level) & 1) == 0
    d = reciprocal(reciprocal((0.5 * RATE) * (edge[1] + edge_theirs[1])) + edge[0] + edge_theirs[0])
    flow = (mine[0] - theirs[0]) * d
    zero = jnp.zeros_like(flow)
    low, high = jnp.where(is_left, zero, -flow), jnp.where(is_left, -flow, zero)
    for level in range(level - 1, -1, -1):
        joint = joints[level]
        is_left = (lax.shift_right_logical(index, level) & 1) == 0
        flow = flows[level][0] + (joint[1] * low - joint[2] * high) * joint[0]
        low, high = jnp.where(is_left, low, flow), jnp.where(is_left, -flow, high)
    return low, high


def solve_open(values, phi, psi, scale, base, ports):
    count = base.shape[0]
    total = jnp.zeros(base.shape[1:], F32)
    following = (values[0], phi[0], psi[0])
    for j in range(count):
        value, low, high = following
        if j + 1 < count:
            following = (values[j + 1], phi[j + 1], psi[j + 1])
        total = total + low * value
        base[j] = high * total
    ports[1] = scale * total
    total = jnp.zeros(base.shape[1:], F32)
    following = (base[count - 1], values[count - 1], phi[count - 1], psi[count - 1])
    for j in range(count - 1, -1, -1):
        below, value, low, high = following
        if j > 0:
            following = (base[j - 1], values[j - 1], phi[j - 1], psi[j - 1])
        base[j] = scale * (below + low * total)
        total = total + high * value
    ports[0] = scale * total


def advect_kernel(
    tracer, y_speed, z_speed, a, b, o, e, corner, ab, ports_y, r_y_far, r_z_far, ports_z,
    base, sources, r_y, r_z, ports_out, c, ys, zs, sy, sz, phi, psi, kept, sem,
):
    z, y, z_count, y_count = place()
    depth, width, band = tracer.shape
    rows, cols = depth + 8, width + 8
    copies = [
        pltpu.make_async_copy(own, field.at[pl.ds(4, depth), pl.ds(0, width), :], sem.at[k])
        for k, (field, own) in enumerate(((ys, y_speed), (zs, z_speed), (c, tracer)))
    ]
    y_copy = pltpu.make_async_copy(r_y_far, r_y, sem.at[3])
    z_copy = pltpu.make_async_copy(r_z_far, r_z, sem.at[4])
    for copy in copies:
        copy.start()
    y_copy.start()
    z_copy.start()
    ports_out[...] = ports_z[...]
    z_odd, y_odd = lax.rem(z, 2), lax.rem(y, 2)
    keep_b = jnp.where((z_odd == 0) & (z == 0) | (z_odd == 1) & (z == z_count - 1), 0.0, 1.0)
    keep_o = jnp.where((y_odd == 0) & (y == 0) | (y_odd == 1) & (y == y_count - 1), 0.0, 1.0)
    keep_below = jnp.where(z_odd == 0, keep_b, 1.0)
    keep_above = jnp.where(z_odd == 1, keep_b, 1.0)
    column = lax.broadcasted_iota(jnp.int32, (8, band), 0)
    outside = (column < 4) & (y == y_count - 1) | (column >= 4) & (y == 0)
    inside = jnp.where(outside, 0.0, 1.0)

    for field in (c, ys, zs):
        field[0:4, width:cols, :] = jnp.zeros((4, 8, band), F32)
        field[4 + depth : rows, width:cols, :] = jnp.zeros((4, 8, band), F32)
    ys[0:1, 0:width, :] = jnp.zeros((1, width, band), F32)
    ys[rows - 1 : rows, 0:width, :] = jnp.zeros((1, width, band), F32)
    for ref, low, keep in ((a, z_odd, None), (b, 1 - z_odd, keep_b)):
        scale = (lambda v: v) if keep is None else (lambda v: v * keep)
        four = jnp.where(low == 1, 0, depth + 4)
        three = jnp.where(low == 1, 1, depth + 4)
        c[pl.ds(four, 4), 0:width, :] = scale(ref[0:4])
        zs[pl.ds(four, 4), 0:width, :] = scale(ref[4:8])
        ys[pl.ds(three, 3), 0:width, :] = scale(ref[8:11])

    def sides(o_low):
        def columns(first, count):
            other, pair = o[first : first + count] * keep_o, e[first : first + count]
            above, below = (pair, other) if o_low else (other, pair)
            empty = [jnp.zeros((4 - count, depth, band), F32)] if count < 4 else []
            return turned(jnp.concatenate([above, *empty, *empty, below], axis=0))

        c[4 : 4 + depth, width:cols, :] = columns(0, 4)
        ys[4 : 4 + depth, width:cols, :] = columns(4, 4)
        zs[4 : 4 + depth, width:cols, :] = columns(8, 3)

        def corners(ref, low, keep):
            start = width + (5 if low else 0)
            for f, (field, count) in enumerate(((c, 4), (ys, 3), (zs, 4))):
                for k in range(3):
                    below, above = ref[3 * f + k, 4 - count : 4, :], ref[3 * f + k, 4 : 4 + count, :]
                    field[4 - count : 4, start + k, :] = below * (keep * keep_below)
                    field[depth + 4 : depth + 4 + count, start + k, :] = above * (keep * keep_above)

        corners(corner, o_low, keep_o)
        corners(ab, not o_low, 1.0)

    @pl.when(y_odd == 0)
    def _():
        sides(True)

    @pl.when(y_odd == 1)
    def _():
        sides(False)

    for copy in copies[:2]:
        copy.wait()

    def up(v):
        return pltpu.roll(v, cols - 1, 0)

    def down(v):
        return pltpu.roll(v, 1, 0)

    def flux(speed, here, after):
        return speed * jnp.where(speed > 0.0, here, after)

    def faces(r, before):
        v = ys[r]
        sy[r] = 0.5 * (v + up(v))
        after = zs[r + 1]
        sz[r] = 0.5 * (before + after)
        return after

    lax.fori_loop(0, rows - 1, faces, zs[0], unroll=13)
    copies[2].wait()

    keep_low = jnp.where(z == 0, 0.0, 1.0)
    keep_high = jnp.where(z == z_count - 1, 0.0, 1.0)
    for step in range(1, NSUB + 1):
        here = c[step]

        def row(r, carry):
            here, below = carry
            after = c[r + 1]
            above = flux(sz[r], here, after)
            across = flux(sy[r], here, up(here))
            new = here - (across - down(across)) - (above - below)
            c[r, 0:width, :] = new[0:width]
            c[r, width:cols, :] = new[width:cols] * inside
            return after, above

        lax.fori_loop(step, rows - step, row, (here, flux(sz[step - 1], c[step - 1], here)), unroll=16)
        if step < NSUB:
            c[3] = c[3] * keep_low
            c[4 + depth] = c[4 + depth] * keep_high

    z_copy.wait()
    y_copy.wait()
    factor(((lambda j: r_y[j], width, *outer(ports_y, y, y_count), (phi, psi), None),))
    kept[...] = turned(c[4 : 4 + depth, 0:width, :])
    solve_open(kept, phi, psi, ports_y[1], base, sources)


def advect(tracer, y_speed, z_speed, halos, ports_y, r_y, r_z, ports_z):
    depth, width, band = tracer.shape
    padded = near(depth + 8, width + 8, band)
    along_y, along_z = near(width, depth, band), near(depth, width, band)
    return call(
        advect_kernel,
        "advect",
        [along_y, near(2, depth, band), along_y, along_z, near(5, width, band)],
        [("far", x) for x in (tracer, y_speed, z_speed)]
        + list(halos)
        + [ports_y, ("far", r_y), ("far", r_z), ports_z],
        scratch=[padded] * 5 + [along_y] * 3 + [pltpu.SemaphoreType.DMA((5,))],
        cycles=5000,
    )


def turn_kernel(levels, *refs):
    last, refs = refs[0:4], refs[4:]
    joints, flows = refs[0:levels], refs[levels : 2 * levels]
    ports_y, base_y, r_y, ports_z, r_z, _, base, sources, phi, psi, u, kept = refs[2 * levels :]
    z, y, z_count, y_count = place()
    width, depth = base_y.shape[0], base.shape[0]
    low, high = end_currents("gy", *last, joints, flows)
    edge, _ = outer(ports_y, y, y_count)
    value = low * ports_y[0] + high * ports_y[1]
    current = (1.0 + edge) * value - low
    u[0] = base_y[0] + value
    following = (r_y[1], base_y[1])
    for j in range(1, width):
        (r, own), following = following, (r_y[j + 1], base_y[j + 1]) if j + 1 < width else None
        value = value + r * current
        current = current + value
        u[j] = own + value
    factor(((lambda k: r_z[k], depth, *outer(ports_z, z, z_count), (phi, psi), None),))
    kept[...] = turned(u[...])
    solve_open(kept, phi, psi, ports_z[1], base, sources)


def turn(last, joints, flows, ports_y, base_y, r_y, ports_z, r_z, after):
    width, depth, band = base_y.shape
    along_z = near(depth, width, band)

    def kernel(*refs):
        turn_kernel(len(joints), *refs)

    return call(
        kernel,
        "turn",
        [along_z, near(2, width, band), along_z, along_z],
        [*last, *joints, *flows, ports_y, base_y, r_y, ports_z, r_z, after],
        scratch=[near(width, depth, band), along_z],
        cycles=1500,
    )


def finish_kernel(levels, *refs):
    last, refs = refs[0:4], refs[4:]
    joints, flows = refs[0:levels], refs[levels : 2 * levels]
    ports_z, base, phi, psi, out, u, sem = refs[2 * levels :]
    low, high = end_currents("gz", *last, joints, flows)
    scale = ports_z[1]
    low, high = low * scale, high * scale
    depth = base.shape[0]
    part = depth // 4
    copies = []
    for p in range(4):
        for k in range(p * part, (p + 1) * part):
            u[k] = base[k] + low * psi[k] + high * phi[k]
        block = pl.ds(p * part, part)
        copies.append(pltpu.make_async_copy(u.at[block], out.at[block], sem.at[p]))
        copies[-1].start()
    for copy in copies:
        copy.wait()


def finish(last, joints, flows, ports_z, base, phi, psi):
    def kernel(*refs):
        finish_kernel(len(joints), *refs)

    return call(
        kernel,
        "finish",
        [("far", jax.ShapeDtypeStruct(base.shape, F32))],
        [*last, *joints, *flows, ports_z, base, phi, psi],
        scratch=[near(*base.shape), pltpu.SemaphoreType.DMA((4,))],
        cycles=1000,
    )


def exchange_sources(sources, joints, axis):
    flows = []
    for level, joint in enumerate(joints):
        sources, flow = join_sources(sources, swap(sources, axis, level), joint, axis, level)
        flows.append(flow)
    return sources, swap(sources, axis, len(joints)), flows


def local(tracer, y_speed, z_speed, kappa):
    a, b = z_rims(tracer, y_speed, z_speed)
    o, e, ports_y = begin(tracer, y_speed, z_speed, kappa, a)
    a = send(a, z_partner=pair_up)
    b = send(b, z_partner=z_other)
    e = swap(e, "gy", 0)
    o = send(o, y_partner=y_other)
    r_y, r_z, ports_z = factor_lines(kappa)
    for_pair, for_other = rim(a, b, ports_z)
    corner = send(for_other, y_partner=y_other)
    ab = swap(for_pair, "gy", 0)
    joints_y, edge_y, edge_y_theirs = join_all(ports_y, "gy")

    base, sources, r_y, r_z, ports_z = advect(
        tracer, y_speed, z_speed, (a, b, o, e, corner, ab), ports_y, r_y, r_z, ports_z
    )
    joints_z, edge_z, edge_z_theirs = join_all(ports_z, "gz")
    mine, theirs, flows = exchange_sources(sources, joints_y, "gy")
    base, sources, phi_z, psi_z = turn(
        (mine, theirs, edge_y, edge_y_theirs), joints_y, flows, ports_y, base, r_y, ports_z, r_z, joints_z[-1]
    )
    mine, theirs, flows = exchange_sources(sources, joints_z, "gz")
    return finish((mine, theirs, edge_z, edge_z_theirs), joints_z, flows, ports_z, base, phi_z, psi_z)


def solution(mesh):
    spec = P("gz", "gy", None)
    return jax.shard_map(
        local, mesh=mesh, in_specs=(spec,) * 4, out_specs=spec, check_vma=False
    )
```

```python
import jax
import jax.numpy as jnp
from jax import lax
from jax.experimental import pallas as pl
from jax.experimental.pallas import tpu as pltpu
from jax.sharding import PartitionSpec as P

NSUB = 4
RATE = 500.0
AXES = ("gz", "gy")
F32 = jnp.float32
VMEM_BYTES = 12 << 20


def near(*dims):
    return pltpu.VMEM(dims, F32)


def far(*dims):
    return pltpu.HBM(dims, F32)


def call(kernel, name, outs, operands, scratch=(), cycles=0):
    whole, away = pl.BlockSpec(memory_space=pltpu.VMEM), pl.BlockSpec(memory_space=pltpu.HBM)
    inputs, in_specs = [], []
    for operand in operands:
        where, x = operand if isinstance(operand, tuple) else ("near", operand)
        if where != "plain":
            x = pltpu.with_memory_space_constraint(x, pltpu.VMEM if where == "near" else pltpu.HBM)
        inputs.append(x)
        in_specs.append(away if where == "far" else whole)
    out_specs = [away if isinstance(out, tuple) else whole for out in outs]
    result = pl.pallas_call(
        kernel,
        out_shape=[out[1] if isinstance(out, tuple) else out for out in outs],
        in_specs=in_specs,
        out_specs=out_specs,
        scratch_shapes=scratch,
        compiler_params=pltpu.CompilerParams(vmem_limit_bytes=VMEM_BYTES),
        cost_estimate=pl.CostEstimate(flops=0, bytes_accessed=cycles * 1024, transcendentals=0) if cycles else None,
        name=name,
    )(*inputs)
    return result if len(outs) > 1 else result[0]


def place():
    return (
        lax.axis_index("gz"),
        lax.axis_index("gy"),
        lax.axis_size("gz"),
        lax.axis_size("gy"),
    )


def pair_up(index):
    return index ^ 1


def same(index):
    return index


def z_other(index):
    return index + 1 if index % 2 else index - 1


def y_other(index):
    return index + 1 if index % 2 else index - 1


def y_ring(index):
    return y_other(index) % lax.axis_size("gy")


def permutation(z_partner, y_partner):
    z_count, y_count = lax.axis_size("gz"), lax.axis_size("gy")
    pairs = []
    for z in range(z_count):
        for y in range(y_count):
            to_z, to_y = z_partner(z), y_partner(y)
            if not 0 <= to_z < z_count:
                to_z, to_y = z, pair_up(y)
            elif not 0 <= to_y < y_count:
                to_z, to_y = pair_up(z), y
            pairs.append((z * y_count + y, to_z * y_count + to_y))
    return pairs


def send(x, z_partner=same, y_partner=same):
    return lax.ppermute(x, AXES, permutation(z_partner, y_partner))


def swap(x, axis, level):
    step = 1 << level
    if axis == "gy":
        step |= 1
    return lax.ppermute(x, axis, [(i, i ^ step) for i in range(lax.axis_size(axis))])


def levels_of(axis):
    return (lax.axis_size(axis) - 1).bit_length()


def flux(speed, lower, upper):
    return speed * jnp.where(speed > 0.0, lower, upper)


def z_rims_kernel(tracer, y_speed, z_speed, b_ref, a_ref, outer_rows, sem):
    z, _, _, _ = place()
    depth = tracer.shape[0]
    z_odd = lax.rem(z, 2)
    sides = ((b_ref, 1 - z_odd), (a_ref, z_odd))
    copies = []

    def start(source, target):
        copies.append(pltpu.make_async_copy(source, target, sem.at[len(copies)]))
        copies[-1].start()

    for side, (ref, low) in enumerate(sides):
        near_rows, fourth = (1 - low) * (depth - 3), jnp.where(low == 1, 3, depth - 4)
        for k, field in enumerate((tracer, z_speed)):
            start(field.at[pl.ds(fourth, 1)], outer_rows.at[side, pl.ds(k, 1)])
        for k, field in enumerate((tracer, z_speed, y_speed)):
            start(field.at[pl.ds(near_rows, 3)], ref.at[pl.ds(3 * k, 3)])
    for copy in copies:
        copy.wait()
    for side, (ref, low) in enumerate(sides):
        third, fourth = ref[2 * low], outer_rows[side, 0]
        speed = 0.5 * (ref[3 + 2 * low] + outer_rows[side, 1])
        ref[9] = flux(speed, jnp.where(low == 1, third, fourth), jnp.where(low == 1, fourth, third))


def z_rims(tracer, y_speed, z_speed):
    _, width, band = tracer.shape
    return call(
        z_rims_kernel,
        "z_rims",
        [near(10, width, band)] * 2,
        [("far", x) for x in (tracer, y_speed, z_speed)],
        scratch=[near(2, 2, width, band), pltpu.SemaphoreType.DMA((10,))],
        cycles=1000,
    )


def begin_kernel(tracer, y_speed, z_speed, kappa_far, _, o_ref, e_ref, ports, c, ys, zs, kappa, kappa_y, r_y, sem):
    arrivals = [
        pltpu.make_async_copy(source, target, sem.at[k])
        for k, (source, target) in enumerate(((kappa_far, kappa), (tracer, c), (z_speed, zs), (y_speed, ys)))
    ]
    for copy in arrivals:
        copy.start()
    _, y, _, y_count = place()
    width = c.shape[1]
    y_odd = lax.rem(y, 2)
    arrivals[0].wait()
    kappa_y[...] = turned(kappa[...])
    ports[3], ports[4] = resistances(kappa_y, r_y)
    factor(((lambda j: r_y[j], width, *outer(ports, y, y_count), None, ports),))
    for copy in arrivals[1:]:
        copy.wait()

    def rims(o_low):
        for ref, low in ((o_ref, o_low), (e_ref, not o_low)):
            tile = slice(0, 8) if low else slice(width - 8, width)
            tc, ty, tz = (turned(f[:, tile, :]) for f in (c, ys, zs))
            three = 0 if low else 5
            lower, upper = (2, 3) if low else (4, 5)
            ref[0:3] = tc[three : three + 3]
            ref[3:6] = ty[three : three + 3]
            ref[6:9] = tz[three : three + 3]
            ref[9] = flux(0.5 * (ty[lower] + ty[upper]), tc[lower], tc[upper])

    @pl.when(y_odd == 0)
    def _():
        rims(True)

    @pl.when(y_odd == 1)
    def _():
        rims(False)


def begin(tracer, y_speed, z_speed, kappa, after):
    depth, width, band = tracer.shape
    return call(
        begin_kernel,
        "begin",
        [near(10, depth, band)] * 2 + [near(5, depth, band)],
        [("far", x) for x in (tracer, y_speed, z_speed, kappa)] + [after],
        scratch=[near(depth, width, band)] * 4 + [near(width, depth, band)] * 2 + [pltpu.SemaphoreType.DMA((4,))],
        cycles=2000,
    )


PAD_TILES = 3


def rim_kernel(b, a, _, for_pair, for_other):
    z, y, _, _ = place()
    width = a.shape[1]
    z_odd, y_odd = lax.rem(z, 2) == 1, lax.rem(y, 2)

    def corners(out, low):
        tile, first = (slice(0, 8), 0) if low else (slice(width - 8, width), 5)
        empty = jnp.zeros((3, 1, out.shape[2]), F32)
        for f, row in enumerate((0, 6, 3)):
            side_a, side_b = (turned(ref[row : row + 3, tile, :])[first : first + 3] for ref in (a, b))
            below, above = jnp.where(z_odd, side_a, side_b), jnp.where(z_odd, side_b, side_a)
            out[3 * f : 3 * f + 3] = jnp.concatenate([empty, below, above, empty], axis=1)

    @pl.when(y_odd == 0)
    def _():
        corners(for_other, True)
        corners(for_pair, False)

    @pl.when(y_odd == 1)
    def _():
        corners(for_other, False)
        corners(for_pair, True)

    for_other[9:] = jnp.zeros((PAD_TILES, 8, for_other.shape[2]), F32)


def rim(a, b, after):
    band = a.shape[2]
    return call(rim_kernel, "rim", [near(9, 8, band), near(9 + PAD_TILES, 8, band)], [b, a, after], cycles=200)


def reciprocal(x):
    r = pl.reciprocal(x, approx=True)
    return r * (2.0 - x * r)


def turned(x):
    return jnp.swapaxes(x, 0, 1)


def resistances(kappa, r):
    count = kappa.shape[0]
    before, following = kappa[0], kappa[1]
    r[0] = jnp.zeros_like(before)
    for j in range(1, count):
        here = following
        if j + 1 < count:
            following = kappa[j + 1]
        r[j] = reciprocal((0.5 * RATE) * (before + here))
        before = here
    return kappa[0], before


def factor(sides):
    state = []
    for read, count, edge_low, edge_high, keep, _ in sides:
        one = jnp.ones_like(edge_low)
        if keep:
            keep[0][0] = one
            keep[1][count - 1] = one
        state.append([one, 1.0 + edge_low, one, 1.0 + edge_high])

    def faces(j):
        return [(read(j), read(count - j)) if j < count else None for read, count, _, _, _, _ in sides]

    longest = max(side[1] for side in sides)
    following = faces(1)
    for j in range(1, longest):
        here, following = following, faces(j + 1)
        for s, pair in zip(state, here):
            if pair is not None:
                s[0] = s[0] + pair[0] * s[1]
                s[1] = s[1] + s[0]
                s[2] = s[2] + pair[1] * s[3]
                s[3] = s[3] + s[2]
        for (_, count, _, _, keep, _), s, pair in zip(sides, state, here):
            if pair is not None and keep:
                keep[0][j] = s[0]
                keep[1][count - 1 - j] = s[2]
    for (_, _, _, edge_high, _, ports), s in zip(sides, state):
        if ports is not None:
            inverse = reciprocal(s[1] + edge_high * s[0])
            ports[0] = s[2] * inverse
            ports[1] = inverse
            ports[2] = s[0] * inverse


def outer(ports, index, count):
    return jnp.where(index == 0, RATE, 0.0) * ports[3], jnp.where(index == count - 1, RATE, 0.0) * ports[4]


def factor_kernel(kappa, r_y_far, r_z_far, ports_z, kappa_y, r_y, r_z, sem):
    z, _, z_count, _ = place()
    depth = kappa.shape[0]
    y_copy = pltpu.make_async_copy(r_y, r_y_far, sem.at[0])
    z_copy = pltpu.make_async_copy(r_z, r_z_far, sem.at[1])
    ports_z[3], ports_z[4] = resistances(kappa, r_z)
    z_copy.start()
    kappa_y[...] = turned(kappa[...])
    resistances(kappa_y, r_y)
    y_copy.start()
    factor(((lambda j: r_z[j], depth, *outer(ports_z, z, z_count), None, ports_z),))
    y_copy.wait()
    z_copy.wait()


def factor_lines(kappa):
    depth, width, band = kappa.shape
    along_y, along_z = (width, depth, band), (depth, width, band)
    return call(
        factor_kernel,
        "factor",
        [("far", far(*along_y)), ("far", far(*along_z)), near(5, width, band)],
        [("plain", kappa)],
        scratch=[near(*along_y), near(*along_y), near(*along_z), pltpu.SemaphoreType.DMA((2,))],
        cycles=4000,
    )


def ports_kernel(axis, level, mine, theirs, joint, out):
    index = lax.axis_index(axis)
    is_left = (lax.shift_right_logical(index, level) & 1) == 0
    pairs = [(mine[k], theirs[k]) for k in range(5)]
    left = [jnp.where(is_left, m, t) for m, t in pairs]
    right = [jnp.where(is_left, t, m) for m, t in pairs]
    d = reciprocal(reciprocal((0.5 * RATE) * (left[4] + right[3])) + left[2] + right[0])
    low, high = left[0] - left[1] * left[1] * d, right[2] - right[1] * right[1] * d
    joint[0] = d
    joint[1] = left[1]
    joint[2] = right[1]
    if level + 2 == levels_of(axis):
        next_left = (lax.shift_right_logical(index, level + 1) & 1) == 0
        out[0] = jnp.where(next_left, high, low)
        out[1] = jnp.where(next_left, right[4], left[3])
    else:
        out[0] = low
        out[1] = left[1] * right[1] * d
        out[2] = high
        out[3] = left[3]
        out[4] = right[4]


def join_ports(mine, theirs, axis, level):
    _, lines, band = mine.shape

    def kernel(*refs):
        ports_kernel(axis, level, *refs)

    last = level + 2 == levels_of(axis)
    outs = [near(3, lines, band), near(2 if last else 5, lines, band)]
    return call(kernel, "join_ports", outs, [mine, theirs], cycles=100)


def join_all(ports, axis):
    joints = []
    for level in range(levels_of(axis) - 1):
        joint, ports = join_ports(ports, swap(ports, axis, level), axis, level)
        joints.append(joint)
    return joints, ports, swap(ports, axis, len(joints))


def source_kernel(axis, level, last, mine, theirs, joint, out, flow_ref):
    index = lax.axis_index(axis)
    is_left = (lax.shift_right_logical(index, level) & 1) == 0
    pairs = [(mine[k], theirs[k]) for k in range(2)]
    left = [jnp.where(is_left, m, t) for m, t in pairs]
    right = [jnp.where(is_left, t, m) for m, t in pairs]
    flow = (left[1] - right[0]) * joint[0]
    flow_ref[0] = flow
    low, high = left[0] - joint[1] * flow, right[1] + joint[2] * flow
    if last:
        next_left = (lax.shift_right_logical(index, level + 1) & 1) == 0
        out[0] = jnp.where(next_left, high, low)
    else:
        out[0] = low
        out[1] = high


def join_sources(mine, theirs, joint, axis, level):
    _, lines, band = mine.shape
    last = level + 2 == levels_of(axis)

    def kernel(*refs):
        source_kernel(axis, level, last, *refs)

    outs = [near(1 if last else 2, lines, band), near(1, lines, band)]
    return call(kernel, "join_sources", outs, [mine, theirs, joint], cycles=100)


def end_currents(axis, mine, theirs, edge, edge_theirs, joints, flows):
    index = lax.axis_index(axis)
    level = len(joints)
    is_left = (lax.shift_right_logical(index, level) & 1) == 0
    d = reciprocal(reciprocal((0.5 * RATE) * (edge[1] + edge_theirs[1])) + edge[0] + edge_theirs[0])
    flow = (mine[0] - theirs[0]) * d
    zero = jnp.zeros_like(flow)
    low, high = jnp.where(is_left, zero, -flow), jnp.where(is_left, -flow, zero)
    for level in range(level - 1, -1, -1):
        joint = joints[level]
        is_left = (lax.shift_right_logical(index, level) & 1) == 0
        flow = flows[level][0] + (joint[1] * low - joint[2] * high) * joint[0]
        low, high = jnp.where(is_left, low, flow), jnp.where(is_left, -flow, high)
    return low, high


def solve_open(values, phi, psi, scale, base, ports):
    count = base.shape[0]
    total = jnp.zeros(base.shape[1:], F32)
    following = (values[0], phi[0], psi[0])
    for j in range(count):
        value, low, high = following
        if j + 1 < count:
            following = (values[j + 1], phi[j + 1], psi[j + 1])
        total = total + low * value
        base[j] = high * total
    ports[1] = scale * total
    total = jnp.zeros(base.shape[1:], F32)
    following = (base[count - 1], values[count - 1], phi[count - 1], psi[count - 1])
    for j in range(count - 1, -1, -1):
        below, value, low, high = following
        if j > 0:
            following = (base[j - 1], values[j - 1], phi[j - 1], psi[j - 1])
        base[j] = scale * (below + low * total)
        total = total + high * value
    ports[0] = scale * total


def advect_kernel(
    tracer, y_speed, z_speed, b, a, o, e, corner, ab, ports_y, r_y_far, r_z_far, ports_z,
    base, sources, r_y, r_z, ports_out, c, ys, zs, sy, sz, phi, psi, kept, flux_z, flux_y, sem,
):
    z, y, z_count, y_count = place()
    depth, width, band = tracer.shape
    rows, cols = depth + 8, width + 8
    copies = [
        pltpu.make_async_copy(own, field.at[pl.ds(4, depth), pl.ds(0, width), :], sem.at[k])
        for k, (field, own) in enumerate(((ys, y_speed), (zs, z_speed), (c, tracer)))
    ]
    y_copy = pltpu.make_async_copy(r_y_far, r_y, sem.at[3])
    z_copy = pltpu.make_async_copy(r_z_far, r_z, sem.at[4])
    for copy in copies:
        copy.start()
    y_copy.start()
    z_copy.start()
    ports_out[...] = ports_z[...]
    z_odd, y_odd = lax.rem(z, 2), lax.rem(y, 2)
    keep_b = jnp.where((z_odd == 0) & (z == 0) | (z_odd == 1) & (z == z_count - 1), 0.0, 1.0)
    keep_o = jnp.where((y_odd == 0) & (y == 0) | (y_odd == 1) & (y == y_count - 1), 0.0, 1.0)
    keep_below = jnp.where(z_odd == 0, keep_b, 1.0)
    keep_above = jnp.where(z_odd == 1, keep_b, 1.0)
    column = lax.broadcasted_iota(jnp.int32, (8, band), 0)
    outside = (column < 4) & (y == y_count - 1) | (column >= 4) & (y == 0)
    inside = jnp.where(outside, 0.0, 1.0)

    for field in (c, ys, zs):
        field[0:4, width:cols, :] = jnp.zeros((4, 8, band), F32)
        field[4 + depth : rows, width:cols, :] = jnp.zeros((4, 8, band), F32)
    flux_z[:, width:cols, :] = jnp.zeros((2, 8, band), F32)
    for ref, low, keep in ((a, z_odd, 1.0), (b, 1 - z_odd, keep_b)):
        three = jnp.where(low == 1, 1, depth + 4)
        for k, field in enumerate((c, zs, ys)):
            field[pl.ds(three, 3), 0:width, :] = ref[3 * k : 3 * k + 3] * keep
        flux_z[1 - low, 0:width, :] = ref[9] * keep

    def sides(o_low):
        other, pair = (o, keep_o), (e, 1.0)
        (above, keep_up), (below, keep_down) = (pair, other) if o_low else (other, pair)
        empty = jnp.zeros((2, depth, band), F32)
        for k, field in enumerate((c, ys, zs)):
            three = slice(3 * k, 3 * k + 3)
            tile = jnp.concatenate([above[three] * keep_up, empty, below[three] * keep_down], axis=0)
            field[4 : 4 + depth, width:cols, :] = turned(tile)
        faces = [empty, above[9:10] * keep_up, empty[:1], below[9:10] * keep_down, empty, empty[:1]]
        flux_y[...] = turned(jnp.concatenate(faces, axis=0))

        def corners(ref, low, keep):
            start = width + (5 if low else 0)
            for f, field in enumerate((c, ys, zs)):
                for k in range(3):
                    field[1:4, start + k, :] = ref[3 * f + k, 1:4, :] * (keep * keep_below)
                    field[depth + 4 : depth + 7, start + k, :] = ref[3 * f + k, 4:7, :] * (keep * keep_above)

        corners(corner, o_low, keep_o)
        corners(ab, not o_low, 1.0)

    @pl.when(y_odd == 0)
    def _():
        sides(True)

    @pl.when(y_odd == 1)
    def _():
        sides(False)

    for copy in copies[:2]:
        copy.wait()

    def up(v):
        return pltpu.roll(v, cols - 1, 0)

    def down(v):
        return pltpu.roll(v, 1, 0)

    def faces(r, before):
        v = ys[r]
        sy[r] = 0.5 * (v + up(v))
        after = zs[r + 1]
        sz[r] = 0.5 * (before + after)
        return after

    lax.fori_loop(0, rows - 1, faces, zs[0], unroll=13)
    copies[2].wait()

    keep_low = jnp.where(z == 0, 0.0, 1.0)
    keep_high = jnp.where(z == z_count - 1, 0.0, 1.0)
    given = (column == 2) | (column == 4)
    for step in range(1, NSUB + 1):

        def row(r, carry, side=False, top=None):
            here, below = carry
            after = c[r + 1]
            above = flux(sz[r], here, after) if top is None else top
            across = flux(sy[r], here, up(here))
            if side:
                edge = jnp.where(given, flux_y[r - 4], across[width:cols])
                across = jnp.concatenate([across[0:width], edge], axis=0)
            new = here - (across - down(across)) - (above - below)
            c[r, 0:width, :] = new[0:width]
            c[r, width:cols, :] = new[width:cols] * inside
            return after, above

        if step == 1:
            carry = c[1], flux_z[0]
            for r in range(1, 4):
                carry = row(r, carry)
            side_row = lambda r, carry: row(r, carry, side=True)
            carry = lax.fori_loop(4, 4 + depth, side_row, carry, unroll=16)
            for r in range(4 + depth, rows - 2):
                carry = row(r, carry)
            row(rows - 2, carry, top=flux_z[1])
        else:
            below = flux(sz[step - 1], c[step - 1], c[step])
            lax.fori_loop(step, rows - step, row, (c[step], below), unroll=16)
        if step < NSUB:
            c[3] = c[3] * keep_low
            c[4 + depth] = c[4 + depth] * keep_high

    z_copy.wait()
    y_copy.wait()
    factor(((lambda j: r_y[j], width, *outer(ports_y, y, y_count), (phi, psi), None),))
    kept[...] = turned(c[4 : 4 + depth, 0:width, :])
    solve_open(kept, phi, psi, ports_y[1], base, sources)


def advect(tracer, y_speed, z_speed, halos, ports_y, r_y, r_z, ports_z):
    depth, width, band = tracer.shape
    padded = near(depth + 8, width + 8, band)
    along_y, along_z = near(width, depth, band), near(depth, width, band)
    return call(
        advect_kernel,
        "advect",
        [along_y, near(2, depth, band), along_y, along_z, near(5, width, band)],
        [("far", x) for x in (tracer, y_speed, z_speed)]
        + list(halos)
        + [ports_y, ("far", r_y), ("far", r_z), ports_z],
        scratch=[padded] * 5 + [along_y] * 3
        + [near(2, width + 8, band), near(depth, 8, band), pltpu.SemaphoreType.DMA((5,))],
        cycles=5000,
    )


def turn_kernel(levels, *refs):
    last, refs = refs[0:4], refs[4:]
    joints, flows = refs[0:levels], refs[levels : 2 * levels]
    ports_y, base_y, r_y, ports_z, r_z, _, base, sources, phi, psi, u, kept = refs[2 * levels :]
    z, y, z_count, y_count = place()
    width, depth = base_y.shape[0], base.shape[0]
    low, high = end_currents("gy", *last, joints, flows)
    edge, _ = outer(ports_y, y, y_count)
    value = low * ports_y[0] + high * ports_y[1]
    current = (1.0 + edge) * value - low
    u[0] = base_y[0] + value
    following = (r_y[1], base_y[1])
    for j in range(1, width):
        (r, own), following = following, (r_y[j + 1], base_y[j + 1]) if j + 1 < width else None
        value = value + r * current
        current = current + value
        u[j] = own + value
    factor(((lambda k: r_z[k], depth, *outer(ports_z, z, z_count), (phi, psi), None),))
    kept[...] = turned(u[...])
    solve_open(kept, phi, psi, ports_z[1], base, sources)


def turn(last, joints, flows, ports_y, base_y, r_y, ports_z, r_z, after):
    width, depth, band = base_y.shape
    along_z = near(depth, width, band)

    def kernel(*refs):
        turn_kernel(len(joints), *refs)

    return call(
        kernel,
        "turn",
        [along_z, near(2, width, band), along_z, along_z],
        [*last, *joints, *flows, ports_y, base_y, r_y, ports_z, r_z, after],
        scratch=[near(width, depth, band), along_z],
        cycles=1500,
    )


def finish_kernel(levels, *refs):
    last, refs = refs[0:4], refs[4:]
    joints, flows = refs[0:levels], refs[levels : 2 * levels]
    ports_z, base, phi, psi, out, u, sem = refs[2 * levels :]
    low, high = end_currents("gz", *last, joints, flows)
    scale = ports_z[1]
    low, high = low * scale, high * scale
    depth = base.shape[0]
    part = depth // 4
    copies = []
    for p in range(4):
        for k in range(p * part, (p + 1) * part):
            u[k] = base[k] + low * psi[k] + high * phi[k]
        block = pl.ds(p * part, part)
        copies.append(pltpu.make_async_copy(u.at[block], out.at[block], sem.at[p]))
        copies[-1].start()
    for copy in copies:
        copy.wait()


def finish(last, joints, flows, ports_z, base, phi, psi):
    def kernel(*refs):
        finish_kernel(len(joints), *refs)

    return call(
        kernel,
        "finish",
        [("far", jax.ShapeDtypeStruct(base.shape, F32))],
        [*last, *joints, *flows, ports_z, base, phi, psi],
        scratch=[near(*base.shape), pltpu.SemaphoreType.DMA((4,))],
        cycles=1000,
    )


def exchange_sources(sources, joints, axis):
    flows = []
    for level, joint in enumerate(joints):
        sources, flow = join_sources(sources, swap(sources, axis, level), joint, axis, level)
        flows.append(flow)
    return sources, swap(sources, axis, len(joints)), flows


def local(tracer, y_speed, z_speed, kappa):
    b, a = z_rims(tracer, y_speed, z_speed)
    o, e, ports_y = begin(tracer, y_speed, z_speed, kappa, b)
    b = send(b, z_partner=z_other)
    a = send(a, z_partner=pair_up)
    e = swap(e, "gy", 0)
    o = send(o, y_partner=y_ring)
    r_y, r_z, ports_z = factor_lines(kappa)
    for_pair, for_other = rim(a, b, ports_z)
    corner = send(for_other, y_partner=y_other)
    ab = swap(for_pair, "gy", 0)
    joints_y, edge_y, edge_y_theirs = join_all(ports_y, "gy")

    base, sources, r_y, r_z, ports_z = advect(
        tracer, y_speed, z_speed, (b, a, o, e, corner, ab), ports_y, r_y, r_z, ports_z
    )
    joints_z, edge_z, edge_z_theirs = join_all(ports_z, "gz")
    mine, theirs, flows = exchange_sources(sources, joints_y, "gy")
    base, sources, phi_z, psi_z = turn(
        (mine, theirs, edge_y, edge_y_theirs), joints_y, flows, ports_y, base, r_y, ports_z, r_z, joints_z[-1]
    )
    mine, theirs, flows = exchange_sources(sources, joints_z, "gz")
    return finish((mine, theirs, edge_z, edge_z_theirs), joints_z, flows, ports_z, base, phi_z, psi_z)


def solution(mesh):
    spec = P("gz", "gy", None)
    return jax.shard_map(
        local, mesh=mesh, in_specs=(spec,) * 4, out_specs=spec, check_vma=False
    )
```

```python
import jax
import jax.numpy as jnp
from jax import lax
from jax.experimental import pallas as pl
from jax.experimental.pallas import tpu as pltpu
from jax.sharding import PartitionSpec as P

NSUB = 4
RATE = 500.0
AXES = ("gz", "gy")
F32 = jnp.float32
VMEM_BYTES = 12 << 20


def near(*dims):
    return pltpu.VMEM(dims, F32)


def far(*dims):
    return pltpu.HBM(dims, F32)


def call(kernel, name, outs, operands, scratch=(), cycles=0):
    whole, away = pl.BlockSpec(memory_space=pltpu.VMEM), pl.BlockSpec(memory_space=pltpu.HBM)
    inputs, in_specs = [], []
    for operand in operands:
        where, x = operand if isinstance(operand, tuple) else ("near", operand)
        if where != "plain":
            x = pltpu.with_memory_space_constraint(x, pltpu.VMEM if where == "near" else pltpu.HBM)
        inputs.append(x)
        in_specs.append(away if where == "far" else whole)
    out_specs = [away if isinstance(out, tuple) else whole for out in outs]
    result = pl.pallas_call(
        kernel,
        out_shape=[out[1] if isinstance(out, tuple) else out for out in outs],
        in_specs=in_specs,
        out_specs=out_specs,
        scratch_shapes=scratch,
        compiler_params=pltpu.CompilerParams(vmem_limit_bytes=VMEM_BYTES),
        cost_estimate=pl.CostEstimate(flops=0, bytes_accessed=cycles * 1024, transcendentals=0) if cycles else None,
        name=name,
    )(*inputs)
    return result if len(outs) > 1 else result[0]


def place():
    return (
        lax.axis_index("gz"),
        lax.axis_index("gy"),
        lax.axis_size("gz"),
        lax.axis_size("gy"),
    )


def pair_up(index):
    return index ^ 1


def same(index):
    return index


def z_other(index):
    return index + 1 if index % 2 else index - 1


def y_other(index):
    return index + 1 if index % 2 else index - 1


def y_ring(index):
    return y_other(index) % lax.axis_size("gy")


def permutation(z_partner, y_partner):
    z_count, y_count = lax.axis_size("gz"), lax.axis_size("gy")
    pairs = []
    for z in range(z_count):
        for y in range(y_count):
            to_z, to_y = z_partner(z), y_partner(y)
            if not 0 <= to_z < z_count:
                to_z, to_y = z, pair_up(y)
            elif not 0 <= to_y < y_count:
                to_z, to_y = pair_up(z), y
            pairs.append((z * y_count + y, to_z * y_count + to_y))
    return pairs


def send(x, z_partner=same, y_partner=same):
    return lax.ppermute(x, AXES, permutation(z_partner, y_partner))


def swap(x, axis, level):
    step = 1 << level
    if axis == "gy":
        step |= 1
    return lax.ppermute(x, axis, [(i, i ^ step) for i in range(lax.axis_size(axis))])


def levels_of(axis):
    return (lax.axis_size(axis) - 1).bit_length()


def flux(speed, lower, upper):
    return speed * jnp.where(speed > 0.0, lower, upper)


def z_rims_kernel(tracer, y_speed, z_speed, b_ref, a_ref, outer_rows, sem):
    z, _, _, _ = place()
    depth = tracer.shape[0]
    z_odd = lax.rem(z, 2)
    sides = ((b_ref, 1 - z_odd), (a_ref, z_odd))
    copies = []

    def start(source, target):
        copies.append(pltpu.make_async_copy(source, target, sem.at[len(copies)]))
        copies[-1].start()

    for side, (ref, low) in enumerate(sides):
        near_rows, fourth = (1 - low) * (depth - 3), jnp.where(low == 1, 3, depth - 4)
        for k, field in enumerate((tracer, z_speed)):
            start(field.at[pl.ds(fourth, 1)], outer_rows.at[side, pl.ds(k, 1)])
        for k, field in enumerate((tracer, z_speed, y_speed)):
            start(field.at[pl.ds(near_rows, 3)], ref.at[pl.ds(3 * k, 3)])
    for copy in copies:
        copy.wait()
    for side, (ref, low) in enumerate(sides):
        third, fourth = ref[2 * low], outer_rows[side, 0]
        speed = 0.5 * (ref[3 + 2 * low] + outer_rows[side, 1])
        ref[9] = flux(speed, jnp.where(low == 1, third, fourth), jnp.where(low == 1, fourth, third))


def z_rims(tracer, y_speed, z_speed):
    _, width, band = tracer.shape
    return call(
        z_rims_kernel,
        "z_rims",
        [near(10, width, band)] * 2,
        [("far", x) for x in (tracer, y_speed, z_speed)],
        scratch=[near(2, 2, width, band), pltpu.SemaphoreType.DMA((10,))],
        cycles=1000,
    )


def begin_kernel(tracer, y_speed, z_speed, _, o_ref, e_ref, c, ys, zs, sem):
    arrivals = [
        pltpu.make_async_copy(source, target, sem.at[k])
        for k, (source, target) in enumerate(((tracer, c), (z_speed, zs), (y_speed, ys)))
    ]
    for copy in arrivals:
        copy.start()
    _, y, _, _ = place()
    width = c.shape[1]
    y_odd = lax.rem(y, 2)
    for copy in arrivals:
        copy.wait()

    def rims(o_low):
        for ref, low in ((o_ref, o_low), (e_ref, not o_low)):
            tile = slice(0, 8) if low else slice(width - 8, width)
            tc, ty, tz = (turned(f[:, tile, :]) for f in (c, ys, zs))
            three = 0 if low else 5
            lower, upper = (2, 3) if low else (4, 5)
            ref[0:3] = tc[three : three + 3]
            ref[3:6] = ty[three : three + 3]
            ref[6:9] = tz[three : three + 3]
            ref[9] = flux(0.5 * (ty[lower] + ty[upper]), tc[lower], tc[upper])

    @pl.when(y_odd == 0)
    def _():
        rims(True)

    @pl.when(y_odd == 1)
    def _():
        rims(False)


def begin(tracer, y_speed, z_speed, after):
    depth, width, band = tracer.shape
    return call(
        begin_kernel,
        "begin",
        [near(10, depth, band)] * 2,
        [("far", x) for x in (tracer, y_speed, z_speed)] + [after],
        scratch=[near(depth, width, band)] * 3 + [pltpu.SemaphoreType.DMA((3,))],
        cycles=2000,
    )


PAD_TILES = 1


def rim_kernel(b, a, _, for_pair, for_other):
    z, y, _, _ = place()
    width = a.shape[1]
    z_odd, y_odd = lax.rem(z, 2) == 1, lax.rem(y, 2)

    def corners(out, low):
        tile, first = (slice(0, 8), 0) if low else (slice(width - 8, width), 5)
        empty = jnp.zeros((3, 1, out.shape[2]), F32)
        for f, row in enumerate((0, 6, 3)):
            side_a, side_b = (turned(ref[row : row + 3, tile, :])[first : first + 3] for ref in (a, b))
            below, above = jnp.where(z_odd, side_a, side_b), jnp.where(z_odd, side_b, side_a)
            out[3 * f : 3 * f + 3] = jnp.concatenate([empty, below, above, empty], axis=1)

    @pl.when(y_odd == 0)
    def _():
        corners(for_other, True)
        corners(for_pair, False)

    @pl.when(y_odd == 1)
    def _():
        corners(for_other, False)
        corners(for_pair, True)

    for_other[9:] = jnp.zeros((PAD_TILES, 8, for_other.shape[2]), F32)


def rim(a, b, after):
    band = a.shape[2]
    return call(rim_kernel, "rim", [near(9, 8, band), near(9 + PAD_TILES, 8, band)], [b, a, after], cycles=200)


def reciprocal(x):
    r = pl.reciprocal(x, approx=True)
    return r * (2.0 - x * r)


def turned(x):
    return jnp.swapaxes(x, 0, 1)


def resistances(kappa, r):
    count = kappa.shape[0]
    before, following = kappa[0], kappa[1]
    r[0] = jnp.zeros_like(before)
    for j in range(1, count):
        here = following
        if j + 1 < count:
            following = kappa[j + 1]
        r[j] = reciprocal((0.5 * RATE) * (before + here))
        before = here
    return kappa[0], before


def factor(sides):
    state = []
    for read, count, edge_low, edge_high, keep, _ in sides:
        one = jnp.ones_like(edge_low)
        if keep:
            keep[0][0] = one
            keep[1][count - 1] = one
        state.append([one, 1.0 + edge_low, one, 1.0 + edge_high])

    def faces(j):
        return [(read(j), read(count - j)) if j < count else None for read, count, _, _, _, _ in sides]

    longest = max(side[1] for side in sides)
    following = faces(1)
    for j in range(1, longest):
        here, following = following, faces(j + 1)
        for s, pair in zip(state, here):
            if pair is not None:
                s[0] = s[0] + pair[0] * s[1]
                s[1] = s[1] + s[0]
                s[2] = s[2] + pair[1] * s[3]
                s[3] = s[3] + s[2]
        for (_, count, _, _, keep, _), s, pair in zip(sides, state, here):
            if pair is not None and keep:
                keep[0][j] = s[0]
                keep[1][count - 1 - j] = s[2]
    for (_, _, _, edge_high, _, ports), s in zip(sides, state):
        if ports is not None:
            inverse = reciprocal(s[1] + edge_high * s[0])
            ports[0] = s[2] * inverse
            ports[1] = inverse
            ports[2] = s[0] * inverse


def outer(ports, index, count):
    return jnp.where(index == 0, RATE, 0.0) * ports[3], jnp.where(index == count - 1, RATE, 0.0) * ports[4]


def factor_kernel(kappa, r_y_far, r_z_far, ports_y, ports_z, kappa_y, r_y, r_z, sem):
    z, y, z_count, y_count = place()
    depth, width, _ = kappa.shape
    y_copy = pltpu.make_async_copy(r_y, r_y_far, sem.at[0])
    z_copy = pltpu.make_async_copy(r_z, r_z_far, sem.at[1])
    ports_z[3], ports_z[4] = resistances(kappa, r_z)
    z_copy.start()
    kappa_y[...] = turned(kappa[...])
    ports_y[3], ports_y[4] = resistances(kappa_y, r_y)
    y_copy.start()
    factor((
        (lambda j: r_y[j], width, *outer(ports_y, y, y_count), None, ports_y),
        (lambda j: r_z[j], depth, *outer(ports_z, z, z_count), None, ports_z),
    ))
    y_copy.wait()
    z_copy.wait()


def factor_lines(kappa):
    depth, width, band = kappa.shape
    along_y, along_z = (width, depth, band), (depth, width, band)
    return call(
        factor_kernel,
        "factor",
        [("far", far(*along_y)), ("far", far(*along_z)), near(5, depth, band), near(5, width, band)],
        [("plain", kappa)],
        scratch=[near(*along_y), near(*along_y), near(*along_z), pltpu.SemaphoreType.DMA((2,))],
        cycles=4000,
    )


def ports_kernel(axis, level, mine, theirs, joint, out):
    index = lax.axis_index(axis)
    is_left = (lax.shift_right_logical(index, level) & 1) == 0
    pairs = [(mine[k], theirs[k]) for k in range(5)]
    left = [jnp.where(is_left, m, t) for m, t in pairs]
    right = [jnp.where(is_left, t, m) for m, t in pairs]
    d = reciprocal(reciprocal((0.5 * RATE) * (left[4] + right[3])) + left[2] + right[0])
    low, high = left[0] - left[1] * left[1] * d, right[2] - right[1] * right[1] * d
    joint[0] = d
    joint[1] = left[1]
    joint[2] = right[1]
    if level + 2 == levels_of(axis):
        next_left = (lax.shift_right_logical(index, level + 1) & 1) == 0
        out[0] = jnp.where(next_left, high, low)
        out[1] = jnp.where(next_left, right[4], left[3])
    else:
        out[0] = low
        out[1] = left[1] * right[1] * d
        out[2] = high
        out[3] = left[3]
        out[4] = right[4]


def join_ports(mine, theirs, axis, level):
    _, lines, band = mine.shape

    def kernel(*refs):
        ports_kernel(axis, level, *refs)

    last = level + 2 == levels_of(axis)
    outs = [near(3, lines, band), near(2 if last else 5, lines, band)]
    return call(kernel, "join_ports", outs, [mine, theirs], cycles=100)


def join_all(ports, axis):
    joints = []
    for level in range(levels_of(axis) - 1):
        joint, ports = join_ports(ports, swap(ports, axis, level), axis, level)
        joints.append(joint)
    return joints, ports, swap(ports, axis, len(joints))


def source_kernel(axis, level, last, mine, theirs, joint, out, flow_ref):
    index = lax.axis_index(axis)
    is_left = (lax.shift_right_logical(index, level) & 1) == 0
    pairs = [(mine[k], theirs[k]) for k in range(2)]
    left = [jnp.where(is_left, m, t) for m, t in pairs]
    right = [jnp.where(is_left, t, m) for m, t in pairs]
    flow = (left[1] - right[0]) * joint[0]
    flow_ref[0] = flow
    low, high = left[0] - joint[1] * flow, right[1] + joint[2] * flow
    if last:
        next_left = (lax.shift_right_logical(index, level + 1) & 1) == 0
        out[0] = jnp.where(next_left, high, low)
    else:
        out[0] = low
        out[1] = high


def join_sources(mine, theirs, joint, axis, level):
    _, lines, band = mine.shape
    last = level + 2 == levels_of(axis)

    def kernel(*refs):
        source_kernel(axis, level, last, *refs)

    outs = [near(1 if last else 2, lines, band), near(1, lines, band)]
    return call(kernel, "join_sources", outs, [mine, theirs, joint], cycles=100)


def end_currents(axis, mine, theirs, edge, edge_theirs, joints, flows):
    index = lax.axis_index(axis)
    level = len(joints)
    is_left = (lax.shift_right_logical(index, level) & 1) == 0
    d = reciprocal(reciprocal((0.5 * RATE) * (edge[1] + edge_theirs[1])) + edge[0] + edge_theirs[0])
    flow = (mine[0] - theirs[0]) * d
    zero = jnp.zeros_like(flow)
    low, high = jnp.where(is_left, zero, -flow), jnp.where(is_left, -flow, zero)
    for level in range(level - 1, -1, -1):
        joint = joints[level]
        is_left = (lax.shift_right_logical(index, level) & 1) == 0
        flow = flows[level][0] + (joint[1] * low - joint[2] * high) * joint[0]
        low, high = jnp.where(is_left, low, flow), jnp.where(is_left, -flow, high)
    return low, high


def solve_open(values, phi, psi, scale, base, ports):
    count = base.shape[0]
    total = jnp.zeros(base.shape[1:], F32)
    following = (values[0], phi[0], psi[0])
    for j in range(count):
        value, low, high = following
        if j + 1 < count:
            following = (values[j + 1], phi[j + 1], psi[j + 1])
        total = total + low * value
        base[j] = high * total
    ports[1] = scale * total
    total = jnp.zeros(base.shape[1:], F32)
    following = (base[count - 1], values[count - 1], phi[count - 1], psi[count - 1])
    for j in range(count - 1, -1, -1):
        below, value, low, high = following
        if j > 0:
            following = (base[j - 1], values[j - 1], phi[j - 1], psi[j - 1])
        base[j] = scale * (below + low * total)
        total = total + high * value
    ports[0] = scale * total


def advect_kernel(
    tracer, y_speed, z_speed, b, a, o, e, corner, ab, ports_y, r_y_far, r_z_far, ports_z,
    base, sources, r_y, r_z, ports_out, c, ys, zs, sy, sz, phi, psi, kept, flux_z, flux_y, sem,
):
    z, y, z_count, y_count = place()
    depth, width, band = tracer.shape
    rows, cols = depth + 8, width + 8
    copies = [
        pltpu.make_async_copy(own, field.at[pl.ds(4, depth), pl.ds(0, width), :], sem.at[k])
        for k, (field, own) in enumerate(((ys, y_speed), (zs, z_speed), (c, tracer)))
    ]
    y_copy = pltpu.make_async_copy(r_y_far, r_y, sem.at[3])
    z_copy = pltpu.make_async_copy(r_z_far, r_z, sem.at[4])
    for copy in copies:
        copy.start()
    y_copy.start()
    z_copy.start()
    ports_out[...] = ports_z[...]
    z_odd, y_odd = lax.rem(z, 2), lax.rem(y, 2)
    keep_b = jnp.where((z_odd == 0) & (z == 0) | (z_odd == 1) & (z == z_count - 1), 0.0, 1.0)
    keep_o = jnp.where((y_odd == 0) & (y == 0) | (y_odd == 1) & (y == y_count - 1), 0.0, 1.0)
    keep_below = jnp.where(z_odd == 0, keep_b, 1.0)
    keep_above = jnp.where(z_odd == 1, keep_b, 1.0)
    column = lax.broadcasted_iota(jnp.int32, (8, band), 0)
    outside = (column < 4) & (y == y_count - 1) | (column >= 4) & (y == 0)
    inside = jnp.where(outside, 0.0, 1.0)

    for field in (c, ys, zs):
        field[0:4, width:cols, :] = jnp.zeros((4, 8, band), F32)
        field[4 + depth : rows, width:cols, :] = jnp.zeros((4, 8, band), F32)
    flux_z[:, width:cols, :] = jnp.zeros((2, 8, band), F32)
    for ref, low, keep in ((a, z_odd, 1.0), (b, 1 - z_odd, keep_b)):
        three = jnp.where(low == 1, 1, depth + 4)
        for k, field in enumerate((c, zs, ys)):
            field[pl.ds(three, 3), 0:width, :] = ref[3 * k : 3 * k + 3] * keep
        flux_z[1 - low, 0:width, :] = ref[9] * keep

    def sides(o_low):
        other, pair = (o, keep_o), (e, 1.0)
        (above, keep_up), (below, keep_down) = (pair, other) if o_low else (other, pair)
        empty = jnp.zeros((2, depth, band), F32)
        for k, field in enumerate((c, ys, zs)):
            three = slice(3 * k, 3 * k + 3)
            tile = jnp.concatenate([above[three] * keep_up, empty, below[three] * keep_down], axis=0)
            field[4 : 4 + depth, width:cols, :] = turned(tile)
        faces = [empty, above[9:10] * keep_up, empty[:1], below[9:10] * keep_down, empty, empty[:1]]
        flux_y[...] = turned(jnp.concatenate(faces, axis=0))

        def corners(ref, low, keep):
            start = width + (5 if low else 0)
            for f, field in enumerate((c, ys, zs)):
                for k in range(3):
                    field[1:4, start + k, :] = ref[3 * f + k, 1:4, :] * (keep * keep_below)
                    field[depth + 4 : depth + 7, start + k, :] = ref[3 * f + k, 4:7, :] * (keep * keep_above)

        corners(corner, o_low, keep_o)
        corners(ab, not o_low, 1.0)

    @pl.when(y_odd == 0)
    def _():
        sides(True)

    @pl.when(y_odd == 1)
    def _():
        sides(False)

    for copy in copies[:2]:
        copy.wait()

    def up(v):
        return pltpu.roll(v, cols - 1, 0)

    def down(v):
        return pltpu.roll(v, 1, 0)

    def faces(r, before):
        v = ys[r]
        sy[r] = 0.5 * (v + up(v))
        after = zs[r + 1]
        sz[r] = 0.5 * (before + after)
        return after

    lax.fori_loop(0, rows - 1, faces, zs[0], unroll=13)
    copies[2].wait()

    keep_low = jnp.where(z == 0, 0.0, 1.0)
    keep_high = jnp.where(z == z_count - 1, 0.0, 1.0)
    given = (column == 2) | (column == 4)
    for step in range(1, NSUB + 1):

        def row(r, carry, side=False, top=None):
            here, below = carry
            after = c[r + 1]
            above = flux(sz[r], here, after) if top is None else top
            across = flux(sy[r], here, up(here))
            if side:
                edge = jnp.where(given, flux_y[r - 4], across[width:cols])
                across = jnp.concatenate([across[0:width], edge], axis=0)
            new = here - (across - down(across)) - (above - below)
            c[r, 0:width, :] = new[0:width]
            c[r, width:cols, :] = new[width:cols] * inside
            return after, above

        if step == 1:
            carry = c[1], flux_z[0]
            for r in range(1, 4):
                carry = row(r, carry)
            side_row = lambda r, carry: row(r, carry, side=True)
            carry = lax.fori_loop(4, 4 + depth, side_row, carry, unroll=16)
            for r in range(4 + depth, rows - 2):
                carry = row(r, carry)
            row(rows - 2, carry, top=flux_z[1])
        else:
            below = flux(sz[step - 1], c[step - 1], c[step])
            lax.fori_loop(step, rows - step, row, (c[step], below), unroll=16)
        if step < NSUB:
            c[3] = c[3] * keep_low
            c[4 + depth] = c[4 + depth] * keep_high

    z_copy.wait()
    y_copy.wait()
    factor(((lambda j: r_y[j], width, *outer(ports_y, y, y_count), (phi, psi), None),))
    kept[...] = turned(c[4 : 4 + depth, 0:width, :])
    solve_open(kept, phi, psi, ports_y[1], base, sources)


def advect(tracer, y_speed, z_speed, halos, ports_y, r_y, r_z, ports_z):
    depth, width, band = tracer.shape
    padded = near(depth + 8, width + 8, band)
    along_y, along_z = near(width, depth, band), near(depth, width, band)
    return call(
        advect_kernel,
        "advect",
        [along_y, near(2, depth, band), along_y, along_z, near(5, width, band)],
        [("far", x) for x in (tracer, y_speed, z_speed)]
        + list(halos)
        + [ports_y, ("far", r_y), ("far", r_z), ports_z],
        scratch=[padded] * 5 + [along_y] * 3
        + [near(2, width + 8, band), near(depth, 8, band), pltpu.SemaphoreType.DMA((5,))],
        cycles=5000,
    )


def turn_kernel(levels, *refs):
    last, refs = refs[0:4], refs[4:]
    joints, flows = refs[0:levels], refs[levels : 2 * levels]
    ports_y, base_y, r_y, ports_z, r_z, _, base, sources, phi, psi, u, kept = refs[2 * levels :]
    z, y, z_count, y_count = place()
    width, depth = base_y.shape[0], base.shape[0]
    low, high = end_currents("gy", *last, joints, flows)
    edge, _ = outer(ports_y, y, y_count)
    value = low * ports_y[0] + high * ports_y[1]
    current = (1.0 + edge) * value - low
    u[0] = base_y[0] + value
    following = (r_y[1], base_y[1])
    for j in range(1, width):
        (r, own), following = following, (r_y[j + 1], base_y[j + 1]) if j + 1 < width else None
        value = value + r * current
        current = current + value
        u[j] = own + value
    factor(((lambda k: r_z[k], depth, *outer(ports_z, z, z_count), (phi, psi), None),))
    kept[...] = turned(u[...])
    solve_open(kept, phi, psi, ports_z[1], base, sources)


def turn(last, joints, flows, ports_y, base_y, r_y, ports_z, r_z, after):
    width, depth, band = base_y.shape
    along_z = near(depth, width, band)

    def kernel(*refs):
        turn_kernel(len(joints), *refs)

    return call(
        kernel,
        "turn",
        [along_z, near(2, width, band), along_z, along_z],
        [*last, *joints, *flows, ports_y, base_y, r_y, ports_z, r_z, after],
        scratch=[near(width, depth, band), along_z],
        cycles=1500,
    )


def finish_kernel(levels, *refs):
    last, refs = refs[0:4], refs[4:]
    joints, flows = refs[0:levels], refs[levels : 2 * levels]
    ports_z, base, phi, psi, out, u, sem = refs[2 * levels :]
    low, high = end_currents("gz", *last, joints, flows)
    scale = ports_z[1]
    low, high = low * scale, high * scale
    depth = base.shape[0]
    part = depth // 4
    copies = []
    for p in range(4):
        for k in range(p * part, (p + 1) * part):
            u[k] = base[k] + low * psi[k] + high * phi[k]
        block = pl.ds(p * part, part)
        copies.append(pltpu.make_async_copy(u.at[block], out.at[block], sem.at[p]))
        copies[-1].start()
    for copy in copies:
        copy.wait()


def finish(last, joints, flows, ports_z, base, phi, psi):
    def kernel(*refs):
        finish_kernel(len(joints), *refs)

    return call(
        kernel,
        "finish",
        [("far", jax.ShapeDtypeStruct(base.shape, F32))],
        [*last, *joints, *flows, ports_z, base, phi, psi],
        scratch=[near(*base.shape), pltpu.SemaphoreType.DMA((4,))],
        cycles=1000,
    )


def exchange_sources(sources, joints, axis):
    flows = []
    for level, joint in enumerate(joints):
        sources, flow = join_sources(sources, swap(sources, axis, level), joint, axis, level)
        flows.append(flow)
    return sources, swap(sources, axis, len(joints)), flows


def local(tracer, y_speed, z_speed, kappa):
    b, a = z_rims(tracer, y_speed, z_speed)
    o, e = begin(tracer, y_speed, z_speed, b)
    b = send(b, z_partner=z_other)
    a = send(a, z_partner=pair_up)
    e = swap(e, "gy", 0)
    o = send(o, y_partner=y_ring)
    r_y, r_z, ports_y, ports_z = factor_lines(kappa)
    for_pair, for_other = rim(a, b, ports_z)
    corner = send(for_other, y_partner=y_other)
    ab = swap(for_pair, "gy", 0)
    joints_y, edge_y, edge_y_theirs = join_all(ports_y, "gy")

    base, sources, r_y, r_z, ports_z = advect(
        tracer, y_speed, z_speed, (b, a, o, e, corner, ab), ports_y, r_y, r_z, ports_z
    )
    joints_z, edge_z, edge_z_theirs = join_all(ports_z, "gz")
    mine, theirs, flows = exchange_sources(sources, joints_y, "gy")
    base, sources, phi_z, psi_z = turn(
        (mine, theirs, edge_y, edge_y_theirs), joints_y, flows, ports_y, base, r_y, ports_z, r_z, joints_z[-1]
    )
    mine, theirs, flows = exchange_sources(sources, joints_z, "gz")
    return finish((mine, theirs, edge_z, edge_z_theirs), joints_z, flows, ports_z, base, phi_z, psi_z)


def solution(mesh):
    spec = P("gz", "gy", None)
    return jax.shard_map(
        local, mesh=mesh, in_specs=(spec,) * 4, out_specs=spec, check_vma=False
    )
```

```python
import jax
import jax.numpy as jnp
from jax import lax
from jax.experimental import pallas as pl
from jax.experimental.pallas import tpu as pltpu
from jax.sharding import PartitionSpec as P

NSUB = 4
RATE = 500.0
AXES = ("gz", "gy")
F32 = jnp.float32
VMEM_BYTES = 12 << 20


def near(*dims):
    return pltpu.VMEM(dims, F32)


def far(*dims):
    return pltpu.HBM(dims, F32)


def call(kernel, name, outs, operands, scratch=(), cycles=0):
    whole, away = pl.BlockSpec(memory_space=pltpu.VMEM), pl.BlockSpec(memory_space=pltpu.HBM)
    inputs, in_specs = [], []
    for operand in operands:
        where, x = operand if isinstance(operand, tuple) else ("near", operand)
        if where != "plain":
            x = pltpu.with_memory_space_constraint(x, pltpu.VMEM if where == "near" else pltpu.HBM)
        inputs.append(x)
        in_specs.append(away if where == "far" else whole)
    out_specs = [away if isinstance(out, tuple) else whole for out in outs]
    result = pl.pallas_call(
        kernel,
        out_shape=[out[1] if isinstance(out, tuple) else out for out in outs],
        in_specs=in_specs,
        out_specs=out_specs,
        scratch_shapes=scratch,
        compiler_params=pltpu.CompilerParams(vmem_limit_bytes=VMEM_BYTES),
        cost_estimate=pl.CostEstimate(flops=0, bytes_accessed=cycles * 1024, transcendentals=0) if cycles else None,
        name=name,
    )(*inputs)
    return result if len(outs) > 1 else result[0]


def place():
    return (
        lax.axis_index("gz"),
        lax.axis_index("gy"),
        lax.axis_size("gz"),
        lax.axis_size("gy"),
    )


def pair_up(index):
    return index ^ 1


def same(index):
    return index


def z_other(index):
    return index + 1 if index % 2 else index - 1


def y_other(index):
    return index + 1 if index % 2 else index - 1


def y_ring(index):
    return y_other(index) % lax.axis_size("gy")


def permutation(z_partner, y_partner):
    z_count, y_count = lax.axis_size("gz"), lax.axis_size("gy")
    pairs = []
    for z in range(z_count):
        for y in range(y_count):
            to_z, to_y = z_partner(z), y_partner(y)
            if not 0 <= to_z < z_count:
                to_z, to_y = z, pair_up(y)
            elif not 0 <= to_y < y_count:
                to_z, to_y = pair_up(z), y
            pairs.append((z * y_count + y, to_z * y_count + to_y))
    return pairs


def send(x, z_partner=same, y_partner=same):
    return lax.ppermute(x, AXES, permutation(z_partner, y_partner))


def swap(x, axis, level):
    step = 1 << level
    if axis == "gy":
        step |= 1
    return lax.ppermute(x, axis, [(i, i ^ step) for i in range(lax.axis_size(axis))])


def levels_of(axis):
    return (lax.axis_size(axis) - 1).bit_length()


def flux(speed, lower, upper):
    return speed * jnp.where(speed > 0.0, lower, upper)


def z_rims_kernel(tracer, y_speed, z_speed, b_ref, a_ref, outer_rows, sem):
    z, _, _, _ = place()
    depth = tracer.shape[0]
    z_odd = lax.rem(z, 2)
    sides = ((b_ref, 1 - z_odd), (a_ref, z_odd))
    copies = []

    def start(source, target):
        copies.append(pltpu.make_async_copy(source, target, sem.at[len(copies)]))
        copies[-1].start()

    for side, (ref, low) in enumerate(sides):
        near_rows, fourth = (1 - low) * (depth - 3), jnp.where(low == 1, 3, depth - 4)
        for k, field in enumerate((tracer, z_speed)):
            start(field.at[pl.ds(fourth, 1)], outer_rows.at[side, pl.ds(k, 1)])
        for k, field in enumerate((tracer, z_speed, y_speed)):
            start(field.at[pl.ds(near_rows, 3)], ref.at[pl.ds(3 * k, 3)])
    for copy in copies:
        copy.wait()
    for side, (ref, low) in enumerate(sides):
        third, fourth = ref[2 * low], outer_rows[side, 0]
        speed = 0.5 * (ref[3 + 2 * low] + outer_rows[side, 1])
        ref[9] = flux(speed, jnp.where(low == 1, third, fourth), jnp.where(low == 1, fourth, third))


def z_rims(tracer, y_speed, z_speed):
    _, width, band = tracer.shape
    return call(
        z_rims_kernel,
        "z_rims",
        [near(10, width, band)] * 2,
        [("far", x) for x in (tracer, y_speed, z_speed)],
        scratch=[near(2, 2, width, band), pltpu.SemaphoreType.DMA((10,))],
        cycles=1000,
    )


def begin_kernel(c, ys, zs, _, o_ref, e_ref):
    _, y, _, _ = place()
    width = c.shape[1]
    y_odd = lax.rem(y, 2)
    def rims(o_low):
        for ref, low in ((o_ref, o_low), (e_ref, not o_low)):
            tile = slice(0, 8) if low else slice(width - 8, width)
            tc, ty, tz = (turned(f[:, tile, :]) for f in (c, ys, zs))
            three = 0 if low else 5
            lower, upper = (2, 3) if low else (4, 5)
            ref[0:3] = tc[three : three + 3]
            ref[3:6] = ty[three : three + 3]
            ref[6:9] = tz[three : three + 3]
            ref[9] = flux(0.5 * (ty[lower] + ty[upper]), tc[lower], tc[upper])

    @pl.when(y_odd == 0)
    def _():
        rims(True)

    @pl.when(y_odd == 1)
    def _():
        rims(False)


def begin(tracer, y_speed, z_speed, after):
    depth, width, band = tracer.shape
    return call(
        begin_kernel,
        "begin",
        [near(10, depth, band)] * 2,
        [tracer, y_speed, z_speed, after],
        cycles=2000,
    )


PAD_TILES = 1


def rim_kernel(b, a, _, for_pair, for_other):
    z, y, _, _ = place()
    width = a.shape[1]
    z_odd, y_odd = lax.rem(z, 2) == 1, lax.rem(y, 2)

    def corners(out, low):
        tile, first = (slice(0, 8), 0) if low else (slice(width - 8, width), 5)
        empty = jnp.zeros((3, 1, out.shape[2]), F32)
        for f, row in enumerate((0, 6, 3)):
            side_a, side_b = (turned(ref[row : row + 3, tile, :])[first : first + 3] for ref in (a, b))
            below, above = jnp.where(z_odd, side_a, side_b), jnp.where(z_odd, side_b, side_a)
            out[3 * f : 3 * f + 3] = jnp.concatenate([empty, below, above, empty], axis=1)

    @pl.when(y_odd == 0)
    def _():
        corners(for_other, True)
        corners(for_pair, False)

    @pl.when(y_odd == 1)
    def _():
        corners(for_other, False)
        corners(for_pair, True)

    for_other[9:] = jnp.zeros((PAD_TILES, 8, for_other.shape[2]), F32)


def rim(a, b, after):
    band = a.shape[2]
    return call(rim_kernel, "rim", [near(9, 8, band), near(9 + PAD_TILES, 8, band)], [b, a, after], cycles=200)


def reciprocal(x):
    r = pl.reciprocal(x, approx=True)
    return r * (2.0 - x * r)


def turned(x):
    return jnp.swapaxes(x, 0, 1)


def resistances(kappa, r):
    count = kappa.shape[0]
    before, following = kappa[0], kappa[1]
    r[0] = jnp.zeros_like(before)
    for j in range(1, count):
        here = following
        if j + 1 < count:
            following = kappa[j + 1]
        r[j] = reciprocal((0.5 * RATE) * (before + here))
        before = here
    return kappa[0], before


def factor(sides):
    state = []
    for read, count, edge_low, edge_high, keep, _ in sides:
        one = jnp.ones_like(edge_low)
        if keep:
            keep[0][0] = one
            keep[1][count - 1] = one
        state.append([one, 1.0 + edge_low, one, 1.0 + edge_high])

    def faces(j):
        return [(read(j), read(count - j)) if j < count else None for read, count, _, _, _, _ in sides]

    longest = max(side[1] for side in sides)
    following = faces(1)
    for j in range(1, longest):
        here, following = following, faces(j + 1)
        for s, pair in zip(state, here):
            if pair is not None:
                s[0] = s[0] + pair[0] * s[1]
                s[1] = s[1] + s[0]
                s[2] = s[2] + pair[1] * s[3]
                s[3] = s[3] + s[2]
        for (_, count, _, _, keep, _), s, pair in zip(sides, state, here):
            if pair is not None and keep:
                keep[0][j] = s[0]
                keep[1][count - 1 - j] = s[2]
    for (_, _, _, edge_high, _, ports), s in zip(sides, state):
        if ports is not None:
            inverse = reciprocal(s[1] + edge_high * s[0])
            ports[0] = s[2] * inverse
            ports[1] = inverse
            ports[2] = s[0] * inverse


def outer(ports, index, count):
    return jnp.where(index == 0, RATE, 0.0) * ports[3], jnp.where(index == count - 1, RATE, 0.0) * ports[4]


def factor_kernel(kappa, r_y_far, r_z_far, ports_y, ports_z, kappa_y, r_y, r_z, sem):
    z, y, z_count, y_count = place()
    depth, width, _ = kappa.shape
    y_copy = pltpu.make_async_copy(r_y, r_y_far, sem.at[0])
    z_copy = pltpu.make_async_copy(r_z, r_z_far, sem.at[1])
    ports_z[3], ports_z[4] = resistances(kappa, r_z)
    z_copy.start()
    kappa_y[...] = turned(kappa[...])
    ports_y[3], ports_y[4] = resistances(kappa_y, r_y)
    y_copy.start()
    factor((
        (lambda j: r_y[j], width, *outer(ports_y, y, y_count), None, ports_y),
        (lambda j: r_z[j], depth, *outer(ports_z, z, z_count), None, ports_z),
    ))
    y_copy.wait()
    z_copy.wait()


def factor_lines(kappa):
    depth, width, band = kappa.shape
    along_y, along_z = (width, depth, band), (depth, width, band)
    return call(
        factor_kernel,
        "factor",
        [("far", far(*along_y)), ("far", far(*along_z)), near(5, depth, band), near(5, width, band)],
        [("plain", kappa)],
        scratch=[near(*along_y), near(*along_y), near(*along_z), pltpu.SemaphoreType.DMA((2,))],
        cycles=4000,
    )


def ports_kernel(axis, level, mine, theirs, joint, out):
    index = lax.axis_index(axis)
    is_left = (lax.shift_right_logical(index, level) & 1) == 0
    pairs = [(mine[k], theirs[k]) for k in range(5)]
    left = [jnp.where(is_left, m, t) for m, t in pairs]
    right = [jnp.where(is_left, t, m) for m, t in pairs]
    d = reciprocal(reciprocal((0.5 * RATE) * (left[4] + right[3])) + left[2] + right[0])
    low, high = left[0] - left[1] * left[1] * d, right[2] - right[1] * right[1] * d
    joint[0] = d
    joint[1] = left[1]
    joint[2] = right[1]
    if level + 2 == levels_of(axis):
        next_left = (lax.shift_right_logical(index, level + 1) & 1) == 0
        out[0] = jnp.where(next_left, high, low)
        out[1] = jnp.where(next_left, right[4], left[3])
    else:
        out[0] = low
        out[1] = left[1] * right[1] * d
        out[2] = high
        out[3] = left[3]
        out[4] = right[4]


def join_ports(mine, theirs, axis, level):
    _, lines, band = mine.shape

    def kernel(*refs):
        ports_kernel(axis, level, *refs)

    last = level + 2 == levels_of(axis)
    outs = [near(3, lines, band), near(2 if last else 5, lines, band)]
    return call(kernel, "join_ports", outs, [mine, theirs], cycles=100)


def join_all(ports, axis):
    joints = []
    for level in range(levels_of(axis) - 1):
        joint, ports = join_ports(ports, swap(ports, axis, level), axis, level)
        joints.append(joint)
    return joints, ports, swap(ports, axis, len(joints))


def source_kernel(axis, level, last, mine, theirs, joint, out, flow_ref):
    index = lax.axis_index(axis)
    is_left = (lax.shift_right_logical(index, level) & 1) == 0
    pairs = [(mine[k], theirs[k]) for k in range(2)]
    left = [jnp.where(is_left, m, t) for m, t in pairs]
    right = [jnp.where(is_left, t, m) for m, t in pairs]
    flow = (left[1] - right[0]) * joint[0]
    flow_ref[0] = flow
    low, high = left[0] - joint[1] * flow, right[1] + joint[2] * flow
    if last:
        next_left = (lax.shift_right_logical(index, level + 1) & 1) == 0
        out[0] = jnp.where(next_left, high, low)
    else:
        out[0] = low
        out[1] = high


def join_sources(mine, theirs, joint, axis, level):
    _, lines, band = mine.shape
    last = level + 2 == levels_of(axis)

    def kernel(*refs):
        source_kernel(axis, level, last, *refs)

    outs = [near(1 if last else 2, lines, band), near(1, lines, band)]
    return call(kernel, "join_sources", outs, [mine, theirs, joint], cycles=100)


def end_currents(axis, mine, theirs, edge, edge_theirs, joints, flows):
    index = lax.axis_index(axis)
    level = len(joints)
    is_left = (lax.shift_right_logical(index, level) & 1) == 0
    d = reciprocal(reciprocal((0.5 * RATE) * (edge[1] + edge_theirs[1])) + edge[0] + edge_theirs[0])
    flow = (mine[0] - theirs[0]) * d
    zero = jnp.zeros_like(flow)
    low, high = jnp.where(is_left, zero, -flow), jnp.where(is_left, -flow, zero)
    for level in range(level - 1, -1, -1):
        joint = joints[level]
        is_left = (lax.shift_right_logical(index, level) & 1) == 0
        flow = flows[level][0] + (joint[1] * low - joint[2] * high) * joint[0]
        low, high = jnp.where(is_left, low, flow), jnp.where(is_left, -flow, high)
    return low, high


def solve_open(values, phi, psi, scale, base, ports):
    count = base.shape[0]
    total = jnp.zeros(base.shape[1:], F32)
    following = (values[0], phi[0], psi[0])
    for j in range(count):
        value, low, high = following
        if j + 1 < count:
            following = (values[j + 1], phi[j + 1], psi[j + 1])
        total = total + low * value
        base[j] = high * total
    ports[1] = scale * total
    total = jnp.zeros(base.shape[1:], F32)
    following = (base[count - 1], values[count - 1], phi[count - 1], psi[count - 1])
    for j in range(count - 1, -1, -1):
        below, value, low, high = following
        if j > 0:
            following = (base[j - 1], values[j - 1], phi[j - 1], psi[j - 1])
        base[j] = scale * (below + low * total)
        total = total + high * value
    ports[0] = scale * total


def advect_kernel(
    tracer, y_speed, z_speed, b, a, o, e, corner, ab, ports_y, r_y_far, r_z_far, ports_z,
    base, sources, r_y, r_z, ports_out, c, ys, zs, sy, sz, phi, psi, kept, flux_z, flux_y, sem,
):
    z, y, z_count, y_count = place()
    depth, width, band = tracer.shape
    rows, cols = depth + 8, width + 8
    y_copy = pltpu.make_async_copy(r_y_far, r_y, sem.at[3])
    z_copy = pltpu.make_async_copy(r_z_far, r_z, sem.at[4])
    y_copy.start()
    z_copy.start()
    ports_out[...] = ports_z[...]
    z_odd, y_odd = lax.rem(z, 2), lax.rem(y, 2)
    keep_b = jnp.where((z_odd == 0) & (z == 0) | (z_odd == 1) & (z == z_count - 1), 0.0, 1.0)
    keep_o = jnp.where((y_odd == 0) & (y == 0) | (y_odd == 1) & (y == y_count - 1), 0.0, 1.0)
    keep_below = jnp.where(z_odd == 0, keep_b, 1.0)
    keep_above = jnp.where(z_odd == 1, keep_b, 1.0)
    column = lax.broadcasted_iota(jnp.int32, (8, band), 0)
    outside = (column < 4) & (y == y_count - 1) | (column >= 4) & (y == 0)
    inside = jnp.where(outside, 0.0, 1.0)

    for field in (c, ys, zs):
        field[0:4, width:cols, :] = jnp.zeros((4, 8, band), F32)
        field[4 + depth : rows, width:cols, :] = jnp.zeros((4, 8, band), F32)
    flux_z[:, width:cols, :] = jnp.zeros((2, 8, band), F32)
    for ref, low, keep in ((a, z_odd, 1.0), (b, 1 - z_odd, keep_b)):
        three = jnp.where(low == 1, 1, depth + 4)
        for k, field in enumerate((c, zs, ys)):
            field[pl.ds(three, 3), 0:width, :] = ref[3 * k : 3 * k + 3] * keep
        flux_z[1 - low, 0:width, :] = ref[9] * keep

    def sides(o_low):
        other, pair = (o, keep_o), (e, 1.0)
        (above, keep_up), (below, keep_down) = (pair, other) if o_low else (other, pair)
        empty = jnp.zeros((2, depth, band), F32)
        for k, field in enumerate((c, ys, zs)):
            three = slice(3 * k, 3 * k + 3)
            tile = jnp.concatenate([above[three] * keep_up, empty, below[three] * keep_down], axis=0)
            field[4 : 4 + depth, width:cols, :] = turned(tile)
        faces = [empty, above[9:10] * keep_up, empty[:1], below[9:10] * keep_down, empty, empty[:1]]
        flux_y[...] = turned(jnp.concatenate(faces, axis=0))

        def corners(ref, low, keep):
            start = width + (5 if low else 0)
            for f, field in enumerate((c, ys, zs)):
                for k in range(3):
                    field[1:4, start + k, :] = ref[3 * f + k, 1:4, :] * (keep * keep_below)
                    field[depth + 4 : depth + 7, start + k, :] = ref[3 * f + k, 4:7, :] * (keep * keep_above)

        corners(corner, o_low, keep_o)
        corners(ab, not o_low, 1.0)

    @pl.when(y_odd == 0)
    def _():
        sides(True)

    @pl.when(y_odd == 1)
    def _():
        sides(False)

    for field, own in ((ys, y_speed), (zs, z_speed), (c, tracer)):
        field[4 : 4 + depth, 0:width, :] = own[...]

    def up(v):
        return pltpu.roll(v, cols - 1, 0)

    def down(v):
        return pltpu.roll(v, 1, 0)

    def faces(r, before):
        v = ys[r]
        sy[r] = 0.5 * (v + up(v))
        after = zs[r + 1]
        sz[r] = 0.5 * (before + after)
        return after

    lax.fori_loop(0, rows - 1, faces, zs[0], unroll=13)

    keep_low = jnp.where(z == 0, 0.0, 1.0)
    keep_high = jnp.where(z == z_count - 1, 0.0, 1.0)
    given = (column == 2) | (column == 4)
    for step in range(1, NSUB + 1):

        def row(r, carry, side=False, top=None):
            here, below = carry
            after = c[r + 1]
            above = flux(sz[r], here, after) if top is None else top
            across = flux(sy[r], here, up(here))
            if side:
                edge = jnp.where(given, flux_y[r - 4], across[width:cols])
                across = jnp.concatenate([across[0:width], edge], axis=0)
            new = here - (across - down(across)) - (above - below)
            c[r, 0:width, :] = new[0:width]
            c[r, width:cols, :] = new[width:cols] * inside
            return after, above

        if step == 1:
            carry = c[1], flux_z[0]
            for r in range(1, 4):
                carry = row(r, carry)
            side_row = lambda r, carry: row(r, carry, side=True)
            carry = lax.fori_loop(4, 4 + depth, side_row, carry, unroll=16)
            for r in range(4 + depth, rows - 2):
                carry = row(r, carry)
            row(rows - 2, carry, top=flux_z[1])
        else:
            below = flux(sz[step - 1], c[step - 1], c[step])
            lax.fori_loop(step, rows - step, row, (c[step], below), unroll=16)
        if step < NSUB:
            c[3] = c[3] * keep_low
            c[4 + depth] = c[4 + depth] * keep_high

    z_copy.wait()
    y_copy.wait()
    factor(((lambda j: r_y[j], width, *outer(ports_y, y, y_count), (phi, psi), None),))
    kept[...] = turned(c[4 : 4 + depth, 0:width, :])
    solve_open(kept, phi, psi, ports_y[1], base, sources)


def advect(tracer, y_speed, z_speed, halos, ports_y, r_y, r_z, ports_z):
    depth, width, band = tracer.shape
    padded = near(depth + 8, width + 8, band)
    along_y, along_z = near(width, depth, band), near(depth, width, band)
    return call(
        advect_kernel,
        "advect",
        [along_y, near(2, depth, band), along_y, along_z, near(5, width, band)],
        [tracer, y_speed, z_speed]
        + list(halos)
        + [ports_y, ("far", r_y), ("far", r_z), ports_z],
        scratch=[padded] * 5 + [along_y] * 3
        + [near(2, width + 8, band), near(depth, 8, band), pltpu.SemaphoreType.DMA((5,))],
        cycles=5000,
    )


def turn_kernel(levels, *refs):
    last, refs = refs[0:4], refs[4:]
    joints, flows = refs[0:levels], refs[levels : 2 * levels]
    ports_y, base_y, r_y, ports_z, r_z, _, base, sources, phi, psi, u, kept = refs[2 * levels :]
    z, y, z_count, y_count = place()
    width, depth = base_y.shape[0], base.shape[0]
    low, high = end_currents("gy", *last, joints, flows)
    edge, _ = outer(ports_y, y, y_count)
    value = low * ports_y[0] + high * ports_y[1]
    current = (1.0 + edge) * value - low
    u[0] = base_y[0] + value
    following = (r_y[1], base_y[1])
    for j in range(1, width):
        (r, own), following = following, (r_y[j + 1], base_y[j + 1]) if j + 1 < width else None
        value = value + r * current
        current = current + value
        u[j] = own + value
    factor(((lambda k: r_z[k], depth, *outer(ports_z, z, z_count), (phi, psi), None),))
    kept[...] = turned(u[...])
    solve_open(kept, phi, psi, ports_z[1], base, sources)


def turn(last, joints, flows, ports_y, base_y, r_y, ports_z, r_z, after):
    width, depth, band = base_y.shape
    along_z = near(depth, width, band)

    def kernel(*refs):
        turn_kernel(len(joints), *refs)

    return call(
        kernel,
        "turn",
        [along_z, near(2, width, band), along_z, along_z],
        [*last, *joints, *flows, ports_y, base_y, r_y, ports_z, r_z, after],
        scratch=[near(width, depth, band), along_z],
        cycles=1500,
    )


def finish_kernel(levels, *refs):
    last, refs = refs[0:4], refs[4:]
    joints, flows = refs[0:levels], refs[levels : 2 * levels]
    ports_z, base, phi, psi, out, u, sem = refs[2 * levels :]
    low, high = end_currents("gz", *last, joints, flows)
    scale = ports_z[1]
    low, high = low * scale, high * scale
    depth = base.shape[0]
    part = depth // 4
    copies = []
    for p in range(4):
        for k in range(p * part, (p + 1) * part):
            u[k] = base[k] + low * psi[k] + high * phi[k]
        block = pl.ds(p * part, part)
        copies.append(pltpu.make_async_copy(u.at[block], out.at[block], sem.at[p]))
        copies[-1].start()
    for copy in copies:
        copy.wait()


def finish(last, joints, flows, ports_z, base, phi, psi):
    def kernel(*refs):
        finish_kernel(len(joints), *refs)

    return call(
        kernel,
        "finish",
        [("far", jax.ShapeDtypeStruct(base.shape, F32))],
        [*last, *joints, *flows, ports_z, base, phi, psi],
        scratch=[near(*base.shape), pltpu.SemaphoreType.DMA((4,))],
        cycles=1000,
    )


def exchange_sources(sources, joints, axis):
    flows = []
    for level, joint in enumerate(joints):
        sources, flow = join_sources(sources, swap(sources, axis, level), joint, axis, level)
        flows.append(flow)
    return sources, swap(sources, axis, len(joints)), flows


def local(tracer, y_speed, z_speed, kappa):
    b, a = z_rims(tracer, y_speed, z_speed)
    o, e = begin(tracer, y_speed, z_speed, b)
    b = send(b, z_partner=z_other)
    a = send(a, z_partner=pair_up)
    e = swap(e, "gy", 0)
    o = send(o, y_partner=y_ring)
    r_y, r_z, ports_y, ports_z = factor_lines(kappa)
    for_pair, for_other = rim(a, b, ports_z)
    corner = send(for_other, y_partner=y_other)
    ab = swap(for_pair, "gy", 0)
    joints_y, edge_y, edge_y_theirs = join_all(ports_y, "gy")

    base, sources, r_y, r_z, ports_z = advect(
        tracer, y_speed, z_speed, (b, a, o, e, corner, ab), ports_y, r_y, r_z, ports_z
    )
    joints_z, edge_z, edge_z_theirs = join_all(ports_z, "gz")
    mine, theirs, flows = exchange_sources(sources, joints_y, "gy")
    base, sources, phi_z, psi_z = turn(
        (mine, theirs, edge_y, edge_y_theirs), joints_y, flows, ports_y, base, r_y, ports_z, r_z, joints_z[-1]
    )
    mine, theirs, flows = exchange_sources(sources, joints_z, "gz")
    return finish((mine, theirs, edge_z, edge_z_theirs), joints_z, flows, ports_z, base, phi_z, psi_z)


def solution(mesh):
    spec = P("gz", "gy", None)
    return jax.shard_map(
        local, mesh=mesh, in_specs=(spec,) * 4, out_specs=spec, check_vma=False
    )
```

```python
import jax
import jax.numpy as jnp
from jax import lax
from jax.experimental import pallas as pl
from jax.experimental.pallas import tpu as pltpu
from jax.sharding import PartitionSpec as P

NSUB = 4
RATE = 500.0
AXES = ("gz", "gy")
F32 = jnp.float32
VMEM_BYTES = 12 << 20


def near(*dims):
    return pltpu.VMEM(dims, F32)


def far(*dims):
    return pltpu.HBM(dims, F32)


def call(kernel, name, outs, operands, scratch=(), cycles=0):
    whole, away = pl.BlockSpec(memory_space=pltpu.VMEM), pl.BlockSpec(memory_space=pltpu.HBM)
    inputs, in_specs = [], []
    for operand in operands:
        where, x = operand if isinstance(operand, tuple) else ("near", operand)
        if where != "plain":
            x = pltpu.with_memory_space_constraint(x, pltpu.VMEM if where == "near" else pltpu.HBM)
        inputs.append(x)
        in_specs.append(away if where == "far" else whole)
    out_specs = [away if isinstance(out, tuple) else whole for out in outs]
    result = pl.pallas_call(
        kernel,
        out_shape=[out[1] if isinstance(out, tuple) else out for out in outs],
        in_specs=in_specs,
        out_specs=out_specs,
        scratch_shapes=scratch,
        compiler_params=pltpu.CompilerParams(vmem_limit_bytes=VMEM_BYTES),
        cost_estimate=pl.CostEstimate(flops=0, bytes_accessed=cycles * 1024, transcendentals=0) if cycles else None,
        name=name,
    )(*inputs)
    return result if len(outs) > 1 else result[0]


def place():
    return (
        lax.axis_index("gz"),
        lax.axis_index("gy"),
        lax.axis_size("gz"),
        lax.axis_size("gy"),
    )


def pair_up(index):
    return index ^ 1


def same(index):
    return index


def z_other(index):
    return index + 1 if index % 2 else index - 1


def y_other(index):
    return index + 1 if index % 2 else index - 1


def y_ring(index):
    return y_other(index) % lax.axis_size("gy")


def permutation(z_partner, y_partner):
    z_count, y_count = lax.axis_size("gz"), lax.axis_size("gy")
    pairs = []
    for z in range(z_count):
        for y in range(y_count):
            to_z, to_y = z_partner(z), y_partner(y)
            if not 0 <= to_z < z_count:
                to_z, to_y = z, pair_up(y)
            elif not 0 <= to_y < y_count:
                to_z, to_y = pair_up(z), y
            pairs.append((z * y_count + y, to_z * y_count + to_y))
    return pairs


def send(x, z_partner=same, y_partner=same):
    return lax.ppermute(x, AXES, permutation(z_partner, y_partner))


def swap(x, axis, level):
    step = 1 << level
    if axis == "gy":
        step |= 1
    return lax.ppermute(x, axis, [(i, i ^ step) for i in range(lax.axis_size(axis))])


def levels_of(axis):
    return (lax.axis_size(axis) - 1).bit_length()


def flux(speed, lower, upper):
    return speed * jnp.where(speed > 0.0, lower, upper)


def z_rims_kernel(tracer, y_speed, z_speed, b_ref, a_ref, outer_rows, sem):
    z, _, _, _ = place()
    depth = tracer.shape[0]
    z_odd = lax.rem(z, 2)
    sides = ((b_ref, 1 - z_odd), (a_ref, z_odd))
    copies = []

    def start(source, target):
        copies.append(pltpu.make_async_copy(source, target, sem.at[len(copies)]))
        copies[-1].start()

    for side, (ref, low) in enumerate(sides):
        near_rows, fourth = (1 - low) * (depth - 3), jnp.where(low == 1, 3, depth - 4)
        for k, field in enumerate((tracer, z_speed)):
            start(field.at[pl.ds(fourth, 1)], outer_rows.at[side, pl.ds(k, 1)])
        for k, field in enumerate((tracer, z_speed, y_speed)):
            start(field.at[pl.ds(near_rows, 3)], ref.at[pl.ds(3 * k, 3)])
    for copy in copies:
        copy.wait()
    for side, (ref, low) in enumerate(sides):
        third, fourth = ref[2 * low], outer_rows[side, 0]
        speed = 0.5 * (ref[3 + 2 * low] + outer_rows[side, 1])
        ref[9] = flux(speed, jnp.where(low == 1, third, fourth), jnp.where(low == 1, fourth, third))


def z_rims(tracer, y_speed, z_speed):
    _, width, band = tracer.shape
    return call(
        z_rims_kernel,
        "z_rims",
        [near(10, width, band)] * 2,
        [("far", x) for x in (tracer, y_speed, z_speed)],
        scratch=[near(2, 2, width, band), pltpu.SemaphoreType.DMA((10,))],
        cycles=1000,
    )


def begin_kernel(c, ys, zs, _, o_ref, e_ref):
    _, y, _, _ = place()
    width = c.shape[1]
    y_odd = lax.rem(y, 2)
    def rims(o_low):
        for ref, low in ((o_ref, o_low), (e_ref, not o_low)):
            tile = slice(0, 8) if low else slice(width - 8, width)
            tc, ty, tz = (turned(f[:, tile, :]) for f in (c, ys, zs))
            three = 0 if low else 5
            lower, upper = (2, 3) if low else (4, 5)
            ref[0:3] = tc[three : three + 3]
            ref[3:6] = ty[three : three + 3]
            ref[6:9] = tz[three : three + 3]
            ref[9] = flux(0.5 * (ty[lower] + ty[upper]), tc[lower], tc[upper])

    @pl.when(y_odd == 0)
    def _():
        rims(True)

    @pl.when(y_odd == 1)
    def _():
        rims(False)


def begin(tracer, y_speed, z_speed, after):
    depth, width, band = tracer.shape
    return call(
        begin_kernel,
        "begin",
        [near(10, depth, band)] * 2,
        [tracer, y_speed, z_speed, after],
        cycles=2000,
    )


def rim_kernel(b, a, _, for_pair, for_other):
    z, y, _, _ = place()
    width = a.shape[1]
    z_odd, y_odd = lax.rem(z, 2) == 1, lax.rem(y, 2)

    def corners(out, low):
        tile, first = (slice(0, 8), 0) if low else (slice(width - 8, width), 5)
        empty = jnp.zeros((3, 1, out.shape[2]), F32)
        for f, row in enumerate((0, 6, 3)):
            side_a, side_b = (turned(ref[row : row + 3, tile, :])[first : first + 3] for ref in (a, b))
            below, above = jnp.where(z_odd, side_a, side_b), jnp.where(z_odd, side_b, side_a)
            out[3 * f : 3 * f + 3] = jnp.concatenate([empty, below, above, empty], axis=1)

    @pl.when(y_odd == 0)
    def _():
        corners(for_other, True)
        corners(for_pair, False)

    @pl.when(y_odd == 1)
    def _():
        corners(for_other, False)
        corners(for_pair, True)


def rim(a, b, after):
    band = a.shape[2]
    return call(rim_kernel, "rim", [near(9, 8, band), near(9, 8, band)], [b, a, after], cycles=200)


def reciprocal(x):
    r = pl.reciprocal(x, approx=True)
    return r * (2.0 - x * r)


def turned(x):
    return jnp.swapaxes(x, 0, 1)


def resistances(kappa, r):
    count = kappa.shape[0]
    before, following = kappa[0], kappa[1]
    r[0] = jnp.zeros_like(before)
    for j in range(1, count):
        here = following
        if j + 1 < count:
            following = kappa[j + 1]
        r[j] = reciprocal((0.5 * RATE) * (before + here))
        before = here
    return kappa[0], before


def factor(sides):
    state = []
    for read, count, edge_low, edge_high, keep, _ in sides:
        one = jnp.ones_like(edge_low)
        if keep:
            keep[0][0] = one
            keep[1][count - 1] = one
        state.append([one, 1.0 + edge_low, one, 1.0 + edge_high])

    def faces(j):
        return [(read(j), read(count - j)) if j < count else None for read, count, _, _, _, _ in sides]

    longest = max(side[1] for side in sides)
    following = faces(1)
    for j in range(1, longest):
        here, following = following, faces(j + 1)
        for s, pair in zip(state, here):
            if pair is not None:
                s[0] = s[0] + pair[0] * s[1]
                s[1] = s[1] + s[0]
                s[2] = s[2] + pair[1] * s[3]
                s[3] = s[3] + s[2]
        for (_, count, _, _, keep, _), s, pair in zip(sides, state, here):
            if pair is not None and keep:
                keep[0][j] = s[0]
                keep[1][count - 1 - j] = s[2]
    for (_, _, _, edge_high, _, ports), s in zip(sides, state):
        if ports is not None:
            inverse = reciprocal(s[1] + edge_high * s[0])
            ports[0] = s[2] * inverse
            ports[1] = inverse
            ports[2] = s[0] * inverse


def outer(ports, index, count):
    return jnp.where(index == 0, RATE, 0.0) * ports[3], jnp.where(index == count - 1, RATE, 0.0) * ports[4]


def factor_kernel(kappa, r_y_far, r_z_far, ports_y, ports_z, kappa_y, r_y, r_z, sem):
    z, y, z_count, y_count = place()
    depth, width, _ = kappa.shape
    y_copy = pltpu.make_async_copy(r_y, r_y_far, sem.at[0])
    z_copy = pltpu.make_async_copy(r_z, r_z_far, sem.at[1])
    ports_z[3], ports_z[4] = resistances(kappa, r_z)
    z_copy.start()
    kappa_y[...] = turned(kappa[...])
    ports_y[3], ports_y[4] = resistances(kappa_y, r_y)
    y_copy.start()
    factor((
        (lambda j: r_y[j], width, *outer(ports_y, y, y_count), None, ports_y),
        (lambda j: r_z[j], depth, *outer(ports_z, z, z_count), None, ports_z),
    ))
    y_copy.wait()
    z_copy.wait()


def factor_lines(kappa):
    depth, width, band = kappa.shape
    along_y, along_z = (width, depth, band), (depth, width, band)
    return call(
        factor_kernel,
        "factor",
        [("far", far(*along_y)), ("far", far(*along_z)), near(5, depth, band), near(5, width, band)],
        [("plain", kappa)],
        scratch=[near(*along_y), near(*along_y), near(*along_z), pltpu.SemaphoreType.DMA((2,))],
        cycles=4000,
    )


def ports_kernel(axis, level, mine, theirs, joint, out):
    index = lax.axis_index(axis)
    is_left = (lax.shift_right_logical(index, level) & 1) == 0
    pairs = [(mine[k], theirs[k]) for k in range(5)]
    left = [jnp.where(is_left, m, t) for m, t in pairs]
    right = [jnp.where(is_left, t, m) for m, t in pairs]
    d = reciprocal(reciprocal((0.5 * RATE) * (left[4] + right[3])) + left[2] + right[0])
    low, high = left[0] - left[1] * left[1] * d, right[2] - right[1] * right[1] * d
    joint[0] = d
    joint[1] = left[1]
    joint[2] = right[1]
    if level + 2 == levels_of(axis):
        next_left = (lax.shift_right_logical(index, level + 1) & 1) == 0
        out[0] = jnp.where(next_left, high, low)
        out[1] = jnp.where(next_left, right[4], left[3])
    else:
        out[0] = low
        out[1] = left[1] * right[1] * d
        out[2] = high
        out[3] = left[3]
        out[4] = right[4]


def join_ports(mine, theirs, axis, level):
    _, lines, band = mine.shape

    def kernel(*refs):
        ports_kernel(axis, level, *refs)

    last = level + 2 == levels_of(axis)
    outs = [near(3, lines, band), near(2 if last else 5, lines, band)]
    return call(kernel, "join_ports", outs, [mine, theirs], cycles=100)


def join_all(ports, axis):
    joints = []
    for level in range(levels_of(axis) - 1):
        joint, ports = join_ports(ports, swap(ports, axis, level), axis, level)
        joints.append(joint)
    return joints, ports, swap(ports, axis, len(joints))


def source_kernel(axis, level, last, mine, theirs, joint, out, flow_ref):
    index = lax.axis_index(axis)
    is_left = (lax.shift_right_logical(index, level) & 1) == 0
    pairs = [(mine[k], theirs[k]) for k in range(2)]
    left = [jnp.where(is_left, m, t) for m, t in pairs]
    right = [jnp.where(is_left, t, m) for m, t in pairs]
    flow = (left[1] - right[0]) * joint[0]
    flow_ref[0] = flow
    low, high = left[0] - joint[1] * flow, right[1] + joint[2] * flow
    if last:
        next_left = (lax.shift_right_logical(index, level + 1) & 1) == 0
        out[0] = jnp.where(next_left, high, low)
    else:
        out[0] = low
        out[1] = high


def join_sources(mine, theirs, joint, axis, level):
    _, lines, band = mine.shape
    last = level + 2 == levels_of(axis)

    def kernel(*refs):
        source_kernel(axis, level, last, *refs)

    outs = [near(1 if last else 2, lines, band), near(1, lines, band)]
    return call(kernel, "join_sources", outs, [mine, theirs, joint], cycles=100)


def end_currents(axis, mine, theirs, edge, edge_theirs, joints, flows):
    index = lax.axis_index(axis)
    level = len(joints)
    is_left = (lax.shift_right_logical(index, level) & 1) == 0
    d = reciprocal(reciprocal((0.5 * RATE) * (edge[1] + edge_theirs[1])) + edge[0] + edge_theirs[0])
    flow = (mine[0] - theirs[0]) * d
    zero = jnp.zeros_like(flow)
    low, high = jnp.where(is_left, zero, -flow), jnp.where(is_left, -flow, zero)
    for level in range(level - 1, -1, -1):
        joint = joints[level]
        is_left = (lax.shift_right_logical(index, level) & 1) == 0
        flow = flows[level][0] + (joint[1] * low - joint[2] * high) * joint[0]
        low, high = jnp.where(is_left, low, flow), jnp.where(is_left, -flow, high)
    return low, high


def solve_open(values, phi, psi, scale, base, ports):
    count = base.shape[0]
    total = jnp.zeros(base.shape[1:], F32)
    following = (values[0], phi[0], psi[0])
    for j in range(count):
        value, low, high = following
        if j + 1 < count:
            following = (values[j + 1], phi[j + 1], psi[j + 1])
        total = total + low * value
        base[j] = high * total
    ports[1] = scale * total
    total = jnp.zeros(base.shape[1:], F32)
    following = (base[count - 1], values[count - 1], phi[count - 1], psi[count - 1])
    for j in range(count - 1, -1, -1):
        below, value, low, high = following
        if j > 0:
            following = (base[j - 1], values[j - 1], phi[j - 1], psi[j - 1])
        base[j] = scale * (below + low * total)
        total = total + high * value
    ports[0] = scale * total


def advect_kernel(
    tracer, y_speed, z_speed, b, a, o, e, corner, ab, ports_y, r_y_far, r_z_far,
    base, sources, r_y, r_z, c, ys, zs, sy, sz, phi, psi, kept, flux_z, flux_y, sem,
):
    z, y, z_count, y_count = place()
    depth, width, band = tracer.shape
    rows, cols = depth + 8, width + 8
    y_copy = pltpu.make_async_copy(r_y_far, r_y, sem.at[3])
    z_copy = pltpu.make_async_copy(r_z_far, r_z, sem.at[4])
    y_copy.start()
    z_copy.start()
    z_odd, y_odd = lax.rem(z, 2), lax.rem(y, 2)
    keep_b = jnp.where((z_odd == 0) & (z == 0) | (z_odd == 1) & (z == z_count - 1), 0.0, 1.0)
    keep_o = jnp.where((y_odd == 0) & (y == 0) | (y_odd == 1) & (y == y_count - 1), 0.0, 1.0)
    keep_below = jnp.where(z_odd == 0, keep_b, 1.0)
    keep_above = jnp.where(z_odd == 1, keep_b, 1.0)
    column = lax.broadcasted_iota(jnp.int32, (8, band), 0)
    outside = (column < 4) & (y == y_count - 1) | (column >= 4) & (y == 0)
    inside = jnp.where(outside, 0.0, 1.0)

    for field in (c, ys, zs):
        field[0:4, width:cols, :] = jnp.zeros((4, 8, band), F32)
        field[4 + depth : rows, width:cols, :] = jnp.zeros((4, 8, band), F32)
    flux_z[:, width:cols, :] = jnp.zeros((2, 8, band), F32)
    for ref, low, keep in ((a, z_odd, 1.0), (b, 1 - z_odd, keep_b)):
        three = jnp.where(low == 1, 1, depth + 4)
        for k, field in enumerate((c, zs, ys)):
            field[pl.ds(three, 3), 0:width, :] = ref[3 * k : 3 * k + 3] * keep
        flux_z[1 - low, 0:width, :] = ref[9] * keep

    def sides(o_low):
        other, pair = (o, keep_o), (e, 1.0)
        (above, keep_up), (below, keep_down) = (pair, other) if o_low else (other, pair)
        empty = jnp.zeros((2, depth, band), F32)
        for k, field in enumerate((c, ys, zs)):
            three = slice(3 * k, 3 * k + 3)
            tile = jnp.concatenate([above[three] * keep_up, empty, below[three] * keep_down], axis=0)
            field[4 : 4 + depth, width:cols, :] = turned(tile)
        faces = [empty, above[9:10] * keep_up, empty[:1], below[9:10] * keep_down, empty, empty[:1]]
        flux_y[...] = turned(jnp.concatenate(faces, axis=0))

        def corners(ref, low, keep):
            start = width + (5 if low else 0)
            for f, field in enumerate((c, ys, zs)):
                for k in range(3):
                    field[1:4, start + k, :] = ref[3 * f + k, 1:4, :] * (keep * keep_below)
                    field[depth + 4 : depth + 7, start + k, :] = ref[3 * f + k, 4:7, :] * (keep * keep_above)

        corners(corner, o_low, keep_o)
        corners(ab, not o_low, 1.0)

    @pl.when(y_odd == 0)
    def _():
        sides(True)

    @pl.when(y_odd == 1)
    def _():
        sides(False)

    for field, own in ((ys, y_speed), (zs, z_speed), (c, tracer)):
        field[4 : 4 + depth, 0:width, :] = own[...]

    def up(v):
        return pltpu.roll(v, cols - 1, 0)

    def down(v):
        return pltpu.roll(v, 1, 0)

    def faces(r, before):
        v = ys[r]
        sy[r] = 0.5 * (v + up(v))
        after = zs[r + 1]
        sz[r] = 0.5 * (before + after)
        return after

    lax.fori_loop(0, rows - 1, faces, zs[0], unroll=39)

    keep_low = jnp.where(z == 0, 0.0, 1.0)
    keep_high = jnp.where(z == z_count - 1, 0.0, 1.0)
    given = (column == 2) | (column == 4)
    for step in range(1, NSUB + 1):

        def row(r, carry, side=False, top=None):
            here, below = carry
            after = c[r + 1]
            above = flux(sz[r], here, after) if top is None else top
            across = flux(sy[r], here, up(here))
            if side:
                edge = jnp.where(given, flux_y[r - 4], across[width:cols])
                across = jnp.concatenate([across[0:width], edge], axis=0)
            new = here - (across - down(across)) - (above - below)
            c[r, 0:width, :] = new[0:width]
            c[r, width:cols, :] = new[width:cols] * inside
            return after, above

        if step == 1:
            carry = c[1], flux_z[0]
            for r in range(1, 4):
                carry = row(r, carry)
            side_row = lambda r, carry: row(r, carry, side=True)
            carry = lax.fori_loop(4, 4 + depth, side_row, carry, unroll=16)
            for r in range(4 + depth, rows - 2):
                carry = row(r, carry)
            row(rows - 2, carry, top=flux_z[1])
        else:
            below = flux(sz[step - 1], c[step - 1], c[step])
            lax.fori_loop(step, rows - step, row, (c[step], below), unroll=16)
        if step < NSUB:
            c[3] = c[3] * keep_low
            c[4 + depth] = c[4 + depth] * keep_high

    z_copy.wait()
    y_copy.wait()
    factor(((lambda j: r_y[j], width, *outer(ports_y, y, y_count), (phi, psi), None),))
    kept[...] = turned(c[4 : 4 + depth, 0:width, :])
    solve_open(kept, phi, psi, ports_y[1], base, sources)


def advect(tracer, y_speed, z_speed, halos, ports_y, r_y, r_z):
    depth, width, band = tracer.shape
    padded = near(depth + 8, width + 8, band)
    along_y, along_z = near(width, depth, band), near(depth, width, band)
    return call(
        advect_kernel,
        "advect",
        [along_y, near(2, depth, band), along_y, along_z],
        [tracer, y_speed, z_speed]
        + list(halos)
        + [ports_y, ("far", r_y), ("far", r_z)],
        scratch=[padded] * 5 + [along_y] * 3
        + [near(2, width + 8, band), near(depth, 8, band), pltpu.SemaphoreType.DMA((5,))],
        cycles=5000,
    )


def turn_kernel(levels, *refs):
    last, refs = refs[0:4], refs[4:]
    joints, flows = refs[0:levels], refs[levels : 2 * levels]
    ports_y, base_y, r_y, ports_z, r_z, _, base, sources, phi, psi, u, kept = refs[2 * levels :]
    z, y, z_count, y_count = place()
    width, depth = base_y.shape[0], base.shape[0]
    low, high = end_currents("gy", *last, joints, flows)
    edge, _ = outer(ports_y, y, y_count)
    factor(((lambda k: r_z[k], depth, *outer(ports_z, z, z_count), (phi, psi), None),))
    value = low * ports_y[0] + high * ports_y[1]
    current = (1.0 + edge) * value - low
    u[0] = base_y[0] + value
    following = (r_y[1], base_y[1])
    for j in range(1, width):
        (r, own), following = following, (r_y[j + 1], base_y[j + 1]) if j + 1 < width else None
        value = value + r * current
        current = current + value
        u[j] = own + value
    kept[...] = turned(u[...])
    solve_open(kept, phi, psi, ports_z[1], base, sources)


def turn(last, joints, flows, ports_y, base_y, r_y, ports_z, r_z, after):
    width, depth, band = base_y.shape
    along_z = near(depth, width, band)

    def kernel(*refs):
        turn_kernel(len(joints), *refs)

    return call(
        kernel,
        "turn",
        [along_z, near(2, width, band), along_z, along_z],
        [*last, *joints, *flows, ports_y, base_y, r_y, ports_z, r_z, after],
        scratch=[near(width, depth, band), along_z],
        cycles=1500,
    )


def finish_kernel(levels, *refs):
    last, refs = refs[0:4], refs[4:]
    joints, flows = refs[0:levels], refs[levels : 2 * levels]
    ports_z, base, phi, psi, out, u, sem = refs[2 * levels :]
    low, high = end_currents("gz", *last, joints, flows)
    scale = ports_z[1]
    low, high = low * scale, high * scale
    depth = base.shape[0]
    part = depth // 4
    copies = []
    for p in range(4):
        for k in range(p * part, (p + 1) * part):
            u[k] = base[k] + low * psi[k] + high * phi[k]
        block = pl.ds(p * part, part)
        copies.append(pltpu.make_async_copy(u.at[block], out.at[block], sem.at[p]))
        copies[-1].start()
    for copy in copies:
        copy.wait()


def finish(last, joints, flows, ports_z, base, phi, psi):
    def kernel(*refs):
        finish_kernel(len(joints), *refs)

    return call(
        kernel,
        "finish",
        [("far", jax.ShapeDtypeStruct(base.shape, F32))],
        [*last, *joints, *flows, ports_z, base, phi, psi],
        scratch=[near(*base.shape), pltpu.SemaphoreType.DMA((4,))],
        cycles=1000,
    )


def exchange_sources(sources, joints, axis):
    flows = []
    for level, joint in enumerate(joints):
        sources, flow = join_sources(sources, swap(sources, axis, level), joint, axis, level)
        flows.append(flow)
    return sources, swap(sources, axis, len(joints)), flows


def local(tracer, y_speed, z_speed, kappa):
    b, a = z_rims(tracer, y_speed, z_speed)
    o, e = begin(tracer, y_speed, z_speed, b)
    b = send(b, z_partner=z_other)
    a = send(a, z_partner=pair_up)
    e = swap(e, "gy", 0)
    o = send(o, y_partner=y_ring)
    r_y, r_z, ports_y, ports_z = factor_lines(kappa)
    for_pair, for_other = rim(a, b, ports_z)
    corner = send(for_other, y_partner=y_other)
    ab = swap(for_pair, "gy", 0)
    joints_y, edge_y, edge_y_theirs = join_all(ports_y, "gy")

    base, sources, r_y, r_z = advect(
        tracer, y_speed, z_speed, (b, a, o, e, corner, ab), ports_y, r_y, r_z
    )
    joints_z, edge_z, edge_z_theirs = join_all(ports_z, "gz")
    mine, theirs, flows = exchange_sources(sources, joints_y, "gy")
    base, sources, phi_z, psi_z = turn(
        (mine, theirs, edge_y, edge_y_theirs), joints_y, flows, ports_y, base, r_y, ports_z, r_z, joints_z[-1]
    )
    mine, theirs, flows = exchange_sources(sources, joints_z, "gz")
    return finish((mine, theirs, edge_z, edge_z_theirs), joints_z, flows, ports_z, base, phi_z, psi_z)


def solution(mesh):
    spec = P("gz", "gy", None)
    return jax.shard_map(
        local, mesh=mesh, in_specs=(spec,) * 4, out_specs=spec, check_vma=False
    )
```

```python
import jax
import jax.numpy as jnp
from jax import lax
from jax.experimental import pallas as pl
from jax.experimental.pallas import tpu as pltpu
from jax.sharding import PartitionSpec as P

NSUB = 4
RATE = 500.0
AXES = ("gz", "gy")
F32 = jnp.float32
VMEM_BYTES = 12 << 20


def near(*dims):
    return pltpu.VMEM(dims, F32)


def far(*dims):
    return pltpu.HBM(dims, F32)


def call(kernel, name, outs, operands, scratch=(), cycles=0):
    whole, away = pl.BlockSpec(memory_space=pltpu.VMEM), pl.BlockSpec(memory_space=pltpu.HBM)
    inputs, in_specs = [], []
    for operand in operands:
        where, x = operand if isinstance(operand, tuple) else ("near", operand)
        if where != "plain":
            x = pltpu.with_memory_space_constraint(x, pltpu.VMEM if where == "near" else pltpu.HBM)
        inputs.append(x)
        in_specs.append(away if where == "far" else whole)
    out_specs = [away if isinstance(out, tuple) else whole for out in outs]
    result = pl.pallas_call(
        kernel,
        out_shape=[out[1] if isinstance(out, tuple) else out for out in outs],
        in_specs=in_specs,
        out_specs=out_specs,
        scratch_shapes=scratch,
        compiler_params=pltpu.CompilerParams(vmem_limit_bytes=VMEM_BYTES),
        cost_estimate=pl.CostEstimate(flops=0, bytes_accessed=cycles * 1024, transcendentals=0) if cycles else None,
        name=name,
    )(*inputs)
    return result if len(outs) > 1 else result[0]


def place():
    return (
        lax.axis_index("gz"),
        lax.axis_index("gy"),
        lax.axis_size("gz"),
        lax.axis_size("gy"),
    )


def pair_up(index):
    return index ^ 1


def same(index):
    return index


def z_other(index):
    return index + 1 if index % 2 else index - 1


def y_other(index):
    return index + 1 if index % 2 else index - 1


def y_ring(index):
    return y_other(index) % lax.axis_size("gy")


def permutation(z_partner, y_partner):
    z_count, y_count = lax.axis_size("gz"), lax.axis_size("gy")
    pairs = []
    for z in range(z_count):
        for y in range(y_count):
            to_z, to_y = z_partner(z), y_partner(y)
            if not 0 <= to_z < z_count:
                to_z, to_y = z, pair_up(y)
            elif not 0 <= to_y < y_count:
                to_z, to_y = pair_up(z), y
            pairs.append((z * y_count + y, to_z * y_count + to_y))
    return pairs


def send(x, z_partner=same, y_partner=same):
    return lax.ppermute(x, AXES, permutation(z_partner, y_partner))


def swap(x, axis, level):
    step = 1 << level
    if axis == "gy":
        step |= 1
    return lax.ppermute(x, axis, [(i, i ^ step) for i in range(lax.axis_size(axis))])


def levels_of(axis):
    return (lax.axis_size(axis) - 1).bit_length()


def flux(speed, lower, upper):
    return speed * jnp.where(speed > 0.0, lower, upper)


def z_rims_kernel(tracer, y_speed, z_speed, b_ref, a_ref, outer_rows, sem):
    z, _, _, _ = place()
    depth = tracer.shape[0]
    z_odd = lax.rem(z, 2)
    sides = ((b_ref, 1 - z_odd), (a_ref, z_odd))
    copies = []

    def start(source, target):
        copies.append(pltpu.make_async_copy(source, target, sem.at[len(copies)]))
        copies[-1].start()

    for side, (ref, low) in enumerate(sides):
        near_rows, fourth = (1 - low) * (depth - 3), jnp.where(low == 1, 3, depth - 4)
        for k, field in enumerate((tracer, z_speed)):
            start(field.at[pl.ds(fourth, 1)], outer_rows.at[side, pl.ds(k, 1)])
        for k, field in enumerate((tracer, z_speed, y_speed)):
            start(field.at[pl.ds(near_rows, 3)], ref.at[pl.ds(3 * k, 3)])
    for copy in copies:
        copy.wait()
    for side, (ref, low) in enumerate(sides):
        third, fourth = ref[2 * low], outer_rows[side, 0]
        speed = 0.5 * (ref[3 + 2 * low] + outer_rows[side, 1])
        ref[9] = flux(speed, jnp.where(low == 1, third, fourth), jnp.where(low == 1, fourth, third))


def z_rims(tracer, y_speed, z_speed):
    _, width, band = tracer.shape
    return call(
        z_rims_kernel,
        "z_rims",
        [near(10, width, band)] * 2,
        [("far", x) for x in (tracer, y_speed, z_speed)],
        scratch=[near(2, 2, width, band), pltpu.SemaphoreType.DMA((10,))],
        cycles=1000,
    )


def begin_kernel(c, ys, zs, _, o_ref, e_ref):
    _, y, _, _ = place()
    width = c.shape[1]
    y_odd = lax.rem(y, 2)
    def rims(o_low):
        for ref, low in ((o_ref, o_low), (e_ref, not o_low)):
            tile = slice(0, 8) if low else slice(width - 8, width)
            tc, ty, tz = (turned(f[:, tile, :]) for f in (c, ys, zs))
            three = 0 if low else 5
            lower, upper = (2, 3) if low else (4, 5)
            ref[0:3] = tc[three : three + 3]
            ref[3:6] = ty[three : three + 3]
            ref[6:9] = tz[three : three + 3]
            ref[9] = flux(0.5 * (ty[lower] + ty[upper]), tc[lower], tc[upper])

    @pl.when(y_odd == 0)
    def _():
        rims(True)

    @pl.when(y_odd == 1)
    def _():
        rims(False)


def begin(tracer, y_speed, z_speed, after):
    depth, width, band = tracer.shape
    return call(
        begin_kernel,
        "begin",
        [near(10, depth, band)] * 2,
        [tracer, y_speed, z_speed, after],
        cycles=2000,
    )


def rim_kernel(b, a, _, for_pair, for_other):
    z, y, _, _ = place()
    width = a.shape[1]
    z_odd, y_odd = lax.rem(z, 2) == 1, lax.rem(y, 2)

    def corners(out, low):
        tile, first = (slice(0, 8), 0) if low else (slice(width - 8, width), 5)
        one, two, three = (0, 1, 2) if low else (2, 1, 0)
        empty = jnp.zeros((1, out.shape[2]), F32)
        for f, row in enumerate((0, 6, 3)):
            side_a, side_b = (turned(ref[row : row + 3, tile, :])[first : first + 3] for ref in (a, b))
            below, above = jnp.where(z_odd, side_a, side_b), jnp.where(z_odd, side_b, side_a)
            out[2 * f] = jnp.concatenate([empty, below[one], above[one], empty], axis=0)
            out[2 * f + 1] = jnp.concatenate(
                [empty, below[three, 2:3], below[two, 1:3], above[two, 0:2], above[three, 0:1], empty], axis=0
            )

    for_other[6:] = jnp.zeros((2, 8, for_other.shape[2]), F32)

    @pl.when(y_odd == 0)
    def _():
        corners(for_other, True)
        corners(for_pair, False)

    @pl.when(y_odd == 1)
    def _():
        corners(for_other, False)
        corners(for_pair, True)


def rim(a, b, after):
    band = a.shape[2]
    return call(rim_kernel, "rim", [near(6, 8, band), near(8, 8, band)], [b, a, after], cycles=200)


def reciprocal(x):
    r = pl.reciprocal(x, approx=True)
    return r * (2.0 - x * r)


def turned(x):
    return jnp.swapaxes(x, 0, 1)


def resistances(kappa, r):
    count = kappa.shape[0]
    before, following = kappa[0], kappa[1]
    r[0] = jnp.zeros_like(before)
    for j in range(1, count):
        here = following
        if j + 1 < count:
            following = kappa[j + 1]
        r[j] = reciprocal((0.5 * RATE) * (before + here))
        before = here
    return kappa[0], before


def factor(sides):
    state = []
    for read, count, edge_low, edge_high, keep, _ in sides:
        one = jnp.ones_like(edge_low)
        if keep:
            keep[0][0] = one
            keep[1][count - 1] = one
        state.append([one, 1.0 + edge_low, one, 1.0 + edge_high])

    def faces(j):
        return [(read(j), read(count - j)) if j < count else None for read, count, _, _, _, _ in sides]

    longest = max(side[1] for side in sides)
    following = faces(1)
    for j in range(1, longest):
        here, following = following, faces(j + 1)
        for s, pair in zip(state, here):
            if pair is not None:
                s[0] = s[0] + pair[0] * s[1]
                s[1] = s[1] + s[0]
                s[2] = s[2] + pair[1] * s[3]
                s[3] = s[3] + s[2]
        for (_, count, _, _, keep, _), s, pair in zip(sides, state, here):
            if pair is not None and keep:
                keep[0][j] = s[0]
                keep[1][count - 1 - j] = s[2]
    for (_, _, _, edge_high, _, ports), s in zip(sides, state):
        if ports is not None:
            inverse = reciprocal(s[1] + edge_high * s[0])
            ports[0] = s[2] * inverse
            ports[1] = inverse
            ports[2] = s[0] * inverse


def outer(ports, index, count):
    return jnp.where(index == 0, RATE, 0.0) * ports[3], jnp.where(index == count - 1, RATE, 0.0) * ports[4]


def factor_kernel(kappa, r_y_far, r_z_far, ports_y, ports_z, kappa_y, r_y, r_z, sem):
    z, y, z_count, y_count = place()
    depth, width, _ = kappa.shape
    y_copy = pltpu.make_async_copy(r_y, r_y_far, sem.at[0])
    z_copy = pltpu.make_async_copy(r_z, r_z_far, sem.at[1])
    ports_z[3], ports_z[4] = resistances(kappa, r_z)
    z_copy.start()
    kappa_y[...] = turned(kappa[...])
    ports_y[3], ports_y[4] = resistances(kappa_y, r_y)
    y_copy.start()
    factor((
        (lambda j: r_y[j], width, *outer(ports_y, y, y_count), None, ports_y),
        (lambda j: r_z[j], depth, *outer(ports_z, z, z_count), None, ports_z),
    ))
    y_copy.wait()
    z_copy.wait()


def factor_lines(kappa):
    depth, width, band = kappa.shape
    along_y, along_z = (width, depth, band), (depth, width, band)
    return call(
        factor_kernel,
        "factor",
        [("far", far(*along_y)), ("far", far(*along_z)), near(5, depth, band), near(5, width, band)],
        [("plain", kappa)],
        scratch=[near(*along_y), near(*along_y), near(*along_z), pltpu.SemaphoreType.DMA((2,))],
        cycles=4000,
    )


def ports_kernel(axis, level, mine, theirs, joint, out):
    index = lax.axis_index(axis)
    is_left = (lax.shift_right_logical(index, level) & 1) == 0
    pairs = [(mine[k], theirs[k]) for k in range(5)]
    left = [jnp.where(is_left, m, t) for m, t in pairs]
    right = [jnp.where(is_left, t, m) for m, t in pairs]
    d = reciprocal(reciprocal((0.5 * RATE) * (left[4] + right[3])) + left[2] + right[0])
    low, high = left[0] - left[1] * left[1] * d, right[2] - right[1] * right[1] * d
    joint[0] = d
    joint[1] = left[1]
    joint[2] = right[1]
    if level + 2 == levels_of(axis):
        next_left = (lax.shift_right_logical(index, level + 1) & 1) == 0
        out[0] = jnp.where(next_left, high, low)
        out[1] = jnp.where(next_left, right[4], left[3])
    else:
        out[0] = low
        out[1] = left[1] * right[1] * d
        out[2] = high
        out[3] = left[3]
        out[4] = right[4]


def join_ports(mine, theirs, axis, level):
    _, lines, band = mine.shape

    def kernel(*refs):
        ports_kernel(axis, level, *refs)

    last = level + 2 == levels_of(axis)
    outs = [near(3, lines, band), near(2 if last else 5, lines, band)]
    return call(kernel, "join_ports", outs, [mine, theirs], cycles=100)


def join_all(ports, axis):
    joints = []
    for level in range(levels_of(axis) - 1):
        joint, ports = join_ports(ports, swap(ports, axis, level), axis, level)
        joints.append(joint)
    return joints, ports, swap(ports, axis, len(joints))


def source_kernel(axis, level, last, mine, theirs, joint, out, flow_ref):
    index = lax.axis_index(axis)
    is_left = (lax.shift_right_logical(index, level) & 1) == 0
    pairs = [(mine[k], theirs[k]) for k in range(2)]
    left = [jnp.where(is_left, m, t) for m, t in pairs]
    right = [jnp.where(is_left, t, m) for m, t in pairs]
    flow = (left[1] - right[0]) * joint[0]
    flow_ref[0] = flow
    low, high = left[0] - joint[1] * flow, right[1] + joint[2] * flow
    if last:
        next_left = (lax.shift_right_logical(index, level + 1) & 1) == 0
        out[0] = jnp.where(next_left, high, low)
    else:
        out[0] = low
        out[1] = high


def join_sources(mine, theirs, joint, axis, level):
    _, lines, band = mine.shape
    last = level + 2 == levels_of(axis)

    def kernel(*refs):
        source_kernel(axis, level, last, *refs)

    outs = [near(1 if last else 2, lines, band), near(1, lines, band)]
    return call(kernel, "join_sources", outs, [mine, theirs, joint], cycles=100)


def end_currents(axis, mine, theirs, edge, edge_theirs, joints, flows):
    index = lax.axis_index(axis)
    level = len(joints)
    is_left = (lax.shift_right_logical(index, level) & 1) == 0
    d = reciprocal(reciprocal((0.5 * RATE) * (edge[1] + edge_theirs[1])) + edge[0] + edge_theirs[0])
    flow = (mine[0] - theirs[0]) * d
    zero = jnp.zeros_like(flow)
    low, high = jnp.where(is_left, zero, -flow), jnp.where(is_left, -flow, zero)
    for level in range(level - 1, -1, -1):
        joint = joints[level]
        is_left = (lax.shift_right_logical(index, level) & 1) == 0
        flow = flows[level][0] + (joint[1] * low - joint[2] * high) * joint[0]
        low, high = jnp.where(is_left, low, flow), jnp.where(is_left, -flow, high)
    return low, high


def solve_open(values, phi, psi, scale, base, ports):
    count = base.shape[0]
    total = jnp.zeros(base.shape[1:], F32)
    following = (values[0], phi[0], psi[0])
    for j in range(count):
        value, low, high = following
        if j + 1 < count:
            following = (values[j + 1], phi[j + 1], psi[j + 1])
        total = total + low * value
        base[j] = high * total
    ports[1] = scale * total
    total = jnp.zeros(base.shape[1:], F32)
    following = (base[count - 1], values[count - 1], phi[count - 1], psi[count - 1])
    for j in range(count - 1, -1, -1):
        below, value, low, high = following
        if j > 0:
            following = (base[j - 1], values[j - 1], phi[j - 1], psi[j - 1])
        base[j] = scale * (below + low * total)
        total = total + high * value
    ports[0] = scale * total


def advect_kernel(
    tracer, y_speed, z_speed, b, a, o, e, corner, ab, ports_y, r_y_far, r_z_far,
    base, sources, r_y, r_z, c, ys, zs, sy, sz, phi, psi, kept, flux_z, flux_y, sem,
):
    z, y, z_count, y_count = place()
    depth, width, band = tracer.shape
    rows, cols = depth + 8, width + 8
    y_copy = pltpu.make_async_copy(r_y_far, r_y, sem.at[3])
    z_copy = pltpu.make_async_copy(r_z_far, r_z, sem.at[4])
    y_copy.start()
    z_copy.start()
    z_odd, y_odd = lax.rem(z, 2), lax.rem(y, 2)
    keep_b = jnp.where((z_odd == 0) & (z == 0) | (z_odd == 1) & (z == z_count - 1), 0.0, 1.0)
    keep_o = jnp.where((y_odd == 0) & (y == 0) | (y_odd == 1) & (y == y_count - 1), 0.0, 1.0)
    keep_below = jnp.where(z_odd == 0, keep_b, 1.0)
    keep_above = jnp.where(z_odd == 1, keep_b, 1.0)
    column = lax.broadcasted_iota(jnp.int32, (8, band), 0)
    outside = (column < 4) & (y == y_count - 1) | (column >= 4) & (y == 0)
    inside = jnp.where(outside, 0.0, 1.0)

    for field in (c, ys, zs):
        field[0:4, width:cols, :] = jnp.zeros((4, 8, band), F32)
        field[4 + depth : rows, width:cols, :] = jnp.zeros((4, 8, band), F32)
    flux_z[:, width:cols, :] = jnp.zeros((2, 8, band), F32)
    for ref, low, keep in ((a, z_odd, 1.0), (b, 1 - z_odd, keep_b)):
        three = jnp.where(low == 1, 1, depth + 4)
        for k, field in enumerate((c, zs, ys)):
            field[pl.ds(three, 3), 0:width, :] = ref[3 * k : 3 * k + 3] * keep
        flux_z[1 - low, 0:width, :] = ref[9] * keep

    def sides(o_low):
        other, pair = (o, keep_o), (e, 1.0)
        (above, keep_up), (below, keep_down) = (pair, other) if o_low else (other, pair)
        empty = jnp.zeros((2, depth, band), F32)
        for k, field in enumerate((c, ys, zs)):
            three = slice(3 * k, 3 * k + 3)
            tile = jnp.concatenate([above[three] * keep_up, empty, below[three] * keep_down], axis=0)
            field[4 : 4 + depth, width:cols, :] = turned(tile)
        faces = [empty, above[9:10] * keep_up, empty[:1], below[9:10] * keep_down, empty, empty[:1]]
        flux_y[...] = turned(jnp.concatenate(faces, axis=0))

        def corners(ref, low, keep):
            one, two, three = (width + 7, width + 6, width + 5) if low else (width, width + 1, width + 2)
            top = 4 + depth
            for f, field in enumerate((c, ys, zs)):
                near_tile, far_tile = ref.at[2 * f], ref.at[2 * f + 1]
                field[1:4, one, :] = near_tile[1:4] * (keep * keep_below)
                field[top : top + 3, one, :] = near_tile[4:7] * (keep * keep_above)
                field[2:4, two, :] = far_tile[2:4] * (keep * keep_below)
                field[top : top + 2, two, :] = far_tile[4:6] * (keep * keep_above)
                field[3:4, three, :] = far_tile[1:2] * (keep * keep_below)
                field[top : top + 1, three, :] = far_tile[6:7] * (keep * keep_above)

        corners(corner, o_low, keep_o)
        corners(ab, not o_low, 1.0)

    @pl.when(y_odd == 0)
    def _():
        sides(True)

    @pl.when(y_odd == 1)
    def _():
        sides(False)

    for field, own in ((ys, y_speed), (zs, z_speed), (c, tracer)):
        field[4 : 4 + depth, 0:width, :] = own[...]

    def up(v):
        return pltpu.roll(v, cols - 1, 0)

    def down(v):
        return pltpu.roll(v, 1, 0)

    def faces(r, before):
        v = ys[r]
        sy[r] = 0.5 * (v + up(v))
        after = zs[r + 1]
        sz[r] = 0.5 * (before + after)
        return after

    lax.fori_loop(0, rows - 1, faces, zs[0], unroll=39)

    keep_low = jnp.where(z == 0, 0.0, 1.0)
    keep_high = jnp.where(z == z_count - 1, 0.0, 1.0)
    given = (column == 2) | (column == 4)
    for step in range(1, NSUB + 1):

        def row(r, carry, side=False, top=None):
            here, below = carry
            after = c[r + 1]
            above = flux(sz[r], here, after) if top is None else top
            across = flux(sy[r], here, up(here))
            if side:
                edge = jnp.where(given, flux_y[r - 4], across[width:cols])
                across = jnp.concatenate([across[0:width], edge], axis=0)
            new = here - (across - down(across)) - (above - below)
            c[r, 0:width, :] = new[0:width]
            c[r, width:cols, :] = new[width:cols] * inside
            return after, above

        if step == 1:
            carry = c[1], flux_z[0]
            for r in range(1, 4):
                carry = row(r, carry)
            side_row = lambda r, carry: row(r, carry, side=True)
            carry = lax.fori_loop(4, 4 + depth, side_row, carry, unroll=16)
            for r in range(4 + depth, rows - 2):
                carry = row(r, carry)
            row(rows - 2, carry, top=flux_z[1])
        else:
            below = flux(sz[step - 1], c[step - 1], c[step])
            lax.fori_loop(step, rows - step, row, (c[step], below), unroll=16)
        if step < NSUB:
            c[3] = c[3] * keep_low
            c[4 + depth] = c[4 + depth] * keep_high

    z_copy.wait()
    y_copy.wait()
    factor(((lambda j: r_y[j], width, *outer(ports_y, y, y_count), (phi, psi), None),))
    kept[...] = turned(c[4 : 4 + depth, 0:width, :])
    solve_open(kept, phi, psi, ports_y[1], base, sources)


def advect(tracer, y_speed, z_speed, halos, ports_y, r_y, r_z):
    depth, width, band = tracer.shape
    padded = near(depth + 8, width + 8, band)
    along_y, along_z = near(width, depth, band), near(depth, width, band)
    return call(
        advect_kernel,
        "advect",
        [along_y, near(2, depth, band), along_y, along_z],
        [tracer, y_speed, z_speed]
        + list(halos)
        + [ports_y, ("far", r_y), ("far", r_z)],
        scratch=[padded] * 5 + [along_y] * 3
        + [near(2, width + 8, band), near(depth, 8, band), pltpu.SemaphoreType.DMA((5,))],
        cycles=5000,
    )


def turn_kernel(levels, *refs):
    last, refs = refs[0:4], refs[4:]
    joints, flows = refs[0:levels], refs[levels : 2 * levels]
    ports_y, base_y, r_y, ports_z, r_z, _, base, sources, phi, psi, u, kept = refs[2 * levels :]
    z, y, z_count, y_count = place()
    width, depth = base_y.shape[0], base.shape[0]
    low, high = end_currents("gy", *last, joints, flows)
    edge, _ = outer(ports_y, y, y_count)
    factor(((lambda k: r_z[k], depth, *outer(ports_z, z, z_count), (phi, psi), None),))
    value = low * ports_y[0] + high * ports_y[1]
    current = (1.0 + edge) * value - low
    u[0] = base_y[0] + value
    following = (r_y[1], base_y[1])
    for j in range(1, width):
        (r, own), following = following, (r_y[j + 1], base_y[j + 1]) if j + 1 < width else None
        value = value + r * current
        current = current + value
        u[j] = own + value
    kept[...] = turned(u[...])
    solve_open(kept, phi, psi, ports_z[1], base, sources)


def turn(last, joints, flows, ports_y, base_y, r_y, ports_z, r_z, after):
    width, depth, band = base_y.shape
    along_z = near(depth, width, band)

    def kernel(*refs):
        turn_kernel(len(joints), *refs)

    return call(
        kernel,
        "turn",
        [along_z, near(2, width, band), along_z, along_z],
        [*last, *joints, *flows, ports_y, base_y, r_y, ports_z, r_z, after],
        scratch=[near(width, depth, band), along_z],
        cycles=1500,
    )


def finish_kernel(levels, *refs):
    last, refs = refs[0:4], refs[4:]
    joints, flows = refs[0:levels], refs[levels : 2 * levels]
    ports_z, base, phi, psi, out, u, sem = refs[2 * levels :]
    low, high = end_currents("gz", *last, joints, flows)
    scale = ports_z[1]
    low, high = low * scale, high * scale
    depth = base.shape[0]
    part = depth // 4
    copies = []
    for p in range(4):
        for k in range(p * part, (p + 1) * part):
            u[k] = base[k] + low * psi[k] + high * phi[k]
        block = pl.ds(p * part, part)
        copies.append(pltpu.make_async_copy(u.at[block], out.at[block], sem.at[p]))
        copies[-1].start()
    for copy in copies:
        copy.wait()


def finish(last, joints, flows, ports_z, base, phi, psi):
    def kernel(*refs):
        finish_kernel(len(joints), *refs)

    return call(
        kernel,
        "finish",
        [("far", jax.ShapeDtypeStruct(base.shape, F32))],
        [*last, *joints, *flows, ports_z, base, phi, psi],
        scratch=[near(*base.shape), pltpu.SemaphoreType.DMA((4,))],
        cycles=1000,
    )


def exchange_sources(sources, joints, axis):
    flows = []
    for level, joint in enumerate(joints):
        sources, flow = join_sources(sources, swap(sources, axis, level), joint, axis, level)
        flows.append(flow)
    return sources, swap(sources, axis, len(joints)), flows


def local(tracer, y_speed, z_speed, kappa):
    b, a = z_rims(tracer, y_speed, z_speed)
    o, e = begin(tracer, y_speed, z_speed, b)
    b = send(b, z_partner=z_other)
    a = send(a, z_partner=pair_up)
    e = swap(e, "gy", 0)
    o = send(o, y_partner=y_ring)
    r_y, r_z, ports_y, ports_z = factor_lines(kappa)
    for_pair, for_other = rim(a, b, ports_z)
    corner = send(for_other, y_partner=y_other)
    ab = swap(for_pair, "gy", 0)
    joints_y, edge_y, edge_y_theirs = join_all(ports_y, "gy")

    base, sources, r_y, r_z = advect(
        tracer, y_speed, z_speed, (b, a, o, e, corner, ab), ports_y, r_y, r_z
    )
    joints_z, edge_z, edge_z_theirs = join_all(ports_z, "gz")
    mine, theirs, flows = exchange_sources(sources, joints_y, "gy")
    base, sources, phi_z, psi_z = turn(
        (mine, theirs, edge_y, edge_y_theirs), joints_y, flows, ports_y, base, r_y, ports_z, r_z, joints_z[-1]
    )
    mine, theirs, flows = exchange_sources(sources, joints_z, "gz")
    return finish((mine, theirs, edge_z, edge_z_theirs), joints_z, flows, ports_z, base, phi_z, psi_z)


def solution(mesh):
    spec = P("gz", "gy", None)
    return jax.shard_map(
        local, mesh=mesh, in_specs=(spec,) * 4, out_specs=spec, check_vma=False
    )
```

```python
import jax
import jax.numpy as jnp
from jax import lax
from jax.experimental import pallas as pl
from jax.experimental.pallas import tpu as pltpu
from jax.sharding import PartitionSpec as P

NSUB = 4
RATE = 500.0
AXES = ("gz", "gy")
F32 = jnp.float32
VMEM_BYTES = 12 << 20


def near(*dims):
    return pltpu.VMEM(dims, F32)


def far(*dims):
    return pltpu.HBM(dims, F32)


def call(kernel, name, outs, operands, scratch=(), cycles=0):
    whole, away = pl.BlockSpec(memory_space=pltpu.VMEM), pl.BlockSpec(memory_space=pltpu.HBM)
    inputs, in_specs = [], []
    for operand in operands:
        where, x = operand if isinstance(operand, tuple) else ("near", operand)
        if where != "plain":
            x = pltpu.with_memory_space_constraint(x, pltpu.VMEM if where == "near" else pltpu.HBM)
        inputs.append(x)
        in_specs.append(away if where == "far" else whole)
    out_specs = [away if isinstance(out, tuple) else whole for out in outs]
    result = pl.pallas_call(
        kernel,
        out_shape=[out[1] if isinstance(out, tuple) else out for out in outs],
        in_specs=in_specs,
        out_specs=out_specs,
        scratch_shapes=scratch,
        compiler_params=pltpu.CompilerParams(vmem_limit_bytes=VMEM_BYTES),
        cost_estimate=pl.CostEstimate(flops=0, bytes_accessed=cycles * 1024, transcendentals=0) if cycles else None,
        name=name,
    )(*inputs)
    return result if len(outs) > 1 else result[0]


def place():
    return (
        lax.axis_index("gz"),
        lax.axis_index("gy"),
        lax.axis_size("gz"),
        lax.axis_size("gy"),
    )


def pair_up(index):
    return index ^ 1


def same(index):
    return index


def z_other(index):
    return index + 1 if index % 2 else index - 1


def y_other(index):
    return index + 1 if index % 2 else index - 1


def y_ring(index):
    return y_other(index) % lax.axis_size("gy")


def permutation(z_partner, y_partner):
    z_count, y_count = lax.axis_size("gz"), lax.axis_size("gy")
    pairs = []
    for z in range(z_count):
        for y in range(y_count):
            to_z, to_y = z_partner(z), y_partner(y)
            if not 0 <= to_z < z_count:
                to_z, to_y = z, pair_up(y)
            elif not 0 <= to_y < y_count:
                to_z, to_y = pair_up(z), y
            pairs.append((z * y_count + y, to_z * y_count + to_y))
    return pairs


def send(x, z_partner=same, y_partner=same):
    return lax.ppermute(x, AXES, permutation(z_partner, y_partner))


def swap(x, axis, level):
    step = 1 << level
    if axis == "gy":
        step |= 1
    return lax.ppermute(x, axis, [(i, i ^ step) for i in range(lax.axis_size(axis))])


def levels_of(axis):
    return (lax.axis_size(axis) - 1).bit_length()


def flux(speed, lower, upper):
    return speed * jnp.where(speed > 0.0, lower, upper)


def z_rims_kernel(tracer, y_speed, z_speed, b_ref, a_ref, outer_rows, sem):
    z, _, _, _ = place()
    depth = tracer.shape[0]
    z_odd = lax.rem(z, 2)
    sides = ((b_ref, 1 - z_odd), (a_ref, z_odd))
    copies = []

    def start(source, target):
        copies.append(pltpu.make_async_copy(source, target, sem.at[len(copies)]))
        copies[-1].start()

    for side, (ref, low) in enumerate(sides):
        near_rows, fourth = (1 - low) * (depth - 3), jnp.where(low == 1, 3, depth - 4)
        for k, field in enumerate((tracer, z_speed)):
            start(field.at[pl.ds(fourth, 1)], outer_rows.at[side, pl.ds(k, 1)])
        for k, field in enumerate((tracer, z_speed, y_speed)):
            start(field.at[pl.ds(near_rows, 3)], ref.at[pl.ds(3 * k, 3)])
    for copy in copies:
        copy.wait()
    for side, (ref, low) in enumerate(sides):
        third, fourth = ref[2 * low], outer_rows[side, 0]
        speed = 0.5 * (ref[3 + 2 * low] + outer_rows[side, 1])
        ref[9] = flux(speed, jnp.where(low == 1, third, fourth), jnp.where(low == 1, fourth, third))


def z_rims(tracer, y_speed, z_speed):
    _, width, band = tracer.shape
    return call(
        z_rims_kernel,
        "z_rims",
        [near(10, width, band)] * 2,
        [("far", x) for x in (tracer, y_speed, z_speed)],
        scratch=[near(2, 2, width, band), pltpu.SemaphoreType.DMA((10,))],
        cycles=1000,
    )


def begin_kernel(c, ys, zs, _, o_ref, e_ref):
    _, y, _, _ = place()
    width = c.shape[1]
    y_odd = lax.rem(y, 2)
    def rims(o_low):
        for ref, low in ((o_ref, o_low), (e_ref, not o_low)):
            tile = slice(0, 8) if low else slice(width - 8, width)
            tc, ty, tz = (turned(f[:, tile, :]) for f in (c, ys, zs))
            three = 0 if low else 5
            lower, upper = (2, 3) if low else (4, 5)
            ref[0:3] = tc[three : three + 3]
            ref[3:6] = ty[three : three + 3]
            ref[6:9] = tz[three : three + 3]
            ref[9] = flux(0.5 * (ty[lower] + ty[upper]), tc[lower], tc[upper])

    @pl.when(y_odd == 0)
    def _():
        rims(True)

    @pl.when(y_odd == 1)
    def _():
        rims(False)


def begin(tracer, y_speed, z_speed, after):
    depth, width, band = tracer.shape
    return call(
        begin_kernel,
        "begin",
        [near(10, depth, band)] * 2,
        [tracer, y_speed, z_speed, after],
        cycles=2000,
    )


def rim_kernel(b, a, for_pair, for_other):
    z, y, _, _ = place()
    width = a.shape[1]
    z_odd, y_odd = lax.rem(z, 2) == 1, lax.rem(y, 2)

    def corners(out, low):
        tile, first = (slice(0, 8), 0) if low else (slice(width - 8, width), 5)
        one, two, three = (0, 1, 2) if low else (2, 1, 0)
        empty = jnp.zeros((1, out.shape[2]), F32)
        for f, row in enumerate((0, 6, 3)):
            side_a, side_b = (turned(ref[row : row + 3, tile, :])[first : first + 3] for ref in (a, b))
            below, above = jnp.where(z_odd, side_a, side_b), jnp.where(z_odd, side_b, side_a)
            out[2 * f] = jnp.concatenate([empty, below[one], above[one], empty], axis=0)
            out[2 * f + 1] = jnp.concatenate(
                [empty, below[three, 2:3], below[two, 1:3], above[two, 0:2], above[three, 0:1], empty], axis=0
            )

    for_other[6:] = jnp.zeros((2, 8, for_other.shape[2]), F32)

    @pl.when(y_odd == 0)
    def _():
        corners(for_other, True)
        corners(for_pair, False)

    @pl.when(y_odd == 1)
    def _():
        corners(for_other, False)
        corners(for_pair, True)


def rim(a, b):
    band = a.shape[2]
    return call(rim_kernel, "rim", [near(6, 8, band), near(8, 8, band)], [b, a], cycles=200)


def reciprocal(x):
    r = pl.reciprocal(x, approx=True)
    return r * (2.0 - x * r)


def turned(x):
    return jnp.swapaxes(x, 0, 1)


def resistances(kappa, r):
    count = kappa.shape[0]
    before, following = kappa[0], kappa[1]
    r[0] = jnp.zeros_like(before)
    for j in range(1, count):
        here = following
        if j + 1 < count:
            following = kappa[j + 1]
        r[j] = reciprocal((0.5 * RATE) * (before + here))
        before = here
    return kappa[0], before


def factor(sides):
    state = []
    for read, count, edge_low, edge_high, keep, _ in sides:
        one = jnp.ones_like(edge_low)
        if keep:
            keep[0][0] = one
            keep[1][count - 1] = one
        state.append([one, 1.0 + edge_low, one, 1.0 + edge_high])

    def faces(j):
        return [(read(j), read(count - j)) if j < count else None for read, count, _, _, _, _ in sides]

    longest = max(side[1] for side in sides)
    following = faces(1)
    for j in range(1, longest):
        here, following = following, faces(j + 1)
        for s, pair in zip(state, here):
            if pair is not None:
                s[0] = s[0] + pair[0] * s[1]
                s[1] = s[1] + s[0]
                s[2] = s[2] + pair[1] * s[3]
                s[3] = s[3] + s[2]
        for (_, count, _, _, keep, _), s, pair in zip(sides, state, here):
            if pair is not None and keep:
                keep[0][j] = s[0]
                keep[1][count - 1 - j] = s[2]
    for (_, _, _, edge_high, _, ports), s in zip(sides, state):
        if ports is not None:
            inverse = reciprocal(s[1] + edge_high * s[0])
            ports[0] = s[2] * inverse
            ports[1] = inverse
            ports[2] = s[0] * inverse


def outer(ports, index, count):
    return jnp.where(index == 0, RATE, 0.0) * ports[3], jnp.where(index == count - 1, RATE, 0.0) * ports[4]


def factor_kernel(kappa, r_y_far, r_z_far, ports_y, ports_z, kappa_y, r_y, r_z, sem):
    z, y, z_count, y_count = place()
    depth, width, _ = kappa.shape
    y_copy = pltpu.make_async_copy(r_y, r_y_far, sem.at[0])
    z_copy = pltpu.make_async_copy(r_z, r_z_far, sem.at[1])
    ports_z[3], ports_z[4] = resistances(kappa, r_z)
    z_copy.start()
    kappa_y[...] = turned(kappa[...])
    ports_y[3], ports_y[4] = resistances(kappa_y, r_y)
    y_copy.start()
    factor((
        (lambda j: r_y[j], width, *outer(ports_y, y, y_count), None, ports_y),
        (lambda j: r_z[j], depth, *outer(ports_z, z, z_count), None, ports_z),
    ))
    y_copy.wait()
    z_copy.wait()


def factor_lines(kappa):
    depth, width, band = kappa.shape
    along_y, along_z = (width, depth, band), (depth, width, band)
    return call(
        factor_kernel,
        "factor",
        [("far", far(*along_y)), ("far", far(*along_z)), near(5, depth, band), near(5, width, band)],
        [("plain", kappa)],
        scratch=[near(*along_y), near(*along_y), near(*along_z), pltpu.SemaphoreType.DMA((2,))],
        cycles=4000,
    )


def ports_kernel(axis, level, mine, theirs, joint, out):
    index = lax.axis_index(axis)
    is_left = (lax.shift_right_logical(index, level) & 1) == 0
    pairs = [(mine[k], theirs[k]) for k in range(5)]
    left = [jnp.where(is_left, m, t) for m, t in pairs]
    right = [jnp.where(is_left, t, m) for m, t in pairs]
    d = reciprocal(reciprocal((0.5 * RATE) * (left[4] + right[3])) + left[2] + right[0])
    low, high = left[0] - left[1] * left[1] * d, right[2] - right[1] * right[1] * d
    joint[0] = d
    joint[1] = left[1]
    joint[2] = right[1]
    if level + 2 == levels_of(axis):
        next_left = (lax.shift_right_logical(index, level + 1) & 1) == 0
        out[0] = jnp.where(next_left, high, low)
        out[1] = jnp.where(next_left, right[4], left[3])
    else:
        out[0] = low
        out[1] = left[1] * right[1] * d
        out[2] = high
        out[3] = left[3]
        out[4] = right[4]


def join_ports(mine, theirs, axis, level):
    _, lines, band = mine.shape

    def kernel(*refs):
        ports_kernel(axis, level, *refs)

    last = level + 2 == levels_of(axis)
    outs = [near(3, lines, band), near(2 if last else 5, lines, band)]
    return call(kernel, "join_ports", outs, [mine, theirs], cycles=100)


def join_all(ports, axis):
    joints = []
    for level in range(levels_of(axis) - 1):
        joint, ports = join_ports(ports, swap(ports, axis, level), axis, level)
        joints.append(joint)
    return joints, ports, swap(ports, axis, len(joints))


def source_kernel(axis, level, last, mine, theirs, joint, out, flow_ref):
    index = lax.axis_index(axis)
    is_left = (lax.shift_right_logical(index, level) & 1) == 0
    pairs = [(mine[k], theirs[k]) for k in range(2)]
    left = [jnp.where(is_left, m, t) for m, t in pairs]
    right = [jnp.where(is_left, t, m) for m, t in pairs]
    flow = (left[1] - right[0]) * joint[0]
    flow_ref[0] = flow
    low, high = left[0] - joint[1] * flow, right[1] + joint[2] * flow
    if last:
        next_left = (lax.shift_right_logical(index, level + 1) & 1) == 0
        out[0] = jnp.where(next_left, high, low)
    else:
        out[0] = low
        out[1] = high


def join_sources(mine, theirs, joint, axis, level):
    _, lines, band = mine.shape
    last = level + 2 == levels_of(axis)

    def kernel(*refs):
        source_kernel(axis, level, last, *refs)

    outs = [near(1 if last else 2, lines, band), near(1, lines, band)]
    return call(kernel, "join_sources", outs, [mine, theirs, joint], cycles=100)


def end_currents(axis, mine, theirs, edge, edge_theirs, joints, flows):
    index = lax.axis_index(axis)
    level = len(joints)
    is_left = (lax.shift_right_logical(index, level) & 1) == 0
    d = reciprocal(reciprocal((0.5 * RATE) * (edge[1] + edge_theirs[1])) + edge[0] + edge_theirs[0])
    flow = (mine[0] - theirs[0]) * d
    zero = jnp.zeros_like(flow)
    low, high = jnp.where(is_left, zero, -flow), jnp.where(is_left, -flow, zero)
    for level in range(level - 1, -1, -1):
        joint = joints[level]
        is_left = (lax.shift_right_logical(index, level) & 1) == 0
        flow = flows[level][0] + (joint[1] * low - joint[2] * high) * joint[0]
        low, high = jnp.where(is_left, low, flow), jnp.where(is_left, -flow, high)
    return low, high


def solve_open(values, phi, psi, scale, base, ports):
    count = base.shape[0]
    total = jnp.zeros(base.shape[1:], F32)
    following = (values[0], phi[0], psi[0])
    for j in range(count):
        value, low, high = following
        if j + 1 < count:
            following = (values[j + 1], phi[j + 1], psi[j + 1])
        total = total + low * value
        base[j] = high * total
    ports[1] = scale * total
    total = jnp.zeros(base.shape[1:], F32)
    following = (base[count - 1], values[count - 1], phi[count - 1], psi[count - 1])
    for j in range(count - 1, -1, -1):
        below, value, low, high = following
        if j > 0:
            following = (base[j - 1], values[j - 1], phi[j - 1], psi[j - 1])
        base[j] = scale * (below + low * total)
        total = total + high * value
    ports[0] = scale * total


def advect_kernel(
    tracer, y_speed, z_speed, b, a, o, e, corner, ab, ports_y, r_y_far, r_z_far,
    base, sources, r_y, r_z, c, ys, zs, sy, sz, phi, psi, kept, flux_z, flux_y, sem,
):
    z, y, z_count, y_count = place()
    depth, width, band = tracer.shape
    rows, cols = depth + 8, width + 8
    y_copy = pltpu.make_async_copy(r_y_far, r_y, sem.at[3])
    z_copy = pltpu.make_async_copy(r_z_far, r_z, sem.at[4])
    y_copy.start()
    z_copy.start()
    z_odd, y_odd = lax.rem(z, 2), lax.rem(y, 2)
    keep_b = jnp.where((z_odd == 0) & (z == 0) | (z_odd == 1) & (z == z_count - 1), 0.0, 1.0)
    keep_o = jnp.where((y_odd == 0) & (y == 0) | (y_odd == 1) & (y == y_count - 1), 0.0, 1.0)
    keep_below = jnp.where(z_odd == 0, keep_b, 1.0)
    keep_above = jnp.where(z_odd == 1, keep_b, 1.0)
    column = lax.broadcasted_iota(jnp.int32, (8, band), 0)
    outside = (column < 4) & (y == y_count - 1) | (column >= 4) & (y == 0)
    inside = jnp.where(outside, 0.0, 1.0)

    for field in (c, ys, zs):
        field[0:4, width:cols, :] = jnp.zeros((4, 8, band), F32)
        field[4 + depth : rows, width:cols, :] = jnp.zeros((4, 8, band), F32)
    flux_z[:, width:cols, :] = jnp.zeros((2, 8, band), F32)
    for ref, low, keep in ((a, z_odd, 1.0), (b, 1 - z_odd, keep_b)):
        three = jnp.where(low == 1, 1, depth + 4)
        for k, field in enumerate((c, zs, ys)):
            field[pl.ds(three, 3), 0:width, :] = ref[3 * k : 3 * k + 3] * keep
        flux_z[1 - low, 0:width, :] = ref[9] * keep

    def sides(o_low):
        other, pair = (o, keep_o), (e, 1.0)
        (above, keep_up), (below, keep_down) = (pair, other) if o_low else (other, pair)
        empty = jnp.zeros((2, depth, band), F32)
        for k, field in enumerate((c, ys, zs)):
            three = slice(3 * k, 3 * k + 3)
            tile = jnp.concatenate([above[three] * keep_up, empty, below[three] * keep_down], axis=0)
            field[4 : 4 + depth, width:cols, :] = turned(tile)
        faces = [empty, above[9:10] * keep_up, empty[:1], below[9:10] * keep_down, empty, empty[:1]]
        flux_y[...] = turned(jnp.concatenate(faces, axis=0))

        def corners(ref, low, keep):
            one, two, three = (width + 7, width + 6, width + 5) if low else (width, width + 1, width + 2)
            top = 4 + depth
            for f, field in enumerate((c, ys, zs)):
                near_tile, far_tile = ref.at[2 * f], ref.at[2 * f + 1]
                field[1:4, one, :] = near_tile[1:4] * (keep * keep_below)
                field[top : top + 3, one, :] = near_tile[4:7] * (keep * keep_above)
                field[2:4, two, :] = far_tile[2:4] * (keep * keep_below)
                field[top : top + 2, two, :] = far_tile[4:6] * (keep * keep_above)
                field[3:4, three, :] = far_tile[1:2] * (keep * keep_below)
                field[top : top + 1, three, :] = far_tile[6:7] * (keep * keep_above)

        corners(corner, o_low, keep_o)
        corners(ab, not o_low, 1.0)

    @pl.when(y_odd == 0)
    def _():
        sides(True)

    @pl.when(y_odd == 1)
    def _():
        sides(False)

    for field, own in ((ys, y_speed), (zs, z_speed), (c, tracer)):
        field[4 : 4 + depth, 0:width, :] = own[...]

    def up(v):
        return pltpu.roll(v, cols - 1, 0)

    def down(v):
        return pltpu.roll(v, 1, 0)

    def faces(r, before):
        v = ys[r]
        sy[r] = 0.5 * (v + up(v))
        after = zs[r + 1]
        sz[r] = 0.5 * (before + after)
        return after

    lax.fori_loop(0, rows - 1, faces, zs[0], unroll=39)

    keep_low = jnp.where(z == 0, 0.0, 1.0)
    keep_high = jnp.where(z == z_count - 1, 0.0, 1.0)
    given = (column == 2) | (column == 4)
    for step in range(1, NSUB + 1):

        def row(r, carry, side=False, top=None):
            here, below = carry
            after = c[r + 1]
            above = flux(sz[r], here, after) if top is None else top
            across = flux(sy[r], here, up(here))
            if side:
                edge = jnp.where(given, flux_y[r - 4], across[width:cols])
                across = jnp.concatenate([across[0:width], edge], axis=0)
            new = here - (across - down(across)) - (above - below)
            c[r, 0:width, :] = new[0:width]
            c[r, width:cols, :] = new[width:cols] * inside
            return after, above

        if step == 1:
            carry = c[1], flux_z[0]
            for r in range(1, 4):
                carry = row(r, carry)
            side_row = lambda r, carry: row(r, carry, side=True)
            carry = lax.fori_loop(4, 4 + depth, side_row, carry, unroll=16)
            for r in range(4 + depth, rows - 2):
                carry = row(r, carry)
            row(rows - 2, carry, top=flux_z[1])
        else:
            below = flux(sz[step - 1], c[step - 1], c[step])
            lax.fori_loop(step, rows - step, row, (c[step], below), unroll=16)
        if step < NSUB:
            c[3] = c[3] * keep_low
            c[4 + depth] = c[4 + depth] * keep_high

    z_copy.wait()
    y_copy.wait()
    factor(((lambda j: r_y[j], width, *outer(ports_y, y, y_count), (phi, psi), None),))
    kept[...] = turned(c[4 : 4 + depth, 0:width, :])
    solve_open(kept, phi, psi, ports_y[1], base, sources)


def advect(tracer, y_speed, z_speed, halos, ports_y, r_y, r_z):
    depth, width, band = tracer.shape
    padded = near(depth + 8, width + 8, band)
    along_y, along_z = near(width, depth, band), near(depth, width, band)
    return call(
        advect_kernel,
        "advect",
        [along_y, near(2, depth, band), along_y, along_z],
        [tracer, y_speed, z_speed]
        + list(halos)
        + [ports_y, ("far", r_y), ("far", r_z)],
        scratch=[padded] * 5 + [along_y] * 3
        + [near(2, width + 8, band), near(depth, 8, band), pltpu.SemaphoreType.DMA((5,))],
        cycles=5000,
    )


def turn_kernel(levels, *refs):
    last, refs = refs[0:4], refs[4:]
    joints, flows = refs[0:levels], refs[levels : 2 * levels]
    ports_y, base_y, r_y, ports_z, r_z, _, base, sources, phi, psi, u, kept = refs[2 * levels :]
    z, y, z_count, y_count = place()
    width, depth = base_y.shape[0], base.shape[0]
    low, high = end_currents("gy", *last, joints, flows)
    edge, _ = outer(ports_y, y, y_count)
    factor(((lambda k: r_z[k], depth, *outer(ports_z, z, z_count), (phi, psi), None),))
    value = low * ports_y[0] + high * ports_y[1]
    current = (1.0 + edge) * value - low
    u[0] = base_y[0] + value
    following = (r_y[1], base_y[1])
    for j in range(1, width):
        (r, own), following = following, (r_y[j + 1], base_y[j + 1]) if j + 1 < width else None
        value = value + r * current
        current = current + value
        u[j] = own + value
    kept[...] = turned(u[...])
    solve_open(kept, phi, psi, ports_z[1], base, sources)


def turn(last, joints, flows, ports_y, base_y, r_y, ports_z, r_z, after):
    width, depth, band = base_y.shape
    along_z = near(depth, width, band)

    def kernel(*refs):
        turn_kernel(len(joints), *refs)

    return call(
        kernel,
        "turn",
        [along_z, near(2, width, band), along_z, along_z],
        [*last, *joints, *flows, ports_y, base_y, r_y, ports_z, r_z, after],
        scratch=[near(width, depth, band), along_z],
        cycles=1500,
    )


def finish_kernel(levels, *refs):
    last, refs = refs[0:4], refs[4:]
    joints, flows = refs[0:levels], refs[levels : 2 * levels]
    ports_z, base, phi, psi, out, u, sem = refs[2 * levels :]
    low, high = end_currents("gz", *last, joints, flows)
    scale = ports_z[1]
    low, high = low * scale, high * scale
    depth = base.shape[0]
    part = depth // 4
    copies = []
    for p in range(4):
        for k in range(p * part, (p + 1) * part):
            u[k] = base[k] + low * psi[k] + high * phi[k]
        block = pl.ds(p * part, part)
        copies.append(pltpu.make_async_copy(u.at[block], out.at[block], sem.at[p]))
        copies[-1].start()
    for copy in copies:
        copy.wait()


def finish(last, joints, flows, ports_z, base, phi, psi):
    def kernel(*refs):
        finish_kernel(len(joints), *refs)

    return call(
        kernel,
        "finish",
        [("far", jax.ShapeDtypeStruct(base.shape, F32))],
        [*last, *joints, *flows, ports_z, base, phi, psi],
        scratch=[near(*base.shape), pltpu.SemaphoreType.DMA((4,))],
        cycles=1000,
    )


def exchange_sources(sources, joints, axis):
    flows = []
    for level, joint in enumerate(joints):
        sources, flow = join_sources(sources, swap(sources, axis, level), joint, axis, level)
        flows.append(flow)
    return sources, swap(sources, axis, len(joints)), flows


def local(tracer, y_speed, z_speed, kappa):
    b, a = z_rims(tracer, y_speed, z_speed)
    o, e = begin(tracer, y_speed, z_speed, b)
    b = send(b, z_partner=z_other)
    a = send(a, z_partner=pair_up)
    e = swap(e, "gy", 0)
    o = send(o, y_partner=y_ring)
    r_y, r_z, ports_y, ports_z = factor_lines(kappa)
    for_pair, for_other = rim(a, b)
    corner = send(for_other, y_partner=y_other)
    ab = swap(for_pair, "gy", 0)
    joints_y, edge_y, edge_y_theirs = join_all(ports_y, "gy")

    base, sources, r_y, r_z = advect(
        tracer, y_speed, z_speed, (b, a, o, e, corner, ab), ports_y, r_y, r_z
    )
    joints_z, edge_z, edge_z_theirs = join_all(ports_z, "gz")
    mine, theirs, flows = exchange_sources(sources, joints_y, "gy")
    base, sources, phi_z, psi_z = turn(
        (mine, theirs, edge_y, edge_y_theirs), joints_y, flows, ports_y, base, r_y, ports_z, r_z, joints_z[-1]
    )
    mine, theirs, flows = exchange_sources(sources, joints_z, "gz")
    return finish((mine, theirs, edge_z, edge_z_theirs), joints_z, flows, ports_z, base, phi_z, psi_z)


def solution(mesh):
    spec = P("gz", "gy", None)
    return jax.shard_map(
        local, mesh=mesh, in_specs=(spec,) * 4, out_specs=spec, check_vma=False
    )
```
